32 devices in a mesh: rep: 2 (over x), dp: 4 (over y, core), ctx: 4 (over z).
Axes of the slice: x: 2, y: 2, z: 4, core: 2. Of those that a mesh axis runs over, the one named last changes fastest.
Arguments:
- frames: bfloat16 [8, 512, 1024], P(('rep', 'dp'), 'ctx'), may hold values from -24 to 24
- lengths: int32 [8], P(('rep', 'dp')), may hold values from 64 to 512, as said below
- cotangent: bfloat16 [8, 512, 1024], P(('rep', 'dp'), 'ctx'), may hold values from -6 to 6
- w_query: bfloat16 [1024, 512], P('dp'), may hold values from -0.5 to 0.5
- w_key: bfloat16 [1024, 512], P('dp'), may hold values from -0.5 to 0.5
- w_value: bfloat16 [1024, 512], P('dp'), may hold values from -0.1875 to 0.1875
- w_out: bfloat16 [512, 1024], P('dp'), may hold values from -0.25 to 0.25
Outputs:
- attended: bfloat16 [8, 512, 1024], P(('rep', 'dp'), 'ctx')
- grad_frames: bfloat16 [8, 512, 1024], P(('rep', 'dp'), 'ctx')
- grad_out: float32 [512, 1024], P('dp')
The draws below stay inside these ranges and needn't reach their ends.
Inputs may be any that keep to these rules, and one draw needn't show every extreme that they name: `lengths`: number of real frames of each meeting; one meeting of every draw has all 512 frames real.
All inputs are finite; a program needn't handle non-finite values.
Results may differ from the reference program's by a relative error of at most 0.025.
The reference program's roundings to bfloat16 on the way count: a program that leaves them out, or rounds other values in their place, can miss the bound.
Values may be sent and summed in bfloat16 or wider, within the bound.
A program may use at most 64 MiB of HBM per device.

```python
import jax
import jax.numpy as jnp
from jax import lax

D = 1024
HEAD = 128
HEADS = 4
HD = 512
FRAMES = 512
MEETINGS = 8


def draw_frames(key, part):
    normal_key = jax.random.fold_in(key, 0)
    base = jax.random.normal(normal_key, (MEETINGS, FRAMES, D), jnp.float32)
    return jnp.clip(base, -6.0, 6.0).astype(jnp.bfloat16)


def draw_lengths(key, part):
    first_key, second_key, pick_key = jax.random.split(key, 3)
    lowest = FRAMES // 8
    first_draw = jax.random.randint(first_key, (MEETINGS,), 0, FRAMES - lowest + 1)
    second_draw = jax.random.randint(second_key, (MEETINGS,), 0, FRAMES - lowest + 1)
    chosen = jax.random.randint(pick_key, (), 0, MEETINGS)
    base = lowest + jnp.minimum(first_draw, second_draw)
    return jnp.where(jnp.arange(MEETINGS) == chosen, FRAMES, base).astype(jnp.int32)


def block_levels(rng, extent, shards, smallest, top_value):
    gain = 1.0
    for axis_at, shards_of in shards:
        steps = jax.random.uniform(jax.random.fold_in(jax.random.fold_in(rng, 6), axis_at), (shards_of,), jnp.float32, smallest / len(shards), top_value / len(shards))
        gain = gain * jnp.repeat(jnp.exp(steps), extent[axis_at] // shards_of).reshape((-1,) + (1,) * (len(extent) - 1 - axis_at))
    return gain


def centred(key, dims, spread, most, cuts=(), held_as=jnp.bfloat16):
    values = jax.random.normal(key, dims, jnp.float32) * spread
    if len(cuts) > 0:
        values = block_levels(key, dims, cuts, -0.22, 0.18) * values
    return jnp.clip(values, min=-most, max=most).astype(held_as)


def setup_inputs(seed: int = 0) -> dict:
    arg_keys = jax.random.split(jax.random.key(seed), 8)
    return {
        "frames": draw_frames(jax.random.fold_in(arg_keys[7], 71), 0),
        "lengths": draw_lengths(jax.random.fold_in(arg_keys[7], 71), 0),
        "cotangent": centred(arg_keys[2], (MEETINGS, FRAMES, D), 1.0, 6.0, ((0, 8), (1, 4))),
        "w_query": centred(arg_keys[3], (D, HD), (D ** -0.5), 0.5, ((0, 4),)),
        "w_key": centred(arg_keys[4], (D, HD), (D ** -0.5), 0.5, ((0, 4),)),
        "w_value": centred(arg_keys[5], (D, HD), D ** -0.5, 0.1875, ((0, 4),)),
        "w_out": centred(arg_keys[6], (HD, D), HD ** -0.5, 0.25, ((0, 4),)),
    }


MASKED_SCORE = -1.0e30


def meeting_pass(inputs, upstream, length, w_query, w_key, w_value, w_out):
    frame_count = inputs.shape[0]
    score_scale = HEAD ** -0.5
    usable = jnp.arange(frame_count) < length
    queries = jnp.dot(inputs, w_query, preferred_element_type=jnp.float32).astype(jnp.bfloat16)
    keys = jnp.dot(inputs, w_key, preferred_element_type=jnp.float32).astype(jnp.bfloat16)
    values = jnp.dot(inputs, w_value, preferred_element_type=jnp.float32).astype(jnp.bfloat16)
    masked_grad = jnp.where(usable[:, None], upstream, jnp.zeros_like(upstream))
    contexts = []
    logsums = []
    for head in range(HEADS):
        columns = slice(head * HEAD, (head + 1) * HEAD)
        scores = jnp.dot(queries[:, columns], keys[:, columns].T, preferred_element_type=jnp.float32) * score_scale
        scores = jnp.where(usable[None, :], scores, MASKED_SCORE)
        maxima = jnp.max(scores, axis=1)
        exponent = jnp.where(usable[None, :], jnp.exp(scores - maxima[:, None]), 0.0)
        totals = jnp.sum(exponent, axis=1)
        mixed = jnp.dot(exponent.astype(jnp.bfloat16), values[:, columns], preferred_element_type=jnp.float32)
        contexts.append(mixed / totals[:, None])
        logsums.append(maxima + jnp.log(totals))
    context = jnp.concatenate(contexts, axis=1).astype(jnp.bfloat16)
    attended = jnp.dot(context, w_out, preferred_element_type=jnp.float32)
    attended = jnp.where(usable[:, None], attended, 0.0).astype(jnp.bfloat16)
    grad_term = jnp.dot(context.T, masked_grad, preferred_element_type=jnp.float32)
    grad_context = jnp.dot(masked_grad, w_out.T, preferred_element_type=jnp.float32).astype(jnp.bfloat16)
    grad_queries = []
    grad_keys = []
    grad_values = []
    for head in range(HEADS):
        columns = slice(head * HEAD, (head + 1) * HEAD)
        deltas = jnp.sum(grad_context[:, columns].astype(jnp.float32) * context[:, columns].astype(jnp.float32), axis=1)
        scores = jnp.dot(queries[:, columns], keys[:, columns].T, preferred_element_type=jnp.float32) * score_scale
        attention = jnp.where(usable[None, :], jnp.exp(scores - logsums[head][:, None]), 0.0)
        grad_values.append(jnp.dot(attention.astype(jnp.bfloat16).T, grad_context[:, columns], preferred_element_type=jnp.float32))
        grad_prob = jnp.dot(grad_context[:, columns], values[:, columns].T, preferred_element_type=jnp.float32)
        grad_score = (attention * (grad_prob - deltas[:, None])).astype(jnp.bfloat16)
        grad_queries.append(jnp.dot(grad_score, keys[:, columns], preferred_element_type=jnp.float32) * score_scale)
        grad_keys.append(jnp.dot(grad_score.T, queries[:, columns], preferred_element_type=jnp.float32) * score_scale)
    grad_query = jnp.concatenate(grad_queries, axis=1).astype(jnp.bfloat16)
    grad_key = jnp.concatenate(grad_keys, axis=1).astype(jnp.bfloat16)
    grad_value = jnp.concatenate(grad_values, axis=1).astype(jnp.bfloat16)
    grad_input = jnp.dot(grad_query, w_query.T, preferred_element_type=jnp.float32)
    grad_input = grad_input + jnp.dot(grad_key, w_key.T, preferred_element_type=jnp.float32)
    grad_input = grad_input + jnp.dot(grad_value, w_value.T, preferred_element_type=jnp.float32)
    return attended, grad_input.astype(jnp.bfloat16), grad_term


def reference(frames, lengths, cotangent, w_query, w_key, w_value, w_out):
    def one_meeting(meeting):
        return meeting_pass(meeting[0], meeting[1], meeting[2], w_query, w_key, w_value, w_out)

    attended, grad_frames, grad_terms = lax.map(one_meeting, (frames, cotangent, lengths))
    return attended, grad_frames, jnp.sum(grad_terms, axis=0)
```

```python
import functools
import math

import jax
import jax.numpy as jnp
from jax import lax
from jax.experimental import pallas as pl
from jax.experimental.pallas import tpu as pltpu
from jax.sharding import PartitionSpec as P

HEAD = 128


MASKED_SCORE = -1e30


def head_split(matrix, head_count):
    return matrix.reshape(matrix.shape[0], head_count, matrix.shape[1] // head_count)


def forward_step(carry, key_part, value_part, offset, query_heads, length, score_scale):
    head_count = query_heads.shape[1]
    amount = key_part.shape[0]
    maxima, totals, accumulated = carry
    key_heads = head_split(key_part, head_count)
    value_heads = head_split(value_part, head_count)
    scores = (
        jnp.einsum("rhe,nhe->hrn", query_heads, key_heads, preferred_element_type=jnp.float32)
        * score_scale
    )
    usable = offset + jnp.arange(amount) < length
    scores = jnp.where(usable[None, None, :], scores, MASKED_SCORE)
    new_maxima = jnp.maximum(maxima, jnp.max(scores, axis=2))
    factor = jnp.exp(maxima - new_maxima)
    exponent = jnp.where(usable[None, None, :], jnp.exp(scores - new_maxima[:, :, None]), 0.0)
    totals = totals * factor + jnp.sum(exponent, axis=2)
    mixed = jnp.einsum(
        "hrn,nhe->hre",
        exponent.astype(jnp.bfloat16),
        value_heads,
        preferred_element_type=jnp.float32,
    )
    accumulated = accumulated * factor[:, :, None] + mixed
    return (new_maxima, totals, accumulated)


def query_step(
    grad_accum,
    key_part,
    value_part,
    offset,
    query_heads,
    context_heads,
    logsum,
    deltas,
    length,
    score_scale,
):
    head_count = query_heads.shape[1]
    amount = key_part.shape[0]
    key_heads = head_split(key_part, head_count)
    value_heads = head_split(value_part, head_count)
    scores = (
        jnp.einsum("rhe,nhe->hrn", query_heads, key_heads, preferred_element_type=jnp.float32)
        * score_scale
    )
    usable = offset + jnp.arange(amount) < length
    attention = jnp.where(usable[None, None, :], jnp.exp(scores - logsum[:, :, None]), 0.0)
    grad_prob = jnp.einsum(
        "rhe,nhe->hrn", context_heads, value_heads, preferred_element_type=jnp.float32
    )
    grad_score = (attention * (grad_prob - deltas[:, :, None])).astype(jnp.bfloat16)
    added = jnp.einsum("hrn,nhe->rhe", grad_score, key_heads, preferred_element_type=jnp.float32)
    return grad_accum + added * score_scale


def key_step(
    query_part,
    context_part,
    all_logsum,
    all_deltas,
    key_heads,
    value_heads,
    key_usable,
    score_scale,
):
    head_count = key_heads.shape[1]
    query_heads = head_split(query_part, head_count)
    context_heads = head_split(context_part, head_count)
    scores = (
        jnp.einsum("rhe,nhe->hrn", query_heads, key_heads, preferred_element_type=jnp.float32)
        * score_scale
    )
    attention = jnp.where(key_usable[None, None, :], jnp.exp(scores - all_logsum[:, :, None]), 0.0)
    grad_value = jnp.einsum(
        "hrn,rhe->nhe",
        attention.astype(jnp.bfloat16),
        context_heads,
        preferred_element_type=jnp.float32,
    )
    grad_prob = jnp.einsum(
        "rhe,nhe->hrn", context_heads, value_heads, preferred_element_type=jnp.float32
    )
    grad_score = (attention * (grad_prob - all_deltas[:, :, None])).astype(jnp.bfloat16)
    added = jnp.einsum("hrn,rhe->nhe", grad_score, query_heads, preferred_element_type=jnp.float32)
    return (added * score_scale, grad_value)


def back_project(gradient, weight):
    return lax.dot_general(
        gradient, weight, (((1,), (1,)), ((), ())), preferred_element_type=jnp.float32
    )


def shards(frames, lengths, cotangent, w_query, w_key, w_value, w_out):
    full_query, full_key, full_value, full_out = (
        lax.all_gather(w_query, "dp", axis=0, tiled=True),
        lax.all_gather(w_key, "dp", axis=0, tiled=True),
        lax.all_gather(w_value, "dp", axis=0, tiled=True),
        lax.all_gather(w_out, "dp", axis=0, tiled=True),
    )
    inputs = frames[0]
    upstream = cotangent[0]
    length = lengths[0]
    row_count = inputs.shape[0]
    inner_width = full_query.shape[1]
    head_count = inner_width // HEAD
    score_scale = HEAD ** (-0.5)
    first_frame = lax.axis_index("ctx") * row_count
    row_usable = first_frame + jnp.arange(row_count) < length
    queries = jnp.dot(inputs, full_query, preferred_element_type=jnp.float32).astype(jnp.bfloat16)
    keys = jnp.dot(inputs, full_key, preferred_element_type=jnp.float32).astype(jnp.bfloat16)
    values = jnp.dot(inputs, full_value, preferred_element_type=jnp.float32).astype(jnp.bfloat16)
    query_heads = head_split(queries, head_count)
    key_heads = head_split(keys, head_count)
    value_heads = head_split(values, head_count)
    start_state = (
        jnp.full((head_count, row_count), MASKED_SCORE, jnp.float32),
        jnp.zeros((head_count, row_count), jnp.float32),
        jnp.zeros((head_count, row_count, HEAD), jnp.float32),
    )
    all_keys, all_values = (
        lax.all_gather(keys, "ctx", axis=0, tiled=True),
        lax.all_gather(values, "ctx", axis=0, tiled=True),
    )
    key_block = row_count * math.gcd(max(1, 512 // row_count), lax.axis_size("ctx"))
    block_count = all_keys.shape[0] // key_block
    key_blocks = all_keys.reshape(block_count, key_block, inner_width)
    value_blocks = all_values.reshape(block_count, key_block, inner_width)
    block_starts = jnp.arange(block_count, dtype=jnp.int32) * key_block

    def scan_forward(current, scan_item):
        return (
            forward_step(
                current, scan_item[0], scan_item[1], scan_item[2], query_heads, length, score_scale
            ),
            None,
        )

    softmax_state, unused = lax.scan(
        scan_forward, start_state, (key_blocks, value_blocks, block_starts)
    )
    maxima, totals, accumulated = softmax_state
    context = (
        (accumulated / totals[:, :, None])
        .transpose(1, 0, 2)
        .reshape(row_count, inner_width)
        .astype(jnp.bfloat16)
    )
    logsum = maxima + jnp.log(totals)
    attended = jnp.dot(context, full_out, preferred_element_type=jnp.float32)
    attended = jnp.where(row_usable[:, None], attended, 0.0).astype(jnp.bfloat16)
    masked_grad = jnp.where(row_usable[:, None], upstream, jnp.zeros_like(upstream))
    grad_context = back_project(masked_grad, full_out).astype(jnp.bfloat16)
    deltas = jnp.sum(
        (grad_context.astype(jnp.float32) * context.astype(jnp.float32)).reshape(
            row_count, head_count, HEAD
        ),
        axis=2,
    )
    context_heads = head_split(grad_context, head_count)
    delta_heads = deltas.T
    all_logsum, all_deltas = (
        lax.all_gather(logsum, "ctx", axis=1, tiled=True),
        lax.all_gather(delta_heads, "ctx", axis=1, tiled=True),
    )
    zero_grad = jnp.zeros((row_count, head_count, HEAD), jnp.float32)

    def scan_query(current, scan_item):
        return (
            query_step(
                current,
                scan_item[0],
                scan_item[1],
                scan_item[2],
                query_heads,
                context_heads,
                logsum,
                delta_heads,
                length,
                score_scale,
            ),
            None,
        )

    grad_query, unused = lax.scan(scan_query, zero_grad, (key_blocks, value_blocks, block_starts))
    grad_key, grad_value = key_step(
        lax.all_gather(queries, "ctx", axis=0, tiled=True),
        lax.all_gather(grad_context, "ctx", axis=0, tiled=True),
        all_logsum,
        all_deltas,
        key_heads,
        value_heads,
        row_usable,
        score_scale,
    )
    grad_query = grad_query.reshape(row_count, inner_width).astype(jnp.bfloat16)
    grad_key = grad_key.reshape(row_count, inner_width).astype(jnp.bfloat16)
    grad_value = grad_value.reshape(row_count, inner_width).astype(jnp.bfloat16)
    grad_input = (
        back_project(grad_query, full_query)
        + back_project(grad_key, full_key)
        + back_project(grad_value, full_value)
    )
    grad_frames = grad_input.astype(jnp.bfloat16)
    summed_grad = lax.psum(
        lax.dot_general(
            context, masked_grad, (((0,), (0,)), ((), ())), preferred_element_type=jnp.float32
        ),
        ("rep", "ctx"),
    )
    grad_out = lax.psum_scatter(summed_grad, "dp", scatter_dimension=0, tiled=True)
    return (attended[None], grad_frames[None], grad_out)


MESH = pl.DeviceIdType.MESH


def dot(left, right, left_dim, right_dim):
    return lax.dot_general(
        left, right, (((left_dim,), (right_dim,)), ((), ())), preferred_element_type=jnp.float32
    )


def fused_kernel(
    frames_ref,
    length_ref,
    cot_ref,
    wq_ref,
    wk_ref,
    wv_ref,
    wo_ref,
    attended_ref,
    grad_frames_ref,
    grad_out_ref,
    xs,
    upstream,
    mine,
    cs,
    wq,
    wk,
    wv,
    wo,
    qs,
    ks,
    vs,
    gs,
    ctx,
    logsum,
    deltas,
    dq,
    dk,
    dv,
    part,
    part_in,
    slices,
    send_sem,
    recv_sem,
    local_sem,
):
    rep, dp, z = lax.axis_index("rep"), lax.axis_index("dp"), lax.axis_index("ctx")
    count = 4
    heads = 4
    rows = frames_ref.shape[1]
    full = rows * count
    width = slices.shape[2]
    scale = HEAD ** (-0.5)
    sibling = dp + 1 - 2 * lax.rem(dp, 2)
    across = lax.rem(dp + 2, 4)
    across_sibling = lax.rem(sibling + 2, 4)
    other_rep = 1 - rep
    group = rep * 4 + dp

    local = [
        pltpu.make_async_copy(source, target, local_sem.at[at])
        for at, (source, target) in enumerate(
            (
                (wk_ref, wk.at[dp]),
                (wv_ref, wv.at[dp]),
                (wq_ref, wq.at[dp]),
                (wo_ref, wo.at[dp]),
                (frames_ref.at[0], xs.at[z]),
                (cot_ref.at[0], upstream),
            )
        )
    ]
    for copy in local:
        copy.start()

    barrier = pltpu.get_barrier_semaphore()
    for step in range(1, count):
        pl.semaphore_signal(
            barrier, inc=1, device_id=(rep, dp, lax.rem(z + step, count)), device_id_type=MESH
        )
    for step in range(1, 8):
        peer = lax.rem(group + step, 8)
        pl.semaphore_signal(
            barrier, inc=1, device_id=(peer // 4, lax.rem(peer, 4), z), device_id_type=MESH
        )
    pl.semaphore_wait(barrier, 10)

    def remote(source, target, index, device):
        return pltpu.make_async_remote_copy(
            src_ref=source,
            dst_ref=target,
            send_sem=send_sem.at[index],
            recv_sem=recv_sem.at[index],
            device_id=device,
            device_id_type=MESH,
        )

    def chain(which, side, hop):
        sign = 1 - 2 * side
        pool = (xs, gs)[which]
        owner = z - sign * (hop - 1)
        slot = jnp.clip(owner, 0, count - 1)
        source = frames_ref.at[0] if which == 0 and hop == 1 else pool.at[slot]
        target = jnp.clip(z + sign, 0, count - 1)
        index = which * 6 + side * 3 + hop - 1
        valid = (z + sign >= 0) & (z + sign < count) & (owner >= 0) & (owner < count)
        return valid, remote(source, pool.at[slot], index, (rep, dp, target))

    def chain_send(which, hop):
        for side in range(2):
            valid, copy = chain(which, side, hop)

            @pl.when(valid)
            def _():
                copy.start()

    def chain_recv(which, hop):
        for side in range(2):
            sign = 1 - 2 * side
            pool = (xs, gs)[which]
            owner = z - sign * hop
            slot = jnp.clip(owner, 0, count - 1)
            index = which * 6 + side * 3 + hop - 1

            @pl.when((owner >= 0) & (owner < count))
            def _():
                remote(pool.at[slot], pool.at[slot], index, (rep, dp, z)).wait_recv()

    weights = ((wo_ref, wo), (wk_ref, wk), (wv_ref, wv), (wq_ref, wq))

    def half(ref, which):
        size = ref.shape[0] // 2
        return ref.at[pl.ds(pl.multiple_of(which * size, size), size)]

    def chunk(ref, which, at):
        size = ref.shape[0] // 4
        return ref.at[pl.ds(pl.multiple_of((which * 2 + at) * size, size), size)]

    def weight_copy(piece, step):
        shard, pool = weights[piece]
        index = 12 + piece * 7 + step
        if step == 0:
            return remote(shard, pool.at[dp], index, (rep, sibling, z))
        if step < 3:
            target = chunk(pool.at[dp], rep, step - 1)
            return remote(chunk(shard, rep, step - 1), target, index, (rep, across, z))
        mine_at = pool.at[across]
        if step < 5:
            source = chunk(mine_at, rep, step - 3)
            return remote(source, source, index, (other_rep, dp, z))
        source = half(mine_at, rep if step == 5 else other_rep)
        return remote(source, source, index, (rep, sibling, z))

    def weight_recv(piece, step):
        pool = weights[piece][1]
        index = 12 + piece * 7 + step
        if step == 0:
            target = pool.at[sibling]
        elif step < 3:
            target = chunk(pool.at[across], rep, step - 1)
        elif step < 5:
            target = chunk(pool.at[across], other_rep, step - 3)
        else:
            target = half(pool.at[across_sibling], rep if step == 5 else other_rep)
        remote(target, target, index, (rep, dp, z)).wait_recv()

    def finish_chunk(at):
        weight_recv(at // 2, 3 + at % 2)
        if at % 2 == 1:
            weight_copy(at // 2, 6).start()

    def weight_chunk(at):
        weight_recv(at // 2, 1 + at % 2)
        weight_copy(at // 2, 3 + at % 2).start()
        if at + 2 < 8:
            weight_copy((at + 2) // 2, 1 + at % 2).start()
        if at % 2 == 1:
            weight_copy(at // 2, 5).start()
        if at >= 2:
            finish_chunk(at - 2)

    def cot_copy(step):
        peer = lax.rem(z + step, count)
        return remote(mine.at[peer], cs.at[z], 52 + step, (rep, dp, peer))

    chain_send(0, 1)
    for at in range(2):
        weight_copy(0, 1 + at).start()
    for piece in range(4):
        weight_copy(piece, 0).start()
    for copy in local:
        copy.wait()

    length = length_ref[0]
    columns = [slice(at * width, (at + 1) * width) for at in range(count)]
    real = z * rows + lax.broadcasted_iota(jnp.int32, (rows, width), 0) < length
    for at in range(count):
        kept = jnp.where(real, upstream[:, columns[at]].astype(jnp.float32), 0.0)
        mine[at] = kept.astype(jnp.bfloat16)
    cs[z] = mine[z]

    for at in range(4):
        weight_chunk(at)
    chain_recv(0, 1)
    chain_send(0, 2)
    for at in range(4, 6):
        weight_chunk(at)
    for step in (0, 5, 6):
        weight_recv(0, step)
    masked = jnp.concatenate([mine[at] for at in range(count)], axis=1)
    matrix = dot(masked, wo[...].reshape(512, 1024), 1, 1).astype(jnp.bfloat16)
    for head in range(heads):
        gs[z, head] = matrix[:, head * HEAD : (head + 1) * HEAD]
    weight_chunk(6)
    chain_recv(0, 2)
    chain_send(0, 3)
    for step in range(1, count):
        cot_copy(step).start()
    chain_send(1, 1)
    weight_chunk(7)
    finish_chunk(6)
    finish_chunk(7)
    for piece in range(1, 4):
        for step in (0, 5, 6):
            weight_recv(piece, step)

    def project(block):
        inputs = xs[block]
        start = pl.multiple_of(block * rows, rows)
        for pool, kept in ((wk, ks), (wv, vs), (wq, qs)):
            matrix = dot(inputs, pool[...].reshape(1024, 512), 1, 0).astype(jnp.bfloat16)
            for head in range(heads):
                kept[head, pl.ds(start, rows), :] = matrix[:, head * HEAD : (head + 1) * HEAD]

    def project_hops(first, last):
        def body(step, carry):
            hop = step // 2
            block = z + hop * (1 - 2 * lax.rem(step, 2))

            @pl.when((block >= 0) & (block < count))
            def _():
                project(jnp.clip(block, 0, count - 1))

            return carry

        lax.fori_loop(first, last, body, 0)

    project_hops(1, 6)
    chain_recv(0, 3)
    project_hops(6, 8)

    def key_mask(amount):
        return lax.broadcasted_iota(jnp.int32, (amount, full), 1) < length

    def forward(step, carry):
        head = step // 2
        amount = full // 2
        start = pl.multiple_of(lax.rem(step, 2) * amount, amount)
        usable = key_mask(amount)
        scores = dot(qs[head, pl.ds(start, amount), :], ks[head], 1, 1) * scale
        scores = jnp.where(usable, scores, MASKED_SCORE)
        maxima = jnp.max(scores, axis=1, keepdims=True)
        exponent = jnp.exp(scores - maxima)
        totals = jnp.sum(exponent, axis=1, keepdims=True)
        mixed = dot(exponent.astype(jnp.bfloat16), vs[head], 1, 0)
        ctx[head, pl.ds(start, amount), :] = (mixed * (1.0 / totals)).astype(jnp.bfloat16)
        logsum[head, pl.ds(start, amount), :] = maxima + jnp.log(totals)
        return carry

    lax.fori_loop(0, 4, forward, 0)
    chain_recv(1, 1)
    chain_send(1, 2)
    lax.fori_loop(4, 8, forward, 0)

    own = pl.ds(pl.multiple_of(z * rows, rows), rows)
    for step in range(1, count):
        source = lax.rem(z + count - step, count)
        remote(cs.at[source], cs.at[source], 52 + step, (rep, dp, z)).wait_recv()
    masked_slice = cs[...].reshape(full, width)
    for head in range(heads):
        part[head] = dot(ctx[head], masked_slice, 0, 0).astype(jnp.bfloat16)

    def part_copy(step):
        peer = lax.rem(group + step, 8)
        peer_dp = lax.rem(peer, 4)
        return remote(part.at[peer_dp], part_in.at[step], 40 + step, (peer // 4, peer_dp, z))

    for step in range(1, 8):
        part_copy(step).start()
    chain_recv(1, 2)
    chain_send(1, 3)

    own_context = jnp.concatenate([ctx[head, own, :] for head in range(heads)], axis=1)
    attended = dot(own_context, wo[...].reshape(512, 1024), 1, 0)
    row_at = z * rows + lax.broadcasted_iota(jnp.int32, attended.shape, 0)
    attended_ref[0] = jnp.where(row_at < length, attended, 0.0).astype(jnp.bfloat16)

    total = part[dp].astype(jnp.float32)
    for step in range(1, 8):
        part_copy(step).wait_recv()
        total = total + part_in[step].astype(jnp.float32)
    slices[z] = total.astype(jnp.bfloat16)

    def slice_copy(step):
        return remote(
            slices.at[z], slices.at[z], 48 + step, (rep, dp, lax.rem(z + step, count))
        )

    for step in range(1, count):
        slice_copy(step).start()

    chain_recv(1, 3)

    def backward(head, carry):
        queries, keys, values = qs[head], ks[head], vs[head]
        grads = gs[:, head].reshape(full, HEAD)
        terms = grads.astype(jnp.float32) * ctx[head].astype(jnp.float32)
        deltas[...] = jnp.sum(terms, axis=1, keepdims=True)
        own_keys, own_values = ks[head, own, :], vs[head, own, :]
        scores = dot(queries, own_keys, 1, 1) * scale
        at = z * rows + lax.broadcasted_iota(jnp.int32, scores.shape, 1)
        attention = jnp.where(at < length, jnp.exp(scores - logsum[head]), 0.0)
        dv[head] = dot(attention.astype(jnp.bfloat16), grads, 0, 0).astype(jnp.bfloat16)
        grad_prob = dot(grads, own_values, 1, 1)
        grad_score = (attention * (grad_prob - deltas[...])).astype(jnp.bfloat16)
        dk[head] = (dot(grad_score, queries, 0, 0) * scale).astype(jnp.bfloat16)
        scores = dot(qs[head, own, :], keys, 1, 1) * scale
        attention = jnp.where(key_mask(rows), jnp.exp(scores - logsum[head, own, :]), 0.0)
        grad_prob = dot(gs[z, head], values, 1, 1)
        grad_score = (attention * (grad_prob - deltas[own, :])).astype(jnp.bfloat16)
        dq[head] = (dot(grad_score, keys, 1, 0) * scale).astype(jnp.bfloat16)
        return carry

    lax.fori_loop(0, heads, backward, 0)

    grads = [
        jnp.concatenate([kept[head] for head in range(heads)], axis=1) for kept in (dq, dk, dv)
    ]
    for shard in range(4):
        added = (
            dot(grads[0], wq[shard], 1, 1)
            + dot(grads[1], wk[shard], 1, 1)
            + dot(grads[2], wv[shard], 1, 1)
        )
        grad_frames_ref[0, :, shard * 256 : (shard + 1) * 256] = added.astype(jnp.bfloat16)

    for piece in range(4):
        for step in range(7):
            weight_copy(piece, step).wait_send()
    for which in range(2):
        for hop in range(1, count):
            for side in range(2):
                valid, copy = chain(which, side, hop)

                @pl.when(valid)
                def _():
                    copy.wait_send()

    for step in range(1, count):
        cot_copy(step).wait_send()
    for step in range(1, 8):
        part_copy(step).wait_send()
    for step in range(1, count):
        source = lax.rem(z + count - step, count)
        remote(slices.at[source], slices.at[source], 48 + step, (rep, dp, z)).wait_recv()
    for step in range(1, count):
        slice_copy(step).wait_send()
    for at in range(count):
        grad_out_ref[:, at * width : (at + 1) * width] = slices[at].astype(jnp.float32)


def fused(frames, lengths, cotangent, w_query, w_key, w_value, w_out):
    vmem = pl.BlockSpec(memory_space=pltpu.VMEM)
    hbm = pl.BlockSpec(memory_space=pltpu.HBM)
    bf16, f32 = jnp.bfloat16, jnp.float32
    per_head = pltpu.VMEM((4, 512, HEAD), bf16)
    own_head = pltpu.VMEM((4, 128, HEAD), bf16)
    return pl.pallas_call(
        fused_kernel,
        out_shape=(
            jax.ShapeDtypeStruct(frames.shape, bf16),
            jax.ShapeDtypeStruct(frames.shape, bf16),
            jax.ShapeDtypeStruct(w_out.shape, f32),
        ),
        in_specs=[hbm, pl.BlockSpec(memory_space=pltpu.SMEM)] + [hbm] * 5,
        out_specs=(vmem, vmem, vmem),
        scratch_shapes=[
            pltpu.VMEM((4, 128, 1024), bf16),
            pltpu.VMEM((128, 1024), bf16),
            pltpu.VMEM((4, 128, 256), bf16),
            pltpu.VMEM((4, 128, 256), bf16),
            pltpu.VMEM((4, 256, 512), bf16),
            pltpu.VMEM((4, 256, 512), bf16),
            pltpu.VMEM((4, 256, 512), bf16),
            pltpu.VMEM((4, 128, 1024), bf16),
            per_head,
            per_head,
            per_head,
            pltpu.VMEM((4, 4, 128, HEAD), bf16),
            per_head,
            pltpu.VMEM((4, 512, 1), f32),
            pltpu.VMEM((512, 1), f32),
            own_head,
            own_head,
            own_head,
            pltpu.VMEM((4, 128, 256), bf16),
            pltpu.VMEM((8, 128, 256), bf16),
            pltpu.VMEM((4, 128, 256), bf16),
            pltpu.SemaphoreType.DMA((56,)),
            pltpu.SemaphoreType.DMA((56,)),
            pltpu.SemaphoreType.DMA((6,)),
        ],
        compiler_params=pltpu.CompilerParams(
            collective_id=0, has_side_effects=True, vmem_limit_bytes=56 * 1024 * 1024
        ),
    )(frames, lengths, cotangent, w_query, w_key, w_value, w_out)


def either(sizes, frames, lengths, cotangent, w_query, w_key, w_value, w_out):
    fits = sizes == (2, 4, 4) and frames.shape == (1, 128, 1024) and w_query.shape == (256, 512)
    chosen = fused if fits else shards
    return chosen(frames, lengths, cotangent, w_query, w_key, w_value, w_out)


def solution(mesh):
    in_specs = (
        P(("rep", "dp"), "ctx", None),
        P(("rep", "dp")),
        P(("rep", "dp"), "ctx", None),
        P("dp", None),
        P("dp", None),
        P("dp", None),
        P("dp", None),
    )
    out_specs = (P(("rep", "dp"), "ctx", None), P(("rep", "dp"), "ctx", None), P("dp", None))
    sizes = (mesh.shape["rep"], mesh.shape["dp"], mesh.shape["ctx"])
    body = functools.partial(either, sizes)
    return jax.shard_map(body, mesh=mesh, in_specs=in_specs, out_specs=out_specs, check_vma=False)
```

```python
import functools
import math

import jax
import jax.numpy as jnp
from jax import lax
from jax.experimental import pallas as pl
from jax.experimental.pallas import tpu as pltpu
from jax.sharding import PartitionSpec as P

HEAD = 128


MASKED_SCORE = -1e30


def head_split(matrix, head_count):
    return matrix.reshape(matrix.shape[0], head_count, matrix.shape[1] // head_count)


def forward_step(carry, key_part, value_part, offset, query_heads, length, score_scale):
    head_count = query_heads.shape[1]
    amount = key_part.shape[0]
    maxima, totals, accumulated = carry
    key_heads = head_split(key_part, head_count)
    value_heads = head_split(value_part, head_count)
    scores = (
        jnp.einsum("rhe,nhe->hrn", query_heads, key_heads, preferred_element_type=jnp.float32)
        * score_scale
    )
    usable = offset + jnp.arange(amount) < length
    scores = jnp.where(usable[None, None, :], scores, MASKED_SCORE)
    new_maxima = jnp.maximum(maxima, jnp.max(scores, axis=2))
    factor = jnp.exp(maxima - new_maxima)
    exponent = jnp.where(usable[None, None, :], jnp.exp(scores - new_maxima[:, :, None]), 0.0)
    totals = totals * factor + jnp.sum(exponent, axis=2)
    mixed = jnp.einsum(
        "hrn,nhe->hre",
        exponent.astype(jnp.bfloat16),
        value_heads,
        preferred_element_type=jnp.float32,
    )
    accumulated = accumulated * factor[:, :, None] + mixed
    return (new_maxima, totals, accumulated)


def query_step(
    grad_accum,
    key_part,
    value_part,
    offset,
    query_heads,
    context_heads,
    logsum,
    deltas,
    length,
    score_scale,
):
    head_count = query_heads.shape[1]
    amount = key_part.shape[0]
    key_heads = head_split(key_part, head_count)
    value_heads = head_split(value_part, head_count)
    scores = (
        jnp.einsum("rhe,nhe->hrn", query_heads, key_heads, preferred_element_type=jnp.float32)
        * score_scale
    )
    usable = offset + jnp.arange(amount) < length
    attention = jnp.where(usable[None, None, :], jnp.exp(scores - logsum[:, :, None]), 0.0)
    grad_prob = jnp.einsum(
        "rhe,nhe->hrn", context_heads, value_heads, preferred_element_type=jnp.float32
    )
    grad_score = (attention * (grad_prob - deltas[:, :, None])).astype(jnp.bfloat16)
    added = jnp.einsum("hrn,nhe->rhe", grad_score, key_heads, preferred_element_type=jnp.float32)
    return grad_accum + added * score_scale


def key_step(
    query_part,
    context_part,
    all_logsum,
    all_deltas,
    key_heads,
    value_heads,
    key_usable,
    score_scale,
):
    head_count = key_heads.shape[1]
    query_heads = head_split(query_part, head_count)
    context_heads = head_split(context_part, head_count)
    scores = (
        jnp.einsum("rhe,nhe->hrn", query_heads, key_heads, preferred_element_type=jnp.float32)
        * score_scale
    )
    attention = jnp.where(key_usable[None, None, :], jnp.exp(scores - all_logsum[:, :, None]), 0.0)
    grad_value = jnp.einsum(
        "hrn,rhe->nhe",
        attention.astype(jnp.bfloat16),
        context_heads,
        preferred_element_type=jnp.float32,
    )
    grad_prob = jnp.einsum(
        "rhe,nhe->hrn", context_heads, value_heads, preferred_element_type=jnp.float32
    )
    grad_score = (attention * (grad_prob - all_deltas[:, :, None])).astype(jnp.bfloat16)
    added = jnp.einsum("hrn,rhe->nhe", grad_score, query_heads, preferred_element_type=jnp.float32)
    return (added * score_scale, grad_value)


def back_project(gradient, weight):
    return lax.dot_general(
        gradient, weight, (((1,), (1,)), ((), ())), preferred_element_type=jnp.float32
    )


def shards(frames, lengths, cotangent, w_query, w_key, w_value, w_out):
    full_query, full_key, full_value, full_out = (
        lax.all_gather(w_query, "dp", axis=0, tiled=True),
        lax.all_gather(w_key, "dp", axis=0, tiled=True),
        lax.all_gather(w_value, "dp", axis=0, tiled=True),
        lax.all_gather(w_out, "dp", axis=0, tiled=True),
    )
    inputs = frames[0]
    upstream = cotangent[0]
    length = lengths[0]
    row_count = inputs.shape[0]
    inner_width = full_query.shape[1]
    head_count = inner_width // HEAD
    score_scale = HEAD ** (-0.5)
    first_frame = lax.axis_index("ctx") * row_count
    row_usable = first_frame + jnp.arange(row_count) < length
    queries = jnp.dot(inputs, full_query, preferred_element_type=jnp.float32).astype(jnp.bfloat16)
    keys = jnp.dot(inputs, full_key, preferred_element_type=jnp.float32).astype(jnp.bfloat16)
    values = jnp.dot(inputs, full_value, preferred_element_type=jnp.float32).astype(jnp.bfloat16)
    query_heads = head_split(queries, head_count)
    key_heads = head_split(keys, head_count)
    value_heads = head_split(values, head_count)
    start_state = (
        jnp.full((head_count, row_count), MASKED_SCORE, jnp.float32),
        jnp.zeros((head_count, row_count), jnp.float32),
        jnp.zeros((head_count, row_count, HEAD), jnp.float32),
    )
    all_keys, all_values = (
        lax.all_gather(keys, "ctx", axis=0, tiled=True),
        lax.all_gather(values, "ctx", axis=0, tiled=True),
    )
    key_block = row_count * math.gcd(max(1, 512 // row_count), lax.axis_size("ctx"))
    block_count = all_keys.shape[0] // key_block
    key_blocks = all_keys.reshape(block_count, key_block, inner_width)
    value_blocks = all_values.reshape(block_count, key_block, inner_width)
    block_starts = jnp.arange(block_count, dtype=jnp.int32) * key_block

    def scan_forward(current, scan_item):
        return (
            forward_step(
                current, scan_item[0], scan_item[1], scan_item[2], query_heads, length, score_scale
            ),
            None,
        )

    softmax_state, unused = lax.scan(
        scan_forward, start_state, (key_blocks, value_blocks, block_starts)
    )
    maxima, totals, accumulated = softmax_state
    context = (
        (accumulated / totals[:, :, None])
        .transpose(1, 0, 2)
        .reshape(row_count, inner_width)
        .astype(jnp.bfloat16)
    )
    logsum = maxima + jnp.log(totals)
    attended = jnp.dot(context, full_out, preferred_element_type=jnp.float32)
    attended = jnp.where(row_usable[:, None], attended, 0.0).astype(jnp.bfloat16)
    masked_grad = jnp.where(row_usable[:, None], upstream, jnp.zeros_like(upstream))
    grad_context = back_project(masked_grad, full_out).astype(jnp.bfloat16)
    deltas = jnp.sum(
        (grad_context.astype(jnp.float32) * context.astype(jnp.float32)).reshape(
            row_count, head_count, HEAD
        ),
        axis=2,
    )
    context_heads = head_split(grad_context, head_count)
    delta_heads = deltas.T
    all_logsum, all_deltas = (
        lax.all_gather(logsum, "ctx", axis=1, tiled=True),
        lax.all_gather(delta_heads, "ctx", axis=1, tiled=True),
    )
    zero_grad = jnp.zeros((row_count, head_count, HEAD), jnp.float32)

    def scan_query(current, scan_item):
        return (
            query_step(
                current,
                scan_item[0],
                scan_item[1],
                scan_item[2],
                query_heads,
                context_heads,
                logsum,
                delta_heads,
                length,
                score_scale,
            ),
            None,
        )

    grad_query, unused = lax.scan(scan_query, zero_grad, (key_blocks, value_blocks, block_starts))
    grad_key, grad_value = key_step(
        lax.all_gather(queries, "ctx", axis=0, tiled=True),
        lax.all_gather(grad_context, "ctx", axis=0, tiled=True),
        all_logsum,
        all_deltas,
        key_heads,
        value_heads,
        row_usable,
        score_scale,
    )
    grad_query = grad_query.reshape(row_count, inner_width).astype(jnp.bfloat16)
    grad_key = grad_key.reshape(row_count, inner_width).astype(jnp.bfloat16)
    grad_value = grad_value.reshape(row_count, inner_width).astype(jnp.bfloat16)
    grad_input = (
        back_project(grad_query, full_query)
        + back_project(grad_key, full_key)
        + back_project(grad_value, full_value)
    )
    grad_frames = grad_input.astype(jnp.bfloat16)
    summed_grad = lax.psum(
        lax.dot_general(
            context, masked_grad, (((0,), (0,)), ((), ())), preferred_element_type=jnp.float32
        ),
        ("rep", "ctx"),
    )
    grad_out = lax.psum_scatter(summed_grad, "dp", scatter_dimension=0, tiled=True)
    return (attended[None], grad_frames[None], grad_out)


MESH = pl.DeviceIdType.MESH


def dot(left, right, left_dim, right_dim):
    return lax.dot_general(
        left, right, (((left_dim,), (right_dim,)), ((), ())), preferred_element_type=jnp.float32
    )


def fused_kernel(
    frames_ref,
    length_ref,
    cot_ref,
    wq_ref,
    wk_ref,
    wv_ref,
    wo_ref,
    attended_ref,
    grad_frames_ref,
    grad_out_ref,
    xs,
    upstream,
    mine,
    cs,
    wq,
    wk,
    wv,
    wo,
    qs,
    ks,
    vs,
    gs,
    ctx,
    logsum,
    deltas,
    dq,
    dk,
    dv,
    part,
    part_in,
    slices,
    send_sem,
    recv_sem,
    local_sem,
):
    rep, dp, z = lax.axis_index("rep"), lax.axis_index("dp"), lax.axis_index("ctx")
    count = 4
    heads = 4
    rows = frames_ref.shape[1]
    full = rows * count
    scale = HEAD ** (-0.5)
    sibling = dp + 1 - 2 * lax.rem(dp, 2)
    across = lax.rem(dp + 2, 4)
    across_sibling = lax.rem(sibling + 2, 4)
    other_rep = 1 - rep
    group = rep * 4 + dp
    lower = z < 2
    middle = (z == 1) | (z == 2)
    side_at = jnp.clip(z - 1, 0, 1)

    local = [
        pltpu.make_async_copy(source, target, local_sem.at[at])
        for at, (source, target) in enumerate(
            (
                (cot_ref.at[0], upstream),
                (frames_ref.at[0], xs.at[z]),
                (wk_ref, wk.at[dp]),
                (wv_ref, wv.at[dp]),
                (wq_ref, wq.at[dp]),
                (wo_ref, wo.at[dp]),
            )
        )
    ]
    for copy in local:
        copy.start()

    barrier = pltpu.get_barrier_semaphore()
    for step in range(1, count):
        for to_rep in (rep, other_rep):
            pl.semaphore_signal(
                barrier,
                inc=1,
                device_id=(to_rep, dp, lax.rem(z + step, count)),
                device_id_type=MESH,
            )
    for step in range(1, 8):
        peer = lax.rem(group + step, 8)
        pl.semaphore_signal(
            barrier, inc=1, device_id=(peer // 4, lax.rem(peer, 4), z), device_id_type=MESH
        )
    pl.semaphore_wait(barrier, 13)

    def remote(source, target, sent, received, device):
        return pltpu.make_async_remote_copy(
            src_ref=source,
            dst_ref=target,
            send_sem=send_sem.at[sent],
            recv_sem=recv_sem.at[received],
            device_id=device,
            device_id_type=MESH,
        )

    def arrive(target, received):
        remote(target, target, received, received, (rep, dp, z)).wait_recv()

    def piece_of(which, slot, at):
        if which == 0:
            return xs.at[slot, pl.ds(at * (rows // 2), rows // 2)]
        return gs.at[slot, pl.ds(at * 2, 2)]

    def chain(which, side, hop, at):
        sign = 1 - 2 * side
        owner = z - sign * (hop - 1)
        slot = jnp.clip(owner, 0, count - 1)
        source = piece_of(which, slot, at)
        if which == 0 and hop == 1:
            source = frames_ref.at[0, pl.ds(at * (rows // 2), rows // 2)]
        target = jnp.clip(z + sign, 0, count - 1)
        index = which * 12 + side * 6 + (hop - 1) * 2 + at
        valid = (z + sign >= 0) & (z + sign < count) & (owner >= 0) & (owner < count)
        copy = remote(source, piece_of(which, slot, at), index, index, (rep, dp, target))
        return valid, copy

    def chain_send(which, hop, at):
        for side in range(2):
            valid, copy = chain(which, side, hop, at)

            @pl.when(valid)
            def _():
                copy.start()

    def chain_recv(which, hop, at):
        for side in range(2):
            owner = z - (1 - 2 * side) * hop
            slot = jnp.clip(owner, 0, count - 1)
            index = which * 12 + side * 6 + (hop - 1) * 2 + at

            @pl.when((owner >= 0) & (owner < count))
            def _():
                arrive(piece_of(which, slot, at), index)

    def chain_pass(which, hop, at):
        chain_recv(which, hop, at)
        if hop < 3:
            chain_send(which, hop + 1, at)

    weights = ((wk_ref, wk), (wv_ref, wv), (wq_ref, wq), (wo_ref, wo))

    def half(ref, which):
        size = ref.shape[0] // 2
        return ref.at[pl.ds(pl.multiple_of(which * size, size), size)]

    def chunk(ref, which, at):
        size = ref.shape[0] // 4
        return ref.at[pl.ds(pl.multiple_of((which * 2 + at) * size, size), size)]

    def weight_copy(piece, step):
        shard, pool = weights[piece]
        index = 24 + piece * 7 + step
        if step == 0:
            return remote(shard, pool.at[dp], index, index, (rep, sibling, z))
        if step < 3:
            target = chunk(pool.at[dp], rep, step - 1)
            return remote(chunk(shard, rep, step - 1), target, index, index, (rep, across, z))
        mine_at = pool.at[across]
        if step < 5:
            source = chunk(mine_at, rep, step - 3)
            return remote(source, source, index, index, (other_rep, dp, z))
        source = half(mine_at, rep if step == 5 else other_rep)
        return remote(source, source, index, index, (rep, sibling, z))

    def weight_recv(piece, step):
        pool = weights[piece][1]
        if step == 0:
            target = pool.at[sibling]
        elif step < 3:
            target = chunk(pool.at[across], rep, step - 1)
        elif step < 5:
            target = chunk(pool.at[across], other_rep, step - 3)
        else:
            target = half(pool.at[across_sibling], rep if step == 5 else other_rep)
        arrive(target, 24 + piece * 7 + step)

    def from_y(at):
        weight_recv(at // 2, 1 + at % 2)
        weight_copy(at // 2, 3 + at % 2).start()
        if at % 2 == 1:
            weight_copy(at // 2, 5).start()

    def from_x(at):
        weight_recv(at // 2, 3 + at % 2)
        if at % 2 == 1:
            weight_copy(at // 2, 6).start()

    def cot_copy(near):
        to = jnp.where(lower, 1, 2) if near else jnp.where(lower, 2, 1)
        sent = 52 + (0 if near else 1)
        return remote(mine.at[to - 1], cs.at[z], sent, 52 + z, (rep, dp, to))

    for at in range(2):
        chain_send(0, 1, at)
    for piece in range(4):
        for step in (1, 2):
            weight_copy(piece, step).start()
    for piece in range(4):
        weight_copy(piece, 0).start()
    for copy in local:
        copy.wait()

    length = length_ref[0]
    width = mine.shape[2]
    real = z * rows + lax.broadcasted_iota(jnp.int32, (rows, width), 0) < length
    for at in range(2):
        kept = upstream[:, at * width : (at + 1) * width].astype(jnp.float32)
        mine[at] = jnp.where(real, kept, 0.0).astype(jnp.bfloat16)
    cs[z] = mine[side_at]

    from_y(0)
    from_y(1)
    chain_pass(0, 1, 0)
    from_y(2)
    from_x(0)
    from_y(3)
    chain_pass(0, 1, 1)

    @pl.when(jnp.logical_not(middle))
    def _():
        cot_copy(True).start()

    cot_copy(False).start()
    from_x(1)
    from_y(4)
    from_x(2)
    from_y(5)
    chain_pass(0, 2, 0)
    from_x(3)
    from_y(6)
    from_x(4)
    from_y(7)
    chain_pass(0, 2, 1)
    from_x(5)
    for piece in range(3):
        for step in (0, 5, 6):
            weight_recv(piece, step)

    def project(first, blocks):
        inputs = xs[pl.ds(first, blocks)].reshape(blocks * rows, 1024)
        start = pl.multiple_of(first * rows, rows)
        for pool, kept in ((wk, ks), (wv, vs), (wq, qs)):
            matrix = dot(inputs, pool[...].reshape(1024, 512), 1, 0).astype(jnp.bfloat16)
            for head in range(heads):
                kept[head, pl.ds(start, blocks * rows), :] = matrix[
                    :, head * HEAD : (head + 1) * HEAD
                ]

    project(jnp.where(lower, 0, 1), 3)
    from_x(6)
    from_x(7)
    for step in (0, 5, 6):
        weight_recv(3, step)
    masked = jnp.concatenate([mine[0], mine[1]], axis=1)
    matrix = dot(masked, wo[...].reshape(512, 1024), 1, 1).astype(jnp.bfloat16)
    for head in range(heads):
        gs[z, head] = matrix[:, head * HEAD : (head + 1) * HEAD]
    for at in range(2):
        chain_send(1, 1, at)
    for at in range(2):
        chain_pass(0, 3, at)
    project(jnp.where(lower, 3, 0), 1)

    def key_mask(amount):
        return lax.broadcasted_iota(jnp.int32, (amount, full), 1) < length

    def part_copy(order, head, turned):
        to_rep = other_rep if turned else rep
        index = order * 2 + turned
        return remote(
            part.at[head, to_rep], part_in.at[index], 56 + index, 56 + index, (to_rep, head, z)
        )

    def forward(order, carry):
        head = lax.rem(dp + lax.rem(order, 2) * (sibling - dp) + 2 * (1 - order // 2) + 4, 4)
        amount = full // 2
        usable = key_mask(amount)
        for at in range(2):
            start = at * amount
            scores = dot(qs[head, pl.ds(start, amount), :], ks[head], 1, 1) * scale
            scores = jnp.where(usable, scores, MASKED_SCORE)
            maxima = jnp.max(scores, axis=1, keepdims=True)
            exponent = jnp.exp(scores - maxima)
            totals = jnp.sum(exponent, axis=1, keepdims=True)
            mixed = dot(exponent.astype(jnp.bfloat16), vs[head], 1, 0)
            ctx[head, pl.ds(start, amount), :] = (mixed * (1.0 / totals)).astype(jnp.bfloat16)
            logsum[head, pl.ds(start, amount), :] = maxima + jnp.log(totals)

        @pl.when(middle)
        def _():
            @pl.when(order == 0)
            def _():
                for source in range(count):

                    @pl.when(z != source)
                    def _():
                        arrive(cs.at[source], 52 + source)

            product = dot(ctx[head], cs[...].reshape(full, width), 0, 0)
            for at in range(2):
                part[head, at] = product[:, at * 256 : (at + 1) * 256].astype(jnp.bfloat16)

            @pl.when(order != 2)
            def _():
                part_copy(order, head, 0).start()

            part_copy(order, head, 1).start()

        return carry

    lax.fori_loop(0, heads, forward, 0)

    for at in range(2):
        chain_pass(1, 1, at)
    own = pl.ds(pl.multiple_of(z * rows, rows), rows)
    own_context = jnp.concatenate([ctx[head, own, :] for head in range(heads)], axis=1)
    attended = dot(own_context, wo[...].reshape(512, 1024), 1, 0)
    row_at = z * rows + lax.broadcasted_iota(jnp.int32, attended.shape, 0)
    attended_ref[0] = jnp.where(row_at < length, attended, 0.0).astype(jnp.bfloat16)
    for at in range(2):
        chain_pass(1, 2, at)

    mine_slice = side_at * 2 + rep

    def slice_copy(step, turned):
        to_rep = other_rep if turned else rep
        block = slices.at[mine_slice]
        return remote(
            block,
            block,
            64 + step * 2 + turned,
            64 + mine_slice,
            (to_rep, dp, lax.rem(z + step, count)),
        )

    @pl.when(middle)
    def _():
        total = part[dp, rep].astype(jnp.float32)
        for index in range(8):
            if index != 4:
                arrive(part_in.at[index], 56 + index)
                total = total + part_in[index].astype(jnp.float32)
        slices[mine_slice] = total.astype(jnp.bfloat16)
        for step in (1, 3, 2, 0):
            for turned in range(2):
                if step + turned > 0:
                    slice_copy(step, turned).start()

    for at in range(2):
        chain_pass(1, 3, at)

    def backward(head, carry):
        queries, keys, values = qs[head], ks[head], vs[head]
        grads = gs[:, head].reshape(full, HEAD)
        terms = grads.astype(jnp.float32) * ctx[head].astype(jnp.float32)
        deltas[...] = jnp.sum(terms, axis=1, keepdims=True)
        own_keys, own_values = ks[head, own, :], vs[head, own, :]
        scores = dot(queries, own_keys, 1, 1) * scale
        at = z * rows + lax.broadcasted_iota(jnp.int32, scores.shape, 1)
        attention = jnp.where(at < length, jnp.exp(scores - logsum[head]), 0.0)
        dv[head] = dot(attention.astype(jnp.bfloat16), grads, 0, 0).astype(jnp.bfloat16)
        grad_prob = dot(grads, own_values, 1, 1)
        grad_score = (attention * (grad_prob - deltas[...])).astype(jnp.bfloat16)
        dk[head] = (dot(grad_score, queries, 0, 0) * scale).astype(jnp.bfloat16)
        scores = dot(qs[head, own, :], keys, 1, 1) * scale
        attention = jnp.where(key_mask(rows), jnp.exp(scores - logsum[head, own, :]), 0.0)
        grad_prob = dot(gs[z, head], values, 1, 1)
        grad_score = (attention * (grad_prob - deltas[own, :])).astype(jnp.bfloat16)
        dq[head] = (dot(grad_score, keys, 1, 0) * scale).astype(jnp.bfloat16)
        return carry

    lax.fori_loop(0, heads, backward, 0)

    grads = [
        jnp.concatenate([kept[head] for head in range(heads)], axis=1) for kept in (dq, dk, dv)
    ]
    for shard in range(4):
        added = (
            dot(grads[0], wq[shard], 1, 1)
            + dot(grads[1], wk[shard], 1, 1)
            + dot(grads[2], wv[shard], 1, 1)
        )
        grad_frames_ref[0, :, shard * 256 : (shard + 1) * 256] = added.astype(jnp.bfloat16)

    for piece in range(4):
        for step in range(7):
            weight_copy(piece, step).wait_send()
    for which in range(2):
        for hop in range(1, count):
            for at in range(2):
                for side in range(2):
                    valid, copy = chain(which, side, hop, at)

                    @pl.when(valid)
                    def _():
                        copy.wait_send()

    @pl.when(jnp.logical_not(middle))
    def _():
        cot_copy(True).wait_send()

    cot_copy(False).wait_send()

    @pl.when(middle)
    def _():
        for index in range(8):
            if index != 4:
                part_copy(index // 2, dp, index % 2).wait_send()

    for at in range(count):

        @pl.when(jnp.logical_not(middle & (mine_slice == at)))
        def _():
            arrive(slices.at[at], 64 + at)

    @pl.when(middle)
    def _():
        for step in range(count):
            for turned in range(2):
                if step + turned > 0:
                    slice_copy(step, turned).wait_send()

    for at in range(count):
        grad_out_ref[:, at * 256 : (at + 1) * 256] = slices[at].astype(jnp.float32)


def write_kernel(*refs):
    sems = refs[6]
    copies = [pltpu.make_async_copy(refs[at], refs[at + 3], sems.at[at]) for at in range(3)]
    for copy in copies:
        copy.start()
    for copy in copies:
        copy.wait()


def fused(frames, lengths, cotangent, w_query, w_key, w_value, w_out):
    vmem = pl.BlockSpec(memory_space=pltpu.VMEM)
    hbm = pl.BlockSpec(memory_space=pltpu.HBM)
    bf16, f32 = jnp.bfloat16, jnp.float32
    per_head = pltpu.VMEM((4, 512, HEAD), bf16)
    own_head = pltpu.VMEM((4, 128, HEAD), bf16)
    results = pl.pallas_call(
        fused_kernel,
        out_shape=(
            pltpu.VMEM(frames.shape, bf16),
            pltpu.VMEM(frames.shape, bf16),
            pltpu.VMEM(w_out.shape, f32),
        ),
        in_specs=[hbm, pl.BlockSpec(memory_space=pltpu.SMEM)] + [hbm] * 5,
        out_specs=(vmem, vmem, vmem),
        scratch_shapes=[
            pltpu.VMEM((4, 128, 1024), bf16),
            pltpu.VMEM((128, 1024), bf16),
            pltpu.VMEM((2, 128, 512), bf16),
            pltpu.VMEM((4, 128, 512), bf16),
            pltpu.VMEM((4, 256, 512), bf16),
            pltpu.VMEM((4, 256, 512), bf16),
            pltpu.VMEM((4, 256, 512), bf16),
            pltpu.VMEM((4, 128, 1024), bf16),
            per_head,
            per_head,
            per_head,
            pltpu.VMEM((4, 4, 128, HEAD), bf16),
            per_head,
            pltpu.VMEM((4, 512, 1), f32),
            pltpu.VMEM((512, 1), f32),
            own_head,
            own_head,
            own_head,
            pltpu.VMEM((4, 2, 128, 256), bf16),
            pltpu.VMEM((8, 128, 256), bf16),
            pltpu.VMEM((4, 128, 256), bf16),
            pltpu.SemaphoreType.DMA((72,)),
            pltpu.SemaphoreType.DMA((72,)),
            pltpu.SemaphoreType.DMA((6,)),
        ],
        compiler_params=pltpu.CompilerParams(
            collective_id=0, has_side_effects=True, vmem_limit_bytes=56 * 1024 * 1024
        ),
    )(frames, lengths, cotangent, w_query, w_key, w_value, w_out)
    return pl.pallas_call(
        write_kernel,
        out_shape=tuple(jax.ShapeDtypeStruct(r.shape, r.dtype) for r in results),
        in_specs=[vmem] * 3,
        out_specs=(hbm, hbm, hbm),
        scratch_shapes=[pltpu.SemaphoreType.DMA((3,))],
        compiler_params=pltpu.CompilerParams(vmem_limit_bytes=4 * 1024 * 1024),
    )(*results)


def either(sizes, frames, lengths, cotangent, w_query, w_key, w_value, w_out):
    fits = sizes == (2, 4, 4) and frames.shape == (1, 128, 1024) and w_query.shape == (256, 512)
    chosen = fused if fits else shards
    return chosen(frames, lengths, cotangent, w_query, w_key, w_value, w_out)


def solution(mesh):
    in_specs = (
        P(("rep", "dp"), "ctx", None),
        P(("rep", "dp")),
        P(("rep", "dp"), "ctx", None),
        P("dp", None),
        P("dp", None),
        P("dp", None),
        P("dp", None),
    )
    out_specs = (P(("rep", "dp"), "ctx", None), P(("rep", "dp"), "ctx", None), P("dp", None))
    sizes = (mesh.shape["rep"], mesh.shape["dp"], mesh.shape["ctx"])
    body = functools.partial(either, sizes)
    return jax.shard_map(body, mesh=mesh, in_specs=in_specs, out_specs=out_specs, check_vma=False)
```

```python
import functools
import math

import jax
import jax.numpy as jnp
from jax import lax
from jax.experimental import pallas as pl
from jax.experimental.pallas import tpu as pltpu
from jax.sharding import PartitionSpec as P

HEAD = 128


MASKED_SCORE = -1e30


def head_split(matrix, head_count):
    return matrix.reshape(matrix.shape[0], head_count, matrix.shape[1] // head_count)


def forward_step(carry, key_part, value_part, offset, query_heads, length, score_scale):
    head_count = query_heads.shape[1]
    amount = key_part.shape[0]
    maxima, totals, accumulated = carry
    key_heads = head_split(key_part, head_count)
    value_heads = head_split(value_part, head_count)
    scores = (
        jnp.einsum("rhe,nhe->hrn", query_heads, key_heads, preferred_element_type=jnp.float32)
        * score_scale
    )
    usable = offset + jnp.arange(amount) < length
    scores = jnp.where(usable[None, None, :], scores, MASKED_SCORE)
    new_maxima = jnp.maximum(maxima, jnp.max(scores, axis=2))
    factor = jnp.exp(maxima - new_maxima)
    exponent = jnp.where(usable[None, None, :], jnp.exp(scores - new_maxima[:, :, None]), 0.0)
    totals = totals * factor + jnp.sum(exponent, axis=2)
    mixed = jnp.einsum(
        "hrn,nhe->hre",
        exponent.astype(jnp.bfloat16),
        value_heads,
        preferred_element_type=jnp.float32,
    )
    accumulated = accumulated * factor[:, :, None] + mixed
    return (new_maxima, totals, accumulated)


def query_step(
    grad_accum,
    key_part,
    value_part,
    offset,
    query_heads,
    context_heads,
    logsum,
    deltas,
    length,
    score_scale,
):
    head_count = query_heads.shape[1]
    amount = key_part.shape[0]
    key_heads = head_split(key_part, head_count)
    value_heads = head_split(value_part, head_count)
    scores = (
        jnp.einsum("rhe,nhe->hrn", query_heads, key_heads, preferred_element_type=jnp.float32)
        * score_scale
    )
    usable = offset + jnp.arange(amount) < length
    attention = jnp.where(usable[None, None, :], jnp.exp(scores - logsum[:, :, None]), 0.0)
    grad_prob = jnp.einsum(
        "rhe,nhe->hrn", context_heads, value_heads, preferred_element_type=jnp.float32
    )
    grad_score = (attention * (grad_prob - deltas[:, :, None])).astype(jnp.bfloat16)
    added = jnp.einsum("hrn,nhe->rhe", grad_score, key_heads, preferred_element_type=jnp.float32)
    return grad_accum + added * score_scale


def key_step(
    query_part,
    context_part,
    all_logsum,
    all_deltas,
    key_heads,
    value_heads,
    key_usable,
    score_scale,
):
    head_count = key_heads.shape[1]
    query_heads = head_split(query_part, head_count)
    context_heads = head_split(context_part, head_count)
    scores = (
        jnp.einsum("rhe,nhe->hrn", query_heads, key_heads, preferred_element_type=jnp.float32)
        * score_scale
    )
    attention = jnp.where(key_usable[None, None, :], jnp.exp(scores - all_logsum[:, :, None]), 0.0)
    grad_value = jnp.einsum(
        "hrn,rhe->nhe",
        attention.astype(jnp.bfloat16),
        context_heads,
        preferred_element_type=jnp.float32,
    )
    grad_prob = jnp.einsum(
        "rhe,nhe->hrn", context_heads, value_heads, preferred_element_type=jnp.float32
    )
    grad_score = (attention * (grad_prob - all_deltas[:, :, None])).astype(jnp.bfloat16)
    added = jnp.einsum("hrn,rhe->nhe", grad_score, query_heads, preferred_element_type=jnp.float32)
    return (added * score_scale, grad_value)


def back_project(gradient, weight):
    return lax.dot_general(
        gradient, weight, (((1,), (1,)), ((), ())), preferred_element_type=jnp.float32
    )


def shards(frames, lengths, cotangent, w_query, w_key, w_value, w_out):
    full_query, full_key, full_value, full_out = (
        lax.all_gather(w_query, "dp", axis=0, tiled=True),
        lax.all_gather(w_key, "dp", axis=0, tiled=True),
        lax.all_gather(w_value, "dp", axis=0, tiled=True),
        lax.all_gather(w_out, "dp", axis=0, tiled=True),
    )
    inputs = frames[0]
    upstream = cotangent[0]
    length = lengths[0]
    row_count = inputs.shape[0]
    inner_width = full_query.shape[1]
    head_count = inner_width // HEAD
    score_scale = HEAD ** (-0.5)
    first_frame = lax.axis_index("ctx") * row_count
    row_usable = first_frame + jnp.arange(row_count) < length
    queries = jnp.dot(inputs, full_query, preferred_element_type=jnp.float32).astype(jnp.bfloat16)
    keys = jnp.dot(inputs, full_key, preferred_element_type=jnp.float32).astype(jnp.bfloat16)
    values = jnp.dot(inputs, full_value, preferred_element_type=jnp.float32).astype(jnp.bfloat16)
    query_heads = head_split(queries, head_count)
    key_heads = head_split(keys, head_count)
    value_heads = head_split(values, head_count)
    start_state = (
        jnp.full((head_count, row_count), MASKED_SCORE, jnp.float32),
        jnp.zeros((head_count, row_count), jnp.float32),
        jnp.zeros((head_count, row_count, HEAD), jnp.float32),
    )
    all_keys, all_values = (
        lax.all_gather(keys, "ctx", axis=0, tiled=True),
        lax.all_gather(values, "ctx", axis=0, tiled=True),
    )
    key_block = row_count * math.gcd(max(1, 512 // row_count), lax.axis_size("ctx"))
    block_count = all_keys.shape[0] // key_block
    key_blocks = all_keys.reshape(block_count, key_block, inner_width)
    value_blocks = all_values.reshape(block_count, key_block, inner_width)
    block_starts = jnp.arange(block_count, dtype=jnp.int32) * key_block

    def scan_forward(current, scan_item):
        return (
            forward_step(
                current, scan_item[0], scan_item[1], scan_item[2], query_heads, length, score_scale
            ),
            None,
        )

    softmax_state, unused = lax.scan(
        scan_forward, start_state, (key_blocks, value_blocks, block_starts)
    )
    maxima, totals, accumulated = softmax_state
    context = (
        (accumulated / totals[:, :, None])
        .transpose(1, 0, 2)
        .reshape(row_count, inner_width)
        .astype(jnp.bfloat16)
    )
    logsum = maxima + jnp.log(totals)
    attended = jnp.dot(context, full_out, preferred_element_type=jnp.float32)
    attended = jnp.where(row_usable[:, None], attended, 0.0).astype(jnp.bfloat16)
    masked_grad = jnp.where(row_usable[:, None], upstream, jnp.zeros_like(upstream))
    grad_context = back_project(masked_grad, full_out).astype(jnp.bfloat16)
    deltas = jnp.sum(
        (grad_context.astype(jnp.float32) * context.astype(jnp.float32)).reshape(
            row_count, head_count, HEAD
        ),
        axis=2,
    )
    context_heads = head_split(grad_context, head_count)
    delta_heads = deltas.T
    all_logsum, all_deltas = (
        lax.all_gather(logsum, "ctx", axis=1, tiled=True),
        lax.all_gather(delta_heads, "ctx", axis=1, tiled=True),
    )
    zero_grad = jnp.zeros((row_count, head_count, HEAD), jnp.float32)

    def scan_query(current, scan_item):
        return (
            query_step(
                current,
                scan_item[0],
                scan_item[1],
                scan_item[2],
                query_heads,
                context_heads,
                logsum,
                delta_heads,
                length,
                score_scale,
            ),
            None,
        )

    grad_query, unused = lax.scan(scan_query, zero_grad, (key_blocks, value_blocks, block_starts))
    grad_key, grad_value = key_step(
        lax.all_gather(queries, "ctx", axis=0, tiled=True),
        lax.all_gather(grad_context, "ctx", axis=0, tiled=True),
        all_logsum,
        all_deltas,
        key_heads,
        value_heads,
        row_usable,
        score_scale,
    )
    grad_query = grad_query.reshape(row_count, inner_width).astype(jnp.bfloat16)
    grad_key = grad_key.reshape(row_count, inner_width).astype(jnp.bfloat16)
    grad_value = grad_value.reshape(row_count, inner_width).astype(jnp.bfloat16)
    grad_input = (
        back_project(grad_query, full_query)
        + back_project(grad_key, full_key)
        + back_project(grad_value, full_value)
    )
    grad_frames = grad_input.astype(jnp.bfloat16)
    summed_grad = lax.psum(
        lax.dot_general(
            context, masked_grad, (((0,), (0,)), ((), ())), preferred_element_type=jnp.float32
        ),
        ("rep", "ctx"),
    )
    grad_out = lax.psum_scatter(summed_grad, "dp", scatter_dimension=0, tiled=True)
    return (attended[None], grad_frames[None], grad_out)


MESH = pl.DeviceIdType.MESH


def dot(left, right, left_dim, right_dim):
    return lax.dot_general(
        left, right, (((left_dim,), (right_dim,)), ((), ())), preferred_element_type=jnp.float32
    )


def fused_kernel(
    frames_ref,
    length_ref,
    cot_ref,
    wq_ref,
    wk_ref,
    wv_ref,
    wo_ref,
    attended_ref,
    grad_frames_ref,
    grad_out_ref,
    xs,
    upstream,
    mine,
    cs,
    wq,
    wk,
    wv,
    wo,
    qs,
    ks,
    vs,
    gs,
    ctx,
    logsum,
    key_sum,
    value_sum,
    dq,
    dk,
    dv,
    part,
    part_in,
    sums,
    sums_in,
    slices,
    send_sem,
    recv_sem,
    local_sem,
):
    rep, dp, z = lax.axis_index("rep"), lax.axis_index("dp"), lax.axis_index("ctx")
    count = 4
    heads = 4
    rows = frames_ref.shape[1]
    full = rows * count
    scale = HEAD ** (-0.5)
    base2 = scale * math.log2(math.e)
    sibling = dp + 1 - 2 * lax.rem(dp, 2)
    across = lax.rem(dp + 2, 4)
    across_sibling = lax.rem(sibling + 2, 4)
    other_rep = 1 - rep
    group = rep * 4 + dp
    lower = z < 2
    middle = (z == 1) | (z == 2)
    side_at = jnp.clip(z - 1, 0, 1)

    local = [
        pltpu.make_async_copy(source, target, local_sem.at[at])
        for at, (source, target) in enumerate(
            (
                (cot_ref.at[0], upstream),
                (frames_ref.at[0], xs.at[z]),
                (wk_ref, wk.at[dp]),
                (wv_ref, wv.at[dp]),
                (wq_ref, wq.at[dp]),
                (wo_ref, wo.at[dp]),
            )
        )
    ]
    for copy in local:
        copy.start()

    barrier = pltpu.get_barrier_semaphore()
    for step in range(1, count):
        for to_rep in (rep, other_rep):
            pl.semaphore_signal(
                barrier,
                inc=1,
                device_id=(to_rep, dp, lax.rem(z + step, count)),
                device_id_type=MESH,
            )
    for step in range(1, 8):
        peer = lax.rem(group + step, 8)
        pl.semaphore_signal(
            barrier, inc=1, device_id=(peer // 4, lax.rem(peer, 4), z), device_id_type=MESH
        )
    pl.semaphore_wait(barrier, 13)

    def remote(source, target, sent, received, device):
        return pltpu.make_async_remote_copy(
            src_ref=source,
            dst_ref=target,
            send_sem=send_sem.at[sent],
            recv_sem=recv_sem.at[received],
            device_id=device,
            device_id_type=MESH,
        )

    def arrive(target, received):
        remote(target, target, received, received, (rep, dp, z)).wait_recv()

    def piece_of(which, slot, at):
        if which == 0:
            return xs.at[slot, pl.ds(at * (rows // 2), rows // 2)]
        return gs.at[slot, pl.ds(at * 2, 2)]

    def chain(which, side, hop, at):
        sign = 1 - 2 * side
        owner = z - sign * (hop - 1)
        slot = jnp.clip(owner, 0, count - 1)
        source = piece_of(which, slot, at)
        if which == 0 and hop == 1:
            source = frames_ref.at[0, pl.ds(at * (rows // 2), rows // 2)]
        target = jnp.clip(z + sign, 0, count - 1)
        index = which * 12 + side * 6 + (hop - 1) * 2 + at
        valid = (z + sign >= 0) & (z + sign < count) & (owner >= 0) & (owner < count)
        copy = remote(source, piece_of(which, slot, at), index, index, (rep, dp, target))
        return valid, copy

    def chain_send(which, hop, at):
        for side in range(2):
            valid, copy = chain(which, side, hop, at)

            @pl.when(valid)
            def _():
                copy.start()

    def chain_recv(which, hop, at):
        for side in range(2):
            owner = z - (1 - 2 * side) * hop
            slot = jnp.clip(owner, 0, count - 1)
            index = which * 12 + side * 6 + (hop - 1) * 2 + at

            @pl.when((owner >= 0) & (owner < count))
            def _():
                arrive(piece_of(which, slot, at), index)

    def gradient_pass(inward):
        for at in range(2):
            for side in range(2):

                @pl.when(middle & (lower == ((side == 0) == inward)))
                def _():
                    owner = z - (1 - 2 * side)
                    arrive(piece_of(1, owner, at), 12 + side * 6 + at)
                    chain(1, side, 2, at)[1].start()

    def chain_pass(which, hop, at):
        chain_recv(which, hop, at)
        if hop < 3:
            chain_send(which, hop + 1, at)

    weights = ((wo_ref, wo), (wk_ref, wk), (wv_ref, wv), (wq_ref, wq))

    def half(ref, which):
        size = ref.shape[0] // 2
        return ref.at[pl.ds(pl.multiple_of(which * size, size), size)]

    def chunk(ref, which, at):
        size = ref.shape[0] // 4
        return ref.at[pl.ds(pl.multiple_of((which * 2 + at) * size, size), size)]

    def weight_copy(piece, step):
        shard, pool = weights[piece]
        index = 24 + piece * 7 + step
        if step == 0:
            return remote(shard, pool.at[dp], index, index, (rep, sibling, z))
        if step < 3:
            target = chunk(pool.at[dp], rep, step - 1)
            return remote(chunk(shard, rep, step - 1), target, index, index, (rep, across, z))
        mine_at = pool.at[across]
        if step < 5:
            source = chunk(mine_at, rep, step - 3)
            return remote(source, source, index, index, (other_rep, dp, z))
        source = half(mine_at, rep if step == 5 else other_rep)
        return remote(source, source, index, index, (rep, sibling, z))

    def weight_recv(piece, step):
        pool = weights[piece][1]
        if step == 0:
            target = pool.at[sibling]
        elif step < 3:
            target = chunk(pool.at[across], rep, step - 1)
        elif step < 5:
            target = chunk(pool.at[across], other_rep, step - 3)
        else:
            target = half(pool.at[across_sibling], rep if step == 5 else other_rep)
        arrive(target, 24 + piece * 7 + step)

    def from_y(at):
        weight_recv(at // 2, 1 + at % 2)
        weight_copy(at // 2, 3 + at % 2).start()
        if at % 2 == 1:
            weight_copy(at // 2, 5).start()

    def from_x(at):
        weight_recv(at // 2, 3 + at % 2)
        if at % 2 == 1:
            weight_copy(at // 2, 6).start()

    def cot_copy(near):
        to = jnp.where(lower, 1, 2) if near else jnp.where(lower, 2, 1)
        sent = 52 + (0 if near else 1)
        return remote(mine.at[to - 1], cs.at[z], sent, 52 + z, (rep, dp, to))

    for at in range(2):
        chain_send(0, 1, at)
    for piece in range(4):
        for step in (1, 2):
            weight_copy(piece, step).start()
    for piece in range(4):
        weight_copy(piece, 0).start()
    for copy in local:
        copy.wait()

    length = length_ref[0]
    width = mine.shape[2]
    real = z * rows + lax.broadcasted_iota(jnp.int32, (rows, width), 0) < length
    for at in range(2):
        kept = upstream[:, at * width : (at + 1) * width].astype(jnp.float32)
        mine[at] = jnp.where(real, kept, 0.0).astype(jnp.bfloat16)
    cs[z] = mine[side_at]

    def whole(piece):
        for step in (0, 5, 6):
            weight_recv(piece, step)

    def project(pool, kept, first, blocks):
        inputs = xs[pl.ds(first, blocks)].reshape(blocks * rows, 1024)
        start = pl.multiple_of(first * rows, rows)
        matrix = dot(inputs, pool[...].reshape(1024, 512), 1, 0).astype(jnp.bfloat16)
        for head in range(heads):
            kept[head, pl.ds(start, blocks * rows), :] = matrix[:, head * HEAD : (head + 1) * HEAD]

    three = jnp.where(lower, 0, 1)
    last = jnp.where(lower, 3, 0)

    from_y(0)
    chain_pass(0, 1, 0)
    from_y(1)
    from_y(2)
    from_x(0)
    from_y(3)
    chain_pass(0, 1, 1)

    @pl.when(jnp.logical_not(middle))
    def _():
        cot_copy(True).start()

    cot_copy(False).start()
    from_x(1)
    from_y(4)
    from_x(2)
    from_y(5)
    chain_pass(0, 2, 0)
    from_x(3)
    from_y(6)
    from_x(4)
    from_y(7)
    chain_pass(0, 2, 1)
    whole(0)
    masked = jnp.concatenate([mine[0], mine[1]], axis=1)
    matrix = dot(masked, wo[...].reshape(512, 1024), 1, 1).astype(jnp.bfloat16)
    for head in range(heads):
        gs[z, head] = matrix[:, head * HEAD : (head + 1) * HEAD]
    for at in range(2):
        chain_send(1, 1, at)
    from_x(5)
    whole(1)
    project(wk, ks, three, 3)
    from_x(6)
    whole(2)
    project(wv, vs, three, 3)

    def project_last():
        project(wk, ks, last, 1)
        project(wv, vs, last, 1)

    @pl.when(middle)
    def _():
        project_last()

    from_x(7)

    @pl.when(jnp.logical_not(middle))
    def _():
        for at in range(2):
            chain_pass(0, 3, at)
        project_last()

    gradient_pass(True)
    whole(3)
    project(wq, qs, 0, 4)

    def key_mask(amount):
        return lax.broadcasted_iota(jnp.int32, (amount, full), 1) < length

    def sibling_copy(batch):
        sent = 56 + batch
        return remote(part.at[batch], part_in.at[batch], sent, sent, (rep, sibling, z))

    def sum_copy(which):
        to_rep, to_dp = ((rep, across), (other_rep, across), (other_rep, dp))[which]
        source = sums.at[which // 2, to_rep]
        sent = 58 + which
        return remote(source, sums_in.at[which], sent, sent, (to_rep, to_dp, z))

    def attend(head):
        amount = full // 2
        usable = key_mask(amount)
        for at in range(2):
            start = at * amount
            scores = dot(qs[head, pl.ds(start, amount), :], ks[head], 1, 1)
            scores = jnp.where(usable, scores, MASKED_SCORE)
            maxima = jnp.max(scores, axis=1, keepdims=True)
            exponent = jnp.exp2((scores - maxima) * base2)
            totals = jnp.sum(exponent, axis=1, keepdims=True)
            mixed = dot(exponent.astype(jnp.bfloat16), vs[head], 1, 0)
            ctx[head, pl.ds(start, amount), :] = (mixed * (1.0 / totals)).astype(jnp.bfloat16)
            logsum[head, pl.ds(start, amount), :] = maxima * base2 + jnp.log2(totals)

    def forward(batch, carry):
        shift = 2 * (1 - batch)
        head = lax.rem(sibling + shift, 4)
        attend(head)

        @pl.when(middle)
        def _():
            @pl.when(batch == 0)
            def _():
                for source in range(count):

                    @pl.when(z != source)
                    def _():
                        arrive(cs.at[source], 52 + source)

            product = dot(ctx[head], cs[...].reshape(full, width), 0, 0)
            part[batch] = product.astype(jnp.bfloat16)
            sibling_copy(batch).start()

            @pl.when(batch == 1)
            def _():
                gradient_pass(False)

        head = lax.rem(dp + shift, 4)
        attend(head)

        @pl.when(middle)
        def _():
            product = dot(ctx[head], cs[...].reshape(full, width), 0, 0)
            arrive(part_in.at[batch], 56 + batch)
            product = product + part_in[batch].astype(jnp.float32)
            for at in range(2):
                sums[batch, at] = product[:, at * 256 : (at + 1) * 256].astype(jnp.bfloat16)

            @pl.when(batch == 0)
            def _():
                sum_copy(0).start()
                sum_copy(1).start()

            @pl.when(batch == 1)
            def _():
                sum_copy(2).start()

        return carry

    lax.fori_loop(0, 2, forward, 0)

    @pl.when(jnp.logical_not(middle))
    def _():
        for at in range(2):
            chain_recv(1, 1, at)

    for at in range(2):
        chain_pass(1, 2, at)
    own = pl.ds(pl.multiple_of(z * rows, rows), rows)
    own_context = jnp.concatenate([ctx[head, own, :] for head in range(heads)], axis=1)
    attended = dot(own_context, wo[...].reshape(512, 1024), 1, 0)
    row_at = z * rows + lax.broadcasted_iota(jnp.int32, attended.shape, 0)
    attended_ref[0] = jnp.where(row_at < length, attended, 0.0).astype(jnp.bfloat16)
    def row_deltas(grads, context):
        terms = grads.astype(jnp.float32) * context.astype(jnp.float32)
        return jnp.sum(terms, axis=1, keepdims=True)

    def own_queries(head, carry):
        grads = gs[z, head]
        scores = dot(qs[head, own, :], ks[head], 1, 1) * base2
        attention = jnp.where(key_mask(rows), jnp.exp2(scores - logsum[head, own, :]), 0.0)
        grad_prob = dot(grads, vs[head], 1, 1)
        minus = row_deltas(grads, ctx[head, own, :])
        grad_score = (attention * (grad_prob - minus)).astype(jnp.bfloat16)
        dq[head] = (dot(grad_score, ks[head], 1, 0) * scale).astype(jnp.bfloat16)
        return carry

    def own_keys(first, blocks, head):
        some = pl.ds(pl.multiple_of(first * rows, rows), blocks * rows)
        queries = qs[head, some, :]
        grads = gs[pl.ds(first, blocks), head].reshape(blocks * rows, HEAD)
        scores = dot(queries, ks[head, own, :], 1, 1) * base2
        at = z * rows + lax.broadcasted_iota(jnp.int32, scores.shape, 1)
        attention = jnp.where(at < length, jnp.exp2(scores - logsum[head, some, :]), 0.0)
        values = dot(attention.astype(jnp.bfloat16), grads, 0, 0)
        grad_prob = dot(grads, vs[head, own, :], 1, 1)
        minus = row_deltas(grads, ctx[head, some, :])
        grad_score = (attention * (grad_prob - minus)).astype(jnp.bfloat16)
        return dot(grad_score, queries, 0, 0), values

    lax.fori_loop(0, heads, own_queries, 0)

    mine_slice = side_at * 2 + rep

    def slice_copy(step, turned):
        to_rep = other_rep if turned else rep
        block = slices.at[mine_slice]
        return remote(
            block,
            block,
            64 + step * 2 + turned,
            64 + mine_slice,
            (to_rep, dp, lax.rem(z + step, count)),
        )

    @pl.when(middle)
    def _():
        total = sums[1, rep].astype(jnp.float32)
        for which in range(3):
            arrive(sums_in.at[which], 58 + which)
            total = total + sums_in[which].astype(jnp.float32)
        slices[mine_slice] = total.astype(jnp.bfloat16)
        for step in (1, 3, 2, 0):
            for turned in range(2):
                if step + turned > 0:
                    slice_copy(step, turned).start()

    def three_keys(head, carry):
        key_sum[head], value_sum[head] = own_keys(three, 3, head)
        return carry

    lax.fori_loop(0, heads, three_keys, 0)
    for at in range(2):
        chain_pass(1, 3, at)

    def last_keys(head, carry):
        keys, values = own_keys(last, 1, head)
        dk[head] = ((key_sum[head] + keys) * scale).astype(jnp.bfloat16)
        dv[head] = (value_sum[head] + values).astype(jnp.bfloat16)
        return carry

    lax.fori_loop(0, heads, last_keys, 0)

    grads = [
        jnp.concatenate([kept[head] for head in range(heads)], axis=1) for kept in (dq, dk, dv)
    ]
    for shard in range(4):
        added = (
            dot(grads[0], wq[shard], 1, 1)
            + dot(grads[1], wk[shard], 1, 1)
            + dot(grads[2], wv[shard], 1, 1)
        )
        grad_frames_ref[0, :, shard * 256 : (shard + 1) * 256] = added.astype(jnp.bfloat16)

    for piece in range(4):
        for step in range(7):
            weight_copy(piece, step).wait_send()
    for which in range(2):
        for hop in range(1, count):
            for at in range(2):
                for side in range(2):
                    valid, copy = chain(which, side, hop, at)

                    @pl.when(valid)
                    def _():
                        copy.wait_send()

    @pl.when(jnp.logical_not(middle))
    def _():
        cot_copy(True).wait_send()

    cot_copy(False).wait_send()

    @pl.when(middle)
    def _():
        for batch in range(2):
            sibling_copy(batch).wait_send()
        for which in range(3):
            sum_copy(which).wait_send()

    for at in range(count):

        @pl.when(jnp.logical_not(middle & (mine_slice == at)))
        def _():
            arrive(slices.at[at], 64 + at)

    @pl.when(middle)
    def _():
        for step in range(count):
            for turned in range(2):
                if step + turned > 0:
                    slice_copy(step, turned).wait_send()

    for at in range(count):
        grad_out_ref[:, at * 256 : (at + 1) * 256] = slices[at].astype(jnp.float32)


def write_kernel(*refs):
    sems = refs[6]
    copies = [pltpu.make_async_copy(refs[at], refs[at + 3], sems.at[at]) for at in range(3)]
    for copy in copies:
        copy.start()
    for copy in copies:
        copy.wait()


def fused(frames, lengths, cotangent, w_query, w_key, w_value, w_out):
    vmem = pl.BlockSpec(memory_space=pltpu.VMEM)
    hbm = pl.BlockSpec(memory_space=pltpu.HBM)
    bf16, f32 = jnp.bfloat16, jnp.float32
    per_head = pltpu.VMEM((4, 512, HEAD), bf16)
    own_head = pltpu.VMEM((4, 128, HEAD), bf16)
    results = pl.pallas_call(
        fused_kernel,
        out_shape=(
            pltpu.VMEM(frames.shape, bf16),
            pltpu.VMEM(frames.shape, bf16),
            pltpu.VMEM(w_out.shape, f32),
        ),
        in_specs=[hbm, pl.BlockSpec(memory_space=pltpu.SMEM)] + [hbm] * 5,
        out_specs=(vmem, vmem, vmem),
        scratch_shapes=[
            pltpu.VMEM((4, 128, 1024), bf16),
            pltpu.VMEM((128, 1024), bf16),
            pltpu.VMEM((2, 128, 512), bf16),
            pltpu.VMEM((4, 128, 512), bf16),
            pltpu.VMEM((4, 256, 512), bf16),
            pltpu.VMEM((4, 256, 512), bf16),
            pltpu.VMEM((4, 256, 512), bf16),
            pltpu.VMEM((4, 128, 1024), bf16),
            per_head,
            per_head,
            per_head,
            pltpu.VMEM((4, 4, 128, HEAD), bf16),
            per_head,
            pltpu.VMEM((4, 512, 1), f32),
            pltpu.VMEM((4, 128, HEAD), f32),
            pltpu.VMEM((4, 128, HEAD), f32),
            own_head,
            own_head,
            own_head,
            pltpu.VMEM((2, 128, 512), bf16),
            pltpu.VMEM((2, 128, 512), bf16),
            pltpu.VMEM((2, 2, 128, 256), bf16),
            pltpu.VMEM((3, 128, 256), bf16),
            pltpu.VMEM((4, 128, 256), bf16),
            pltpu.SemaphoreType.DMA((72,)),
            pltpu.SemaphoreType.DMA((72,)),
            pltpu.SemaphoreType.DMA((6,)),
        ],
        compiler_params=pltpu.CompilerParams(
            collective_id=0, has_side_effects=True, vmem_limit_bytes=56 * 1024 * 1024
        ),
    )(frames, lengths, cotangent, w_query, w_key, w_value, w_out)
    return pl.pallas_call(
        write_kernel,
        out_shape=tuple(jax.ShapeDtypeStruct(r.shape, r.dtype) for r in results),
        in_specs=[vmem] * 3,
        out_specs=(hbm, hbm, hbm),
        scratch_shapes=[pltpu.SemaphoreType.DMA((3,))],
        compiler_params=pltpu.CompilerParams(vmem_limit_bytes=4 * 1024 * 1024),
    )(*results)


def either(sizes, frames, lengths, cotangent, w_query, w_key, w_value, w_out):
    fits = sizes == (2, 4, 4) and frames.shape == (1, 128, 1024) and w_query.shape == (256, 512)
    chosen = fused if fits else shards
    return chosen(frames, lengths, cotangent, w_query, w_key, w_value, w_out)


def solution(mesh):
    in_specs = (
        P(("rep", "dp"), "ctx", None),
        P(("rep", "dp")),
        P(("rep", "dp"), "ctx", None),
        P("dp", None),
        P("dp", None),
        P("dp", None),
        P("dp", None),
    )
    out_specs = (P(("rep", "dp"), "ctx", None), P(("rep", "dp"), "ctx", None), P("dp", None))
    sizes = (mesh.shape["rep"], mesh.shape["dp"], mesh.shape["ctx"])
    body = functools.partial(either, sizes)
    return jax.shard_map(body, mesh=mesh, in_specs=in_specs, out_specs=out_specs, check_vma=False)
```

```python
import functools
import math

import jax
import jax.numpy as jnp
from jax import lax
from jax.experimental import pallas as pl
from jax.experimental.pallas import tpu as pltpu
from jax.sharding import PartitionSpec as P

HEAD = 128


MASKED_SCORE = -1e30


def head_split(matrix, head_count):
    return matrix.reshape(matrix.shape[0], head_count, matrix.shape[1] // head_count)


def forward_step(carry, key_part, value_part, offset, query_heads, length, score_scale):
    head_count = query_heads.shape[1]
    amount = key_part.shape[0]
    maxima, totals, accumulated = carry
    key_heads = head_split(key_part, head_count)
    value_heads = head_split(value_part, head_count)
    scores = (
        jnp.einsum("rhe,nhe->hrn", query_heads, key_heads, preferred_element_type=jnp.float32)
        * score_scale
    )
    usable = offset + jnp.arange(amount) < length
    scores = jnp.where(usable[None, None, :], scores, MASKED_SCORE)
    new_maxima = jnp.maximum(maxima, jnp.max(scores, axis=2))
    factor = jnp.exp(maxima - new_maxima)
    exponent = jnp.where(usable[None, None, :], jnp.exp(scores - new_maxima[:, :, None]), 0.0)
    totals = totals * factor + jnp.sum(exponent, axis=2)
    mixed = jnp.einsum(
        "hrn,nhe->hre",
        exponent.astype(jnp.bfloat16),
        value_heads,
        preferred_element_type=jnp.float32,
    )
    accumulated = accumulated * factor[:, :, None] + mixed
    return (new_maxima, totals, accumulated)


def query_step(
    grad_accum,
    key_part,
    value_part,
    offset,
    query_heads,
    context_heads,
    logsum,
    deltas,
    length,
    score_scale,
):
    head_count = query_heads.shape[1]
    amount = key_part.shape[0]
    key_heads = head_split(key_part, head_count)
    value_heads = head_split(value_part, head_count)
    scores = (
        jnp.einsum("rhe,nhe->hrn", query_heads, key_heads, preferred_element_type=jnp.float32)
        * score_scale
    )
    usable = offset + jnp.arange(amount) < length
    attention = jnp.where(usable[None, None, :], jnp.exp(scores - logsum[:, :, None]), 0.0)
    grad_prob = jnp.einsum(
        "rhe,nhe->hrn", context_heads, value_heads, preferred_element_type=jnp.float32
    )
    grad_score = (attention * (grad_prob - deltas[:, :, None])).astype(jnp.bfloat16)
    added = jnp.einsum("hrn,nhe->rhe", grad_score, key_heads, preferred_element_type=jnp.float32)
    return grad_accum + added * score_scale


def key_step(
    query_part,
    context_part,
    all_logsum,
    all_deltas,
    key_heads,
    value_heads,
    key_usable,
    score_scale,
):
    head_count = key_heads.shape[1]
    query_heads = head_split(query_part, head_count)
    context_heads = head_split(context_part, head_count)
    scores = (
        jnp.einsum("rhe,nhe->hrn", query_heads, key_heads, preferred_element_type=jnp.float32)
        * score_scale
    )
    attention = jnp.where(key_usable[None, None, :], jnp.exp(scores - all_logsum[:, :, None]), 0.0)
    grad_value = jnp.einsum(
        "hrn,rhe->nhe",
        attention.astype(jnp.bfloat16),
        context_heads,
        preferred_element_type=jnp.float32,
    )
    grad_prob = jnp.einsum(
        "rhe,nhe->hrn", context_heads, value_heads, preferred_element_type=jnp.float32
    )
    grad_score = (attention * (grad_prob - all_deltas[:, :, None])).astype(jnp.bfloat16)
    added = jnp.einsum("hrn,rhe->nhe", grad_score, query_heads, preferred_element_type=jnp.float32)
    return (added * score_scale, grad_value)


def back_project(gradient, weight):
    return lax.dot_general(
        gradient, weight, (((1,), (1,)), ((), ())), preferred_element_type=jnp.float32
    )


def shards(frames, lengths, cotangent, w_query, w_key, w_value, w_out):
    full_query, full_key, full_value, full_out = (
        lax.all_gather(w_query, "dp", axis=0, tiled=True),
        lax.all_gather(w_key, "dp", axis=0, tiled=True),
        lax.all_gather(w_value, "dp", axis=0, tiled=True),
        lax.all_gather(w_out, "dp", axis=0, tiled=True),
    )
    inputs = frames[0]
    upstream = cotangent[0]
    length = lengths[0]
    row_count = inputs.shape[0]
    inner_width = full_query.shape[1]
    head_count = inner_width // HEAD
    score_scale = HEAD ** (-0.5)
    first_frame = lax.axis_index("ctx") * row_count
    row_usable = first_frame + jnp.arange(row_count) < length
    queries = jnp.dot(inputs, full_query, preferred_element_type=jnp.float32).astype(jnp.bfloat16)
    keys = jnp.dot(inputs, full_key, preferred_element_type=jnp.float32).astype(jnp.bfloat16)
    values = jnp.dot(inputs, full_value, preferred_element_type=jnp.float32).astype(jnp.bfloat16)
    query_heads = head_split(queries, head_count)
    key_heads = head_split(keys, head_count)
    value_heads = head_split(values, head_count)
    start_state = (
        jnp.full((head_count, row_count), MASKED_SCORE, jnp.float32),
        jnp.zeros((head_count, row_count), jnp.float32),
        jnp.zeros((head_count, row_count, HEAD), jnp.float32),
    )
    all_keys, all_values = (
        lax.all_gather(keys, "ctx", axis=0, tiled=True),
        lax.all_gather(values, "ctx", axis=0, tiled=True),
    )
    key_block = row_count * math.gcd(max(1, 512 // row_count), lax.axis_size("ctx"))
    block_count = all_keys.shape[0] // key_block
    key_blocks = all_keys.reshape(block_count, key_block, inner_width)
    value_blocks = all_values.reshape(block_count, key_block, inner_width)
    block_starts = jnp.arange(block_count, dtype=jnp.int32) * key_block

    def scan_forward(current, scan_item):
        return (
            forward_step(
                current, scan_item[0], scan_item[1], scan_item[2], query_heads, length, score_scale
            ),
            None,
        )

    softmax_state, unused = lax.scan(
        scan_forward, start_state, (key_blocks, value_blocks, block_starts)
    )
    maxima, totals, accumulated = softmax_state
    context = (
        (accumulated / totals[:, :, None])
        .transpose(1, 0, 2)
        .reshape(row_count, inner_width)
        .astype(jnp.bfloat16)
    )
    logsum = maxima + jnp.log(totals)
    attended = jnp.dot(context, full_out, preferred_element_type=jnp.float32)
    attended = jnp.where(row_usable[:, None], attended, 0.0).astype(jnp.bfloat16)
    masked_grad = jnp.where(row_usable[:, None], upstream, jnp.zeros_like(upstream))
    grad_context = back_project(masked_grad, full_out).astype(jnp.bfloat16)
    deltas = jnp.sum(
        (grad_context.astype(jnp.float32) * context.astype(jnp.float32)).reshape(
            row_count, head_count, HEAD
        ),
        axis=2,
    )
    context_heads = head_split(grad_context, head_count)
    delta_heads = deltas.T
    all_logsum, all_deltas = (
        lax.all_gather(logsum, "ctx", axis=1, tiled=True),
        lax.all_gather(delta_heads, "ctx", axis=1, tiled=True),
    )
    zero_grad = jnp.zeros((row_count, head_count, HEAD), jnp.float32)

    def scan_query(current, scan_item):
        return (
            query_step(
                current,
                scan_item[0],
                scan_item[1],
                scan_item[2],
                query_heads,
                context_heads,
                logsum,
                delta_heads,
                length,
                score_scale,
            ),
            None,
        )

    grad_query, unused = lax.scan(scan_query, zero_grad, (key_blocks, value_blocks, block_starts))
    grad_key, grad_value = key_step(
        lax.all_gather(queries, "ctx", axis=0, tiled=True),
        lax.all_gather(grad_context, "ctx", axis=0, tiled=True),
        all_logsum,
        all_deltas,
        key_heads,
        value_heads,
        row_usable,
        score_scale,
    )
    grad_query = grad_query.reshape(row_count, inner_width).astype(jnp.bfloat16)
    grad_key = grad_key.reshape(row_count, inner_width).astype(jnp.bfloat16)
    grad_value = grad_value.reshape(row_count, inner_width).astype(jnp.bfloat16)
    grad_input = (
        back_project(grad_query, full_query)
        + back_project(grad_key, full_key)
        + back_project(grad_value, full_value)
    )
    grad_frames = grad_input.astype(jnp.bfloat16)
    summed_grad = lax.psum(
        lax.dot_general(
            context, masked_grad, (((0,), (0,)), ((), ())), preferred_element_type=jnp.float32
        ),
        ("rep", "ctx"),
    )
    grad_out = lax.psum_scatter(summed_grad, "dp", scatter_dimension=0, tiled=True)
    return (attended[None], grad_frames[None], grad_out)


MESH = pl.DeviceIdType.MESH


def dot(left, right, left_dim, right_dim):
    return lax.dot_general(
        left, right, (((left_dim,), (right_dim,)), ((), ())), preferred_element_type=jnp.float32
    )


def fused_kernel(
    frames_ref,
    length_ref,
    cot_ref,
    wq_ref,
    wk_ref,
    wv_ref,
    wo_ref,
    attended_ref,
    grad_frames_ref,
    grad_out_ref,
    xs,
    upstream,
    mine,
    cs,
    wq,
    wk,
    wv,
    wo,
    qs,
    ks,
    vs,
    gs,
    ctx,
    logsum,
    exps,
    inverse,
    from_queries,
    key_sum,
    value_sum,
    dq,
    dk,
    dv,
    part,
    part_in,
    sums,
    sums_in,
    slices,
    send_sem,
    recv_sem,
    local_sem,
):
    rep, dp, z = lax.axis_index("rep"), lax.axis_index("dp"), lax.axis_index("ctx")
    count = 4
    heads = 4
    rows = frames_ref.shape[1]
    full = rows * count
    scale = HEAD ** (-0.5)
    base2 = scale * math.log2(math.e)
    sibling = dp + 1 - 2 * lax.rem(dp, 2)
    across = lax.rem(dp + 2, 4)
    across_sibling = lax.rem(sibling + 2, 4)
    other_rep = 1 - rep
    group = rep * 4 + dp
    lower = z < 2
    middle = (z == 1) | (z == 2)
    side_at = jnp.clip(z - 1, 0, 1)

    local = [
        pltpu.make_async_copy(source, target, local_sem.at[at])
        for at, (source, target) in enumerate(
            (
                (cot_ref.at[0], upstream),
                (frames_ref.at[0], xs.at[z]),
                (wk_ref, wk.at[dp]),
                (wv_ref, wv.at[dp]),
                (wq_ref, wq.at[dp]),
                (wo_ref, wo.at[dp]),
            )
        )
    ]
    for copy in local:
        copy.start()

    barrier = pltpu.get_barrier_semaphore()
    for step in range(1, count):
        for to_rep in (rep, other_rep):
            pl.semaphore_signal(
                barrier,
                inc=1,
                device_id=(to_rep, dp, lax.rem(z + step, count)),
                device_id_type=MESH,
            )
    for step in range(1, 8):
        peer = lax.rem(group + step, 8)
        pl.semaphore_signal(
            barrier, inc=1, device_id=(peer // 4, lax.rem(peer, 4), z), device_id_type=MESH
        )
    pl.semaphore_wait(barrier, 13)

    def remote(source, target, sent, received, device):
        return pltpu.make_async_remote_copy(
            src_ref=source,
            dst_ref=target,
            send_sem=send_sem.at[sent],
            recv_sem=recv_sem.at[received],
            device_id=device,
            device_id_type=MESH,
        )

    def arrive(target, received):
        remote(target, target, received, received, (rep, dp, z)).wait_recv()

    def piece_of(which, slot, at):
        if which == 0:
            return xs.at[slot, pl.ds(at * (rows // 2), rows // 2)]
        return gs.at[slot, pl.ds(at * 2, 2)]

    def chain(which, side, hop, at):
        sign = 1 - 2 * side
        owner = z - sign * (hop - 1)
        slot = jnp.clip(owner, 0, count - 1)
        source = piece_of(which, slot, at)
        if which == 0 and hop == 1:
            source = frames_ref.at[0, pl.ds(at * (rows // 2), rows // 2)]
        target = jnp.clip(z + sign, 0, count - 1)
        index = which * 12 + side * 6 + (hop - 1) * 2 + at
        valid = (z + sign >= 0) & (z + sign < count) & (owner >= 0) & (owner < count)
        copy = remote(source, piece_of(which, slot, at), index, index, (rep, dp, target))
        return valid, copy

    def chain_send(which, hop, at):
        for side in range(2):
            valid, copy = chain(which, side, hop, at)

            @pl.when(valid)
            def _():
                copy.start()

    def chain_recv(which, hop, at):
        for side in range(2):
            owner = z - (1 - 2 * side) * hop
            slot = jnp.clip(owner, 0, count - 1)
            index = which * 12 + side * 6 + (hop - 1) * 2 + at

            @pl.when((owner >= 0) & (owner < count))
            def _():
                arrive(piece_of(which, slot, at), index)

    def gradient_pass(inward):
        for at in range(2):
            for side in range(2):

                @pl.when(middle & (lower == ((side == 0) == inward)))
                def _():
                    owner = z - (1 - 2 * side)
                    arrive(piece_of(1, owner, at), 12 + side * 6 + at)
                    chain(1, side, 2, at)[1].start()

    def chain_pass(which, hop, at):
        chain_recv(which, hop, at)
        if hop < 3:
            chain_send(which, hop + 1, at)

    weights = ((wo_ref, wo), (wk_ref, wk), (wq_ref, wq), (wv_ref, wv))

    def half(ref, which):
        size = ref.shape[0] // 2
        return ref.at[pl.ds(pl.multiple_of(which * size, size), size)]

    def chunk(ref, which, at):
        size = ref.shape[0] // 4
        return ref.at[pl.ds(pl.multiple_of((which * 2 + at) * size, size), size)]

    def weight_copy(piece, step):
        shard, pool = weights[piece]
        index = 24 + piece * 7 + step
        if step == 0:
            return remote(shard, pool.at[dp], index, index, (rep, sibling, z))
        if step < 3:
            target = chunk(pool.at[dp], rep, step - 1)
            return remote(chunk(shard, rep, step - 1), target, index, index, (rep, across, z))
        mine_at = pool.at[across]
        if step < 5:
            source = chunk(mine_at, rep, step - 3)
            return remote(source, source, index, index, (other_rep, dp, z))
        source = half(mine_at, rep if step == 5 else other_rep)
        return remote(source, source, index, index, (rep, sibling, z))

    def weight_recv(piece, step):
        pool = weights[piece][1]
        if step == 0:
            target = pool.at[sibling]
        elif step < 3:
            target = chunk(pool.at[across], rep, step - 1)
        elif step < 5:
            target = chunk(pool.at[across], other_rep, step - 3)
        else:
            target = half(pool.at[across_sibling], rep if step == 5 else other_rep)
        arrive(target, 24 + piece * 7 + step)

    def from_y(at):
        weight_recv(at // 2, 1 + at % 2)
        weight_copy(at // 2, 3 + at % 2).start()
        if at % 2 == 1:
            weight_copy(at // 2, 5).start()

    def from_x(at):
        weight_recv(at // 2, 3 + at % 2)
        if at % 2 == 1:
            weight_copy(at // 2, 6).start()

    def cot_copy(near):
        to = jnp.where(lower, 1, 2) if near else jnp.where(lower, 2, 1)
        sent = 52 + (0 if near else 1)
        return remote(mine.at[to - 1], cs.at[z], sent, 52 + z, (rep, dp, to))

    for at in range(2):
        chain_send(0, 1, at)
    for piece in range(4):
        for step in (1, 2):
            weight_copy(piece, step).start()
    for piece in range(4):
        weight_copy(piece, 0).start()
    for copy in local:
        copy.wait()

    length = length_ref[0]
    width = mine.shape[2]
    real = z * rows + lax.broadcasted_iota(jnp.int32, (rows, width), 0) < length
    for at in range(2):
        kept = upstream[:, at * width : (at + 1) * width].astype(jnp.float32)
        mine[at] = jnp.where(real, kept, 0.0).astype(jnp.bfloat16)
    cs[z] = mine[side_at]

    def whole(piece):
        for step in (0, 5, 6):
            weight_recv(piece, step)

    def project(pool, kept, first, blocks):
        inputs = xs[pl.ds(first, blocks)].reshape(blocks * rows, 1024)
        start = pl.multiple_of(first * rows, rows)
        matrix = dot(inputs, pool[...].reshape(1024, 512), 1, 0).astype(jnp.bfloat16)
        for head in range(heads):
            kept[head, pl.ds(start, blocks * rows), :] = matrix[:, head * HEAD : (head + 1) * HEAD]

    three = jnp.where(lower, 0, 1)
    last = jnp.where(lower, 3, 0)

    @pl.when(jnp.logical_not(middle))
    def _():
        cot_copy(True).start()
        cot_copy(False).start()

    from_y(0)
    chain_pass(0, 1, 0)
    from_y(1)
    from_y(2)
    from_x(0)
    from_y(3)
    chain_pass(0, 1, 1)

    @pl.when(middle)
    def _():
        cot_copy(False).start()

    from_x(1)
    from_y(4)
    from_x(2)
    from_y(5)
    chain_pass(0, 2, 0)
    from_x(3)
    from_y(6)
    from_x(4)
    from_y(7)
    chain_pass(0, 2, 1)
    whole(0)
    masked = jnp.concatenate([mine[0], mine[1]], axis=1)
    matrix = dot(masked, wo[...].reshape(512, 1024), 1, 1).astype(jnp.bfloat16)
    for head in range(heads):
        gs[z, head] = matrix[:, head * HEAD : (head + 1) * HEAD]
    for at in range(2):
        chain_send(1, 1, at)
    from_x(5)
    whole(1)
    project(wk, ks, three, 3)
    from_x(6)
    whole(2)
    project(wq, qs, three, 3)

    def project_last():
        project(wk, ks, last, 1)
        project(wq, qs, last, 1)

    def key_mask(amount):
        return lax.broadcasted_iota(jnp.int32, (amount, full), 1) < length

    def exponents(head, carry):
        amount = full // 2
        usable = key_mask(amount)
        for at in range(2):
            some = pl.ds(at * amount, amount)
            scores = dot(qs[head, some, :], ks[head], 1, 1)
            scores = jnp.where(usable, scores, MASKED_SCORE)
            maxima = jnp.max(scores, axis=1, keepdims=True)
            exponent = jnp.exp2((scores - maxima) * base2)
            totals = jnp.sum(exponent, axis=1, keepdims=True)
            exps[head, some, :] = exponent.astype(jnp.bfloat16)
            inverse[head, some, :] = 1.0 / totals
            logsum[head, some, :] = maxima * base2 + jnp.log2(totals)
        return carry

    @pl.when(middle)
    def _():
        project_last()
        lax.fori_loop(0, 2, exponents, 0)
        from_x(7)
        gradient_pass(True)
        lax.fori_loop(2, 4, exponents, 0)

    @pl.when(jnp.logical_not(middle))
    def _():
        from_x(7)
        for at in range(2):
            chain_pass(0, 3, at)
        project_last()
        lax.fori_loop(0, 4, exponents, 0)

    whole(3)
    project(wv, vs, 0, 4)

    def sibling_copy(batch):
        sent = 56 + batch
        return remote(part.at[batch], part_in.at[batch], sent, sent, (rep, sibling, z))

    def sum_copy(which):
        to_rep, to_dp = ((rep, across), (other_rep, across), (other_rep, dp))[which]
        source = sums.at[which // 2, to_rep]
        sent = 58 + which
        return remote(source, sums_in.at[which], sent, sent, (to_rep, to_dp, z))

    def attend(head):
        mixed = dot(exps[head], vs[head], 1, 0)
        ctx[head] = (mixed * inverse[head]).astype(jnp.bfloat16)

    def for_sibling(batch, carry):
        head = lax.rem(sibling + 2 * (1 - batch), 4)
        attend(head)

        @pl.when(middle)
        def _():
            @pl.when(batch == 0)
            def _():
                for source in range(count):

                    @pl.when(z != source)
                    def _():
                        arrive(cs.at[source], 52 + source)

            product = dot(ctx[head], cs[...].reshape(full, width), 0, 0)
            part[batch] = product.astype(jnp.bfloat16)
            sibling_copy(batch).start()

        return carry

    def for_plane(batch, carry):
        head = lax.rem(dp + 2 * (1 - batch), 4)
        attend(head)

        @pl.when(middle)
        def _():
            product = dot(ctx[head], cs[...].reshape(full, width), 0, 0)
            arrive(part_in.at[batch], 56 + batch)
            product = product + part_in[batch].astype(jnp.float32)
            for at in range(2):
                sums[batch, at] = product[:, at * 256 : (at + 1) * 256].astype(jnp.bfloat16)

            @pl.when(batch == 0)
            def _():
                sum_copy(0).start()
                sum_copy(1).start()

            @pl.when(batch == 1)
            def _():
                sum_copy(2).start()

        return carry

    lax.fori_loop(0, 2, for_sibling, 0)
    gradient_pass(False)
    lax.fori_loop(0, 2, for_plane, 0)

    @pl.when(jnp.logical_not(middle))
    def _():
        for at in range(2):
            chain_recv(1, 1, at)

    for at in range(2):
        chain_pass(1, 2, at)
    own = pl.ds(pl.multiple_of(z * rows, rows), rows)
    own_context = jnp.concatenate([ctx[head, own, :] for head in range(heads)], axis=1)
    attended = dot(own_context, wo[...].reshape(512, 1024), 1, 0)
    row_at = z * rows + lax.broadcasted_iota(jnp.int32, attended.shape, 0)
    attended_ref[0] = jnp.where(row_at < length, attended, 0.0).astype(jnp.bfloat16)
    def row_deltas(grads, context):
        terms = grads.astype(jnp.float32) * context.astype(jnp.float32)
        return jnp.sum(terms, axis=1, keepdims=True)

    def own_queries(head, carry):
        grads = gs[z, head]
        scores = dot(qs[head, own, :], ks[head], 1, 1) * base2
        attention = jnp.where(key_mask(rows), jnp.exp2(scores - logsum[head, own, :]), 0.0)
        grad_prob = dot(grads, vs[head], 1, 1)
        minus = row_deltas(grads, ctx[head, own, :])
        grad_score = (attention * (grad_prob - minus)).astype(jnp.bfloat16)
        dq[head] = (dot(grad_score, ks[head], 1, 0) * scale).astype(jnp.bfloat16)
        return carry

    def own_keys(first, blocks, head):
        some = pl.ds(pl.multiple_of(first * rows, rows), blocks * rows)
        queries = qs[head, some, :]
        grads = gs[pl.ds(first, blocks), head].reshape(blocks * rows, HEAD)
        scores = dot(queries, ks[head, own, :], 1, 1) * base2
        at = z * rows + lax.broadcasted_iota(jnp.int32, scores.shape, 1)
        attention = jnp.where(at < length, jnp.exp2(scores - logsum[head, some, :]), 0.0)
        values = dot(attention.astype(jnp.bfloat16), grads, 0, 0)
        grad_prob = dot(grads, vs[head, own, :], 1, 1)
        minus = row_deltas(grads, ctx[head, some, :])
        grad_score = (attention * (grad_prob - minus)).astype(jnp.bfloat16)
        return dot(grad_score, queries, 0, 0), values

    lax.fori_loop(0, heads, own_queries, 0)

    mine_slice = side_at * 2 + rep

    def slice_copy(step, turned):
        to_rep = other_rep if turned else rep
        block = slices.at[mine_slice]
        return remote(
            block,
            block,
            64 + step * 2 + turned,
            64 + mine_slice,
            (to_rep, dp, lax.rem(z + step, count)),
        )

    @pl.when(middle)
    def _():
        total = sums[1, rep].astype(jnp.float32)
        for which in range(3):
            arrive(sums_in.at[which], 58 + which)
            total = total + sums_in[which].astype(jnp.float32)
        slices[mine_slice] = total.astype(jnp.bfloat16)
        low, high, mate = lax.rem(count - z, count), 3 - z, jnp.where(lower, 1, 3)
        for step in (low, mate, high):
            for turned in (1, 0):
                slice_copy(step, turned).start()
        slice_copy(0, 1).start()

    def three_keys(head, carry):
        key_sum[head], value_sum[head] = own_keys(three, 3, head)
        return carry

    lax.fori_loop(0, heads, three_keys, 0)
    by_query = jnp.concatenate([dq[head] for head in range(heads)], axis=1)
    for shard in range(4):
        from_queries[:, shard * 256 : (shard + 1) * 256] = dot(by_query, wq[shard], 1, 1)

    for at in range(2):
        chain_pass(1, 3, at)

    def last_keys(head, carry):
        keys, values = own_keys(last, 1, head)
        dk[head] = ((key_sum[head] + keys) * scale).astype(jnp.bfloat16)
        dv[head] = (value_sum[head] + values).astype(jnp.bfloat16)
        return carry

    lax.fori_loop(0, heads, last_keys, 0)

    by_key, by_value = (
        jnp.concatenate([kept[head] for head in range(heads)], axis=1) for kept in (dk, dv)
    )
    for shard in range(4):
        columns = slice(shard * 256, (shard + 1) * 256)
        added = dot(by_key, wk[shard], 1, 1) + dot(by_value, wv[shard], 1, 1)
        added = added + from_queries[:, columns]
        grad_frames_ref[0, :, columns] = added.astype(jnp.bfloat16)

    for piece in range(4):
        for step in range(7):
            weight_copy(piece, step).wait_send()
    for which in range(2):
        for hop in range(1, count):
            for at in range(2):
                for side in range(2):
                    valid, copy = chain(which, side, hop, at)

                    @pl.when(valid)
                    def _():
                        copy.wait_send()

    @pl.when(jnp.logical_not(middle))
    def _():
        cot_copy(True).wait_send()

    cot_copy(False).wait_send()

    @pl.when(middle)
    def _():
        for batch in range(2):
            sibling_copy(batch).wait_send()
        for which in range(3):
            sum_copy(which).wait_send()

    for at in range(count):

        @pl.when(jnp.logical_not(middle & (mine_slice == at)))
        def _():
            arrive(slices.at[at], 64 + at)

    @pl.when(middle)
    def _():
        for step in range(count):
            for turned in range(2):
                if step + turned > 0:
                    slice_copy(step, turned).wait_send()

    for at in range(count):
        grad_out_ref[:, at * 256 : (at + 1) * 256] = slices[at].astype(jnp.float32)


def write_kernel(*refs):
    sems = refs[6]
    copies = [pltpu.make_async_copy(refs[at], refs[at + 3], sems.at[at]) for at in range(3)]
    for copy in copies:
        copy.start()
    for copy in copies:
        copy.wait()


def fused(frames, lengths, cotangent, w_query, w_key, w_value, w_out):
    vmem = pl.BlockSpec(memory_space=pltpu.VMEM)
    hbm = pl.BlockSpec(memory_space=pltpu.HBM)
    bf16, f32 = jnp.bfloat16, jnp.float32
    per_head = pltpu.VMEM((4, 512, HEAD), bf16)
    own_head = pltpu.VMEM((4, 128, HEAD), bf16)
    results = pl.pallas_call(
        fused_kernel,
        out_shape=(
            pltpu.VMEM(frames.shape, bf16),
            pltpu.VMEM(frames.shape, bf16),
            pltpu.VMEM(w_out.shape, f32),
        ),
        in_specs=[hbm, pl.BlockSpec(memory_space=pltpu.SMEM)] + [hbm] * 5,
        out_specs=(vmem, vmem, vmem),
        scratch_shapes=[
            pltpu.VMEM((4, 128, 1024), bf16),
            pltpu.VMEM((128, 1024), bf16),
            pltpu.VMEM((2, 128, 512), bf16),
            pltpu.VMEM((4, 128, 512), bf16),
            pltpu.VMEM((4, 256, 512), bf16),
            pltpu.VMEM((4, 256, 512), bf16),
            pltpu.VMEM((4, 256, 512), bf16),
            pltpu.VMEM((4, 128, 1024), bf16),
            per_head,
            per_head,
            per_head,
            pltpu.VMEM((4, 4, 128, HEAD), bf16),
            per_head,
            pltpu.VMEM((4, 512, 1), f32),
            pltpu.VMEM((4, 512, 512), bf16),
            pltpu.VMEM((4, 512, 1), f32),
            pltpu.VMEM((128, 1024), f32),
            pltpu.VMEM((4, 128, HEAD), f32),
            pltpu.VMEM((4, 128, HEAD), f32),
            own_head,
            own_head,
            own_head,
            pltpu.VMEM((2, 128, 512), bf16),
            pltpu.VMEM((2, 128, 512), bf16),
            pltpu.VMEM((2, 2, 128, 256), bf16),
            pltpu.VMEM((3, 128, 256), bf16),
            pltpu.VMEM((4, 128, 256), bf16),
            pltpu.SemaphoreType.DMA((72,)),
            pltpu.SemaphoreType.DMA((72,)),
            pltpu.SemaphoreType.DMA((6,)),
        ],
        compiler_params=pltpu.CompilerParams(
            collective_id=0, has_side_effects=True, vmem_limit_bytes=56 * 1024 * 1024
        ),
    )(frames, lengths, cotangent, w_query, w_key, w_value, w_out)
    return pl.pallas_call(
        write_kernel,
        out_shape=tuple(jax.ShapeDtypeStruct(r.shape, r.dtype) for r in results),
        in_specs=[vmem] * 3,
        out_specs=(hbm, hbm, hbm),
        scratch_shapes=[pltpu.SemaphoreType.DMA((3,))],
        compiler_params=pltpu.CompilerParams(vmem_limit_bytes=4 * 1024 * 1024),
    )(*results)


def either(sizes, frames, lengths, cotangent, w_query, w_key, w_value, w_out):
    fits = sizes == (2, 4, 4) and frames.shape == (1, 128, 1024) and w_query.shape == (256, 512)
    chosen = fused if fits else shards
    return chosen(frames, lengths, cotangent, w_query, w_key, w_value, w_out)


def solution(mesh):
    in_specs = (
        P(("rep", "dp"), "ctx", None),
        P(("rep", "dp")),
        P(("rep", "dp"), "ctx", None),
        P("dp", None),
        P("dp", None),
        P("dp", None),
        P("dp", None),
    )
    out_specs = (P(("rep", "dp"), "ctx", None), P(("rep", "dp"), "ctx", None), P("dp", None))
    sizes = (mesh.shape["rep"], mesh.shape["dp"], mesh.shape["ctx"])
    body = functools.partial(either, sizes)
    return jax.shard_map(body, mesh=mesh, in_specs=in_specs, out_specs=out_specs, check_vma=False)
```

```python
import functools
import math

import jax
import jax.numpy as jnp
from jax import lax
from jax.experimental import pallas as pl
from jax.experimental.pallas import tpu as pltpu
from jax.sharding import PartitionSpec as P

HEAD = 128


MASKED_SCORE = -1e30


def head_split(matrix, head_count):
    return matrix.reshape(matrix.shape[0], head_count, matrix.shape[1] // head_count)


def forward_step(carry, key_part, value_part, offset, query_heads, length, score_scale):
    head_count = query_heads.shape[1]
    amount = key_part.shape[0]
    maxima, totals, accumulated = carry
    key_heads = head_split(key_part, head_count)
    value_heads = head_split(value_part, head_count)
    scores = (
        jnp.einsum("rhe,nhe->hrn", query_heads, key_heads, preferred_element_type=jnp.float32)
        * score_scale
    )
    usable = offset + jnp.arange(amount) < length
    scores = jnp.where(usable[None, None, :], scores, MASKED_SCORE)
    new_maxima = jnp.maximum(maxima, jnp.max(scores, axis=2))
    factor = jnp.exp(maxima - new_maxima)
    exponent = jnp.where(usable[None, None, :], jnp.exp(scores - new_maxima[:, :, None]), 0.0)
    totals = totals * factor + jnp.sum(exponent, axis=2)
    mixed = jnp.einsum(
        "hrn,nhe->hre",
        exponent.astype(jnp.bfloat16),
        value_heads,
        preferred_element_type=jnp.float32,
    )
    accumulated = accumulated * factor[:, :, None] + mixed
    return (new_maxima, totals, accumulated)


def query_step(
    grad_accum,
    key_part,
    value_part,
    offset,
    query_heads,
    context_heads,
    logsum,
    deltas,
    length,
    score_scale,
):
    head_count = query_heads.shape[1]
    amount = key_part.shape[0]
    key_heads = head_split(key_part, head_count)
    value_heads = head_split(value_part, head_count)
    scores = (
        jnp.einsum("rhe,nhe->hrn", query_heads, key_heads, preferred_element_type=jnp.float32)
        * score_scale
    )
    usable = offset + jnp.arange(amount) < length
    attention = jnp.where(usable[None, None, :], jnp.exp(scores - logsum[:, :, None]), 0.0)
    grad_prob = jnp.einsum(
        "rhe,nhe->hrn", context_heads, value_heads, preferred_element_type=jnp.float32
    )
    grad_score = (attention * (grad_prob - deltas[:, :, None])).astype(jnp.bfloat16)
    added = jnp.einsum("hrn,nhe->rhe", grad_score, key_heads, preferred_element_type=jnp.float32)
    return grad_accum + added * score_scale


def key_step(
    query_part,
    context_part,
    all_logsum,
    all_deltas,
    key_heads,
    value_heads,
    key_usable,
    score_scale,
):
    head_count = key_heads.shape[1]
    query_heads = head_split(query_part, head_count)
    context_heads = head_split(context_part, head_count)
    scores = (
        jnp.einsum("rhe,nhe->hrn", query_heads, key_heads, preferred_element_type=jnp.float32)
        * score_scale
    )
    attention = jnp.where(key_usable[None, None, :], jnp.exp(scores - all_logsum[:, :, None]), 0.0)
    grad_value = jnp.einsum(
        "hrn,rhe->nhe",
        attention.astype(jnp.bfloat16),
        context_heads,
        preferred_element_type=jnp.float32,
    )
    grad_prob = jnp.einsum(
        "rhe,nhe->hrn", context_heads, value_heads, preferred_element_type=jnp.float32
    )
    grad_score = (attention * (grad_prob - all_deltas[:, :, None])).astype(jnp.bfloat16)
    added = jnp.einsum("hrn,rhe->nhe", grad_score, query_heads, preferred_element_type=jnp.float32)
    return (added * score_scale, grad_value)


def back_project(gradient, weight):
    return lax.dot_general(
        gradient, weight, (((1,), (1,)), ((), ())), preferred_element_type=jnp.float32
    )


def shards(frames, lengths, cotangent, w_query, w_key, w_value, w_out):
    full_query, full_key, full_value, full_out = (
        lax.all_gather(w_query, "dp", axis=0, tiled=True),
        lax.all_gather(w_key, "dp", axis=0, tiled=True),
        lax.all_gather(w_value, "dp", axis=0, tiled=True),
        lax.all_gather(w_out, "dp", axis=0, tiled=True),
    )
    inputs = frames[0]
    upstream = cotangent[0]
    length = lengths[0]
    row_count = inputs.shape[0]
    inner_width = full_query.shape[1]
    head_count = inner_width // HEAD
    score_scale = HEAD ** (-0.5)
    first_frame = lax.axis_index("ctx") * row_count
    row_usable = first_frame + jnp.arange(row_count) < length
    queries = jnp.dot(inputs, full_query, preferred_element_type=jnp.float32).astype(jnp.bfloat16)
    keys = jnp.dot(inputs, full_key, preferred_element_type=jnp.float32).astype(jnp.bfloat16)
    values = jnp.dot(inputs, full_value, preferred_element_type=jnp.float32).astype(jnp.bfloat16)
    query_heads = head_split(queries, head_count)
    key_heads = head_split(keys, head_count)
    value_heads = head_split(values, head_count)
    start_state = (
        jnp.full((head_count, row_count), MASKED_SCORE, jnp.float32),
        jnp.zeros((head_count, row_count), jnp.float32),
        jnp.zeros((head_count, row_count, HEAD), jnp.float32),
    )
    all_keys, all_values = (
        lax.all_gather(keys, "ctx", axis=0, tiled=True),
        lax.all_gather(values, "ctx", axis=0, tiled=True),
    )
    key_block = row_count * math.gcd(max(1, 512 // row_count), lax.axis_size("ctx"))
    block_count = all_keys.shape[0] // key_block
    key_blocks = all_keys.reshape(block_count, key_block, inner_width)
    value_blocks = all_values.reshape(block_count, key_block, inner_width)
    block_starts = jnp.arange(block_count, dtype=jnp.int32) * key_block

    def scan_forward(current, scan_item):
        return (
            forward_step(
                current, scan_item[0], scan_item[1], scan_item[2], query_heads, length, score_scale
            ),
            None,
        )

    softmax_state, unused = lax.scan(
        scan_forward, start_state, (key_blocks, value_blocks, block_starts)
    )
    maxima, totals, accumulated = softmax_state
    context = (
        (accumulated / totals[:, :, None])
        .transpose(1, 0, 2)
        .reshape(row_count, inner_width)
        .astype(jnp.bfloat16)
    )
    logsum = maxima + jnp.log(totals)
    attended = jnp.dot(context, full_out, preferred_element_type=jnp.float32)
    attended = jnp.where(row_usable[:, None], attended, 0.0).astype(jnp.bfloat16)
    masked_grad = jnp.where(row_usable[:, None], upstream, jnp.zeros_like(upstream))
    grad_context = back_project(masked_grad, full_out).astype(jnp.bfloat16)
    deltas = jnp.sum(
        (grad_context.astype(jnp.float32) * context.astype(jnp.float32)).reshape(
            row_count, head_count, HEAD
        ),
        axis=2,
    )
    context_heads = head_split(grad_context, head_count)
    delta_heads = deltas.T
    all_logsum, all_deltas = (
        lax.all_gather(logsum, "ctx", axis=1, tiled=True),
        lax.all_gather(delta_heads, "ctx", axis=1, tiled=True),
    )
    zero_grad = jnp.zeros((row_count, head_count, HEAD), jnp.float32)

    def scan_query(current, scan_item):
        return (
            query_step(
                current,
                scan_item[0],
                scan_item[1],
                scan_item[2],
                query_heads,
                context_heads,
                logsum,
                delta_heads,
                length,
                score_scale,
            ),
            None,
        )

    grad_query, unused = lax.scan(scan_query, zero_grad, (key_blocks, value_blocks, block_starts))
    grad_key, grad_value = key_step(
        lax.all_gather(queries, "ctx", axis=0, tiled=True),
        lax.all_gather(grad_context, "ctx", axis=0, tiled=True),
        all_logsum,
        all_deltas,
        key_heads,
        value_heads,
        row_usable,
        score_scale,
    )
    grad_query = grad_query.reshape(row_count, inner_width).astype(jnp.bfloat16)
    grad_key = grad_key.reshape(row_count, inner_width).astype(jnp.bfloat16)
    grad_value = grad_value.reshape(row_count, inner_width).astype(jnp.bfloat16)
    grad_input = (
        back_project(grad_query, full_query)
        + back_project(grad_key, full_key)
        + back_project(grad_value, full_value)
    )
    grad_frames = grad_input.astype(jnp.bfloat16)
    summed_grad = lax.psum(
        lax.dot_general(
            context, masked_grad, (((0,), (0,)), ((), ())), preferred_element_type=jnp.float32
        ),
        ("rep", "ctx"),
    )
    grad_out = lax.psum_scatter(summed_grad, "dp", scatter_dimension=0, tiled=True)
    return (attended[None], grad_frames[None], grad_out)


MESH = pl.DeviceIdType.MESH


def dot(left, right, left_dim, right_dim):
    return lax.dot_general(
        left, right, (((left_dim,), (right_dim,)), ((), ())), preferred_element_type=jnp.float32
    )


def fused_kernel(
    frames_ref,
    length_ref,
    cot_ref,
    wq_ref,
    wk_ref,
    wv_ref,
    wo_ref,
    attended_ref,
    grad_frames_ref,
    grad_out_ref,
    xs,
    upstream,
    mine,
    cs,
    wq,
    wk,
    wv,
    wo,
    qs,
    ks,
    vs,
    gs,
    ctx,
    logsum,
    exps,
    inverse,
    from_queries,
    key_sum,
    value_sum,
    dq,
    dk,
    dv,
    part,
    part_in,
    sums,
    sums_in,
    slices,
    send_sem,
    recv_sem,
    local_sem,
):
    rep, dp, z = lax.axis_index("rep"), lax.axis_index("dp"), lax.axis_index("ctx")
    count = 4
    heads = 4
    rows = frames_ref.shape[1]
    full = rows * count
    scale = HEAD ** (-0.5)
    base2 = scale * math.log2(math.e)
    sibling = dp + 1 - 2 * lax.rem(dp, 2)
    across = lax.rem(dp + 2, 4)
    across_sibling = lax.rem(sibling + 2, 4)
    other_rep = 1 - rep
    group = rep * 4 + dp
    lower = z < 2
    middle = (z == 1) | (z == 2)
    side_at = jnp.clip(z - 1, 0, 1)

    local = [
        pltpu.make_async_copy(source, target, local_sem.at[at])
        for at, (source, target) in enumerate(
            (
                (cot_ref.at[0], upstream),
                (frames_ref.at[0], xs.at[z]),
                (wk_ref, wk.at[dp]),
                (wv_ref, wv.at[dp]),
                (wq_ref, wq.at[dp]),
                (wo_ref, wo.at[dp]),
            )
        )
    ]
    for copy in local:
        copy.start()

    barrier = pltpu.get_barrier_semaphore()
    for step in range(1, count):
        for to_rep in (rep, other_rep):
            pl.semaphore_signal(
                barrier,
                inc=1,
                device_id=(to_rep, dp, lax.rem(z + step, count)),
                device_id_type=MESH,
            )
    for step in range(1, 8):
        peer = lax.rem(group + step, 8)
        pl.semaphore_signal(
            barrier, inc=1, device_id=(peer // 4, lax.rem(peer, 4), z), device_id_type=MESH
        )
    pl.semaphore_wait(barrier, 13)

    def remote(source, target, sent, received, device):
        return pltpu.make_async_remote_copy(
            src_ref=source,
            dst_ref=target,
            send_sem=send_sem.at[sent],
            recv_sem=recv_sem.at[received],
            device_id=device,
            device_id_type=MESH,
        )

    def arrive(target, received):
        remote(target, target, received, received, (rep, dp, z)).wait_recv()

    def piece_of(which, slot, at):
        if which == 0:
            return xs.at[slot, pl.ds(at * (rows // 2), rows // 2)]
        return gs.at[slot, pl.ds(at * 2, 2)]

    def chain(which, side, hop, at):
        sign = 1 - 2 * side
        owner = z - sign * (hop - 1)
        slot = jnp.clip(owner, 0, count - 1)
        source = piece_of(which, slot, at)
        if which == 0 and hop == 1:
            source = frames_ref.at[0, pl.ds(at * (rows // 2), rows // 2)]
        target = jnp.clip(z + sign, 0, count - 1)
        index = which * 12 + side * 6 + (hop - 1) * 2 + at
        valid = (z + sign >= 0) & (z + sign < count) & (owner >= 0) & (owner < count)
        copy = remote(source, piece_of(which, slot, at), index, index, (rep, dp, target))
        return valid, copy

    def chain_send(which, hop, at):
        for side in range(2):
            valid, copy = chain(which, side, hop, at)

            @pl.when(valid)
            def _():
                copy.start()

    def chain_recv(which, hop, at):
        for side in range(2):
            owner = z - (1 - 2 * side) * hop
            slot = jnp.clip(owner, 0, count - 1)
            index = which * 12 + side * 6 + (hop - 1) * 2 + at

            @pl.when((owner >= 0) & (owner < count))
            def _():
                arrive(piece_of(which, slot, at), index)

    def gradient_pass(inward):
        for at in range(2):
            for side in range(2):

                @pl.when(middle & (lower == ((side == 0) == inward)))
                def _():
                    owner = z - (1 - 2 * side)
                    arrive(piece_of(1, owner, at), 12 + side * 6 + at)
                    chain(1, side, 2, at)[1].start()

    def chain_pass(which, hop, at):
        chain_recv(which, hop, at)
        if hop < 3:
            chain_send(which, hop + 1, at)

    weights = ((wo_ref, wo), (wk_ref, wk), (wq_ref, wq), (wv_ref, wv))

    def half(ref, which):
        size = ref.shape[0] // 2
        return ref.at[pl.ds(pl.multiple_of(which * size, size), size)]

    def chunk(ref, which, at):
        size = ref.shape[0] // 4
        return ref.at[pl.ds(pl.multiple_of((which * 2 + at) * size, size), size)]

    def weight_copy(piece, step):
        shard, pool = weights[piece]
        index = 24 + piece * 7 + step
        if step == 0:
            return remote(shard, pool.at[dp], index, index, (rep, sibling, z))
        if step < 3:
            target = chunk(pool.at[dp], rep, step - 1)
            return remote(chunk(shard, rep, step - 1), target, index, index, (rep, across, z))
        mine_at = pool.at[across]
        if step < 5:
            source = chunk(mine_at, rep, step - 3)
            return remote(source, source, index, index, (other_rep, dp, z))
        source = half(mine_at, rep if step == 5 else other_rep)
        return remote(source, source, index, index, (rep, sibling, z))

    def weight_recv(piece, step):
        pool = weights[piece][1]
        if step == 0:
            target = pool.at[sibling]
        elif step < 3:
            target = chunk(pool.at[across], rep, step - 1)
        elif step < 5:
            target = chunk(pool.at[across], other_rep, step - 3)
        else:
            target = half(pool.at[across_sibling], rep if step == 5 else other_rep)
        arrive(target, 24 + piece * 7 + step)

    def from_y(at):
        weight_recv(at // 2, 1 + at % 2)
        weight_copy(at // 2, 3 + at % 2).start()
        if at % 2 == 1:
            weight_copy(at // 2, 5).start()

    def from_x(at):
        weight_recv(at // 2, 3 + at % 2)
        if at % 2 == 1:
            weight_copy(at // 2, 6).start()

    def cot_copy(near):
        to = jnp.where(lower, 1, 2) if near else jnp.where(lower, 2, 1)
        sent = 52 + (0 if near else 1)
        return remote(mine.at[to - 1], cs.at[z], sent, 52 + z, (rep, dp, to))

    for at in range(2):
        chain_send(0, 1, at)
    for piece in range(4):
        for step in (1, 2):
            weight_copy(piece, step).start()
    for piece in range(4):
        weight_copy(piece, 0).start()
    for copy in local:
        copy.wait()

    length = length_ref[0]
    width = mine.shape[2]
    real = z * rows + lax.broadcasted_iota(jnp.int32, (rows, width), 0) < length
    for at in range(2):
        kept = upstream[:, at * width : (at + 1) * width].astype(jnp.float32)
        mine[at] = jnp.where(real, kept, 0.0).astype(jnp.bfloat16)
    cs[z] = mine[side_at]

    def whole(piece):
        for step in (0, 5, 6):
            weight_recv(piece, step)

    def project(pool, kept, first, blocks):
        inputs = xs[pl.ds(first, blocks)].reshape(blocks * rows, 1024)
        start = pl.multiple_of(first * rows, rows)
        matrix = dot(inputs, pool[...].reshape(1024, 512), 1, 0).astype(jnp.bfloat16)
        for head in range(heads):
            kept[head, pl.ds(start, blocks * rows), :] = matrix[:, head * HEAD : (head + 1) * HEAD]

    three = jnp.where(lower, 0, 1)
    last = jnp.where(lower, 3, 0)

    @pl.when(jnp.logical_not(middle))
    def _():
        cot_copy(True).start()
        cot_copy(False).start()

    from_y(0)
    chain_pass(0, 1, 0)
    from_y(1)
    from_y(2)
    chain_pass(0, 1, 1)
    from_x(0)
    from_y(3)

    @pl.when(middle)
    def _():
        cot_copy(False).start()

    from_x(1)
    from_y(4)
    from_x(2)
    from_y(5)
    from_x(3)
    from_y(6)
    chain_pass(0, 2, 0)
    from_x(4)
    from_y(7)
    whole(0)
    masked = jnp.concatenate([mine[0], mine[1]], axis=1)
    matrix = dot(masked, wo[...].reshape(512, 1024), 1, 1).astype(jnp.bfloat16)
    for head in range(heads):
        gs[z, head] = matrix[:, head * HEAD : (head + 1) * HEAD]
    for at in range(2):
        chain_send(1, 1, at)
    from_x(5)
    chain_pass(0, 2, 1)
    whole(1)
    from_x(6)
    project(wk, ks, three, 3)
    whole(2)
    project(wq, qs, three, 3)

    def project_last():
        project(wk, ks, last, 1)
        project(wq, qs, last, 1)

    def key_mask(amount):
        return lax.broadcasted_iota(jnp.int32, (amount, full), 1) < length

    def exponents(head, carry):
        amount = full // 2
        usable = key_mask(amount)
        for at in range(2):
            some = pl.ds(at * amount, amount)
            scores = dot(qs[head, some, :], ks[head], 1, 1)
            scores = jnp.where(usable, scores, MASKED_SCORE)
            maxima = jnp.max(scores, axis=1, keepdims=True)
            exponent = jnp.exp2((scores - maxima) * base2)
            totals = jnp.sum(exponent, axis=1, keepdims=True)
            exps[head, some, :] = exponent.astype(jnp.bfloat16)
            inverse[head, some, :] = 1.0 / totals
            logsum[head, some, :] = maxima * base2 + jnp.log2(totals)
        return carry

    @pl.when(middle)
    def _():
        project_last()
        lax.fori_loop(0, 2, exponents, 0)
        from_x(7)
        gradient_pass(True)
        lax.fori_loop(2, 4, exponents, 0)

    @pl.when(jnp.logical_not(middle))
    def _():
        from_x(7)
        for at in range(2):
            chain_pass(0, 3, at)
        project_last()
        lax.fori_loop(0, 4, exponents, 0)

    whole(3)
    project(wv, vs, 0, 4)

    def sibling_copy(batch):
        sent = 56 + batch
        return remote(part.at[batch], part_in.at[batch], sent, sent, (rep, sibling, z))

    def sum_copy(which):
        to_rep, to_dp = ((rep, across), (other_rep, across), (other_rep, dp))[which]
        source = sums.at[which // 2, to_rep]
        sent = 58 + which
        return remote(source, sums_in.at[which], sent, sent, (to_rep, to_dp, z))

    def attend(head):
        mixed = dot(exps[head], vs[head], 1, 0)
        ctx[head] = (mixed * inverse[head]).astype(jnp.bfloat16)

    def pair_product(first):
        far = lax.rem(first + 2, 4)
        pair = jnp.concatenate([ctx[far], ctx[first]], axis=1)
        return dot(pair, cs[...].reshape(full, width), 0, 0)

    attend(lax.rem(sibling + 2, 4))
    attend(sibling)

    @pl.when(middle)
    def _():
        for source in range(count):

            @pl.when(z != source)
            def _():
                arrive(cs.at[source], 52 + source)

        product = pair_product(sibling)
        for batch in range(2):
            part[batch] = product[batch * 128 : (batch + 1) * 128].astype(jnp.bfloat16)
            sibling_copy(batch).start()

    gradient_pass(False)
    attend(lax.rem(dp + 2, 4))
    attend(dp)

    @pl.when(middle)
    def _():
        product = pair_product(dp)
        for batch in range(2):
            arrive(part_in.at[batch], 56 + batch)
            kept = product[batch * 128 : (batch + 1) * 128]
            kept = kept + part_in[batch].astype(jnp.float32)
            for at in range(2):
                sums[batch, at] = kept[:, at * 256 : (at + 1) * 256].astype(jnp.bfloat16)
            if batch == 0:
                sum_copy(0).start()
                sum_copy(1).start()
            else:
                sum_copy(2).start()


    @pl.when(jnp.logical_not(middle))
    def _():
        for at in range(2):
            chain_recv(1, 1, at)

    for at in range(2):
        chain_pass(1, 2, at)
    own = pl.ds(pl.multiple_of(z * rows, rows), rows)
    own_context = jnp.concatenate([ctx[head, own, :] for head in range(heads)], axis=1)
    attended = dot(own_context, wo[...].reshape(512, 1024), 1, 0)
    row_at = z * rows + lax.broadcasted_iota(jnp.int32, attended.shape, 0)
    attended_ref[0] = jnp.where(row_at < length, attended, 0.0).astype(jnp.bfloat16)
    def row_deltas(grads, context):
        terms = grads.astype(jnp.float32) * context.astype(jnp.float32)
        return jnp.sum(terms, axis=1, keepdims=True)

    def own_queries(head, carry):
        grads = gs[z, head]
        scores = dot(qs[head, own, :], ks[head], 1, 1) * base2
        attention = jnp.where(key_mask(rows), jnp.exp2(scores - logsum[head, own, :]), 0.0)
        grad_prob = dot(grads, vs[head], 1, 1)
        minus = row_deltas(grads, ctx[head, own, :])
        grad_score = (attention * (grad_prob - minus)).astype(jnp.bfloat16)
        dq[head] = (dot(grad_score, ks[head], 1, 0) * scale).astype(jnp.bfloat16)
        return carry

    def own_keys(first, blocks, head):
        some = pl.ds(pl.multiple_of(first * rows, rows), blocks * rows)
        queries = qs[head, some, :]
        grads = gs[pl.ds(first, blocks), head].reshape(blocks * rows, HEAD)
        scores = dot(queries, ks[head, own, :], 1, 1) * base2
        at = z * rows + lax.broadcasted_iota(jnp.int32, scores.shape, 1)
        attention = jnp.where(at < length, jnp.exp2(scores - logsum[head, some, :]), 0.0)
        values = dot(attention.astype(jnp.bfloat16), grads, 0, 0)
        grad_prob = dot(grads, vs[head, own, :], 1, 1)
        minus = row_deltas(grads, ctx[head, some, :])
        grad_score = (attention * (grad_prob - minus)).astype(jnp.bfloat16)
        return dot(grad_score, queries, 0, 0), values

    lax.fori_loop(0, heads, own_queries, 0)

    mine_slice = side_at * 2 + rep

    def slice_copy(step, turned):
        to_rep = other_rep if turned else rep
        block = slices.at[mine_slice]
        return remote(
            block,
            block,
            64 + step * 2 + turned,
            64 + mine_slice,
            (to_rep, dp, lax.rem(z + step, count)),
        )

    @pl.when(middle)
    def _():
        total = sums[1, rep].astype(jnp.float32)
        for which in range(3):
            arrive(sums_in.at[which], 58 + which)
            total = total + sums_in[which].astype(jnp.float32)
        slices[mine_slice] = total.astype(jnp.bfloat16)
        low, high, mate = lax.rem(count - z, count), 3 - z, jnp.where(lower, 1, 3)
        for step in (low, mate, high):
            for turned in (1, 0):
                slice_copy(step, turned).start()
        slice_copy(0, 1).start()

    def three_keys(head, carry):
        key_sum[head], value_sum[head] = own_keys(three, 3, head)
        return carry

    lax.fori_loop(0, heads, three_keys, 0)
    by_query = jnp.concatenate([dq[head] for head in range(heads)], axis=1)
    for shard in range(4):
        from_queries[:, shard * 256 : (shard + 1) * 256] = dot(by_query, wq[shard], 1, 1)

    for at in range(2):
        chain_pass(1, 3, at)

    def last_keys(head, carry):
        keys, values = own_keys(last, 1, head)
        dk[head] = ((key_sum[head] + keys) * scale).astype(jnp.bfloat16)
        dv[head] = (value_sum[head] + values).astype(jnp.bfloat16)
        return carry

    lax.fori_loop(0, heads, last_keys, 0)

    by_key, by_value = (
        jnp.concatenate([kept[head] for head in range(heads)], axis=1) for kept in (dk, dv)
    )
    for shard in range(4):
        columns = slice(shard * 256, (shard + 1) * 256)
        added = dot(by_key, wk[shard], 1, 1) + dot(by_value, wv[shard], 1, 1)
        added = added + from_queries[:, columns]
        grad_frames_ref[0, :, columns] = added.astype(jnp.bfloat16)

    for piece in range(4):
        for step in range(7):
            weight_copy(piece, step).wait_send()
    for which in range(2):
        for hop in range(1, count):
            for at in range(2):
                for side in range(2):
                    valid, copy = chain(which, side, hop, at)

                    @pl.when(valid)
                    def _():
                        copy.wait_send()

    @pl.when(jnp.logical_not(middle))
    def _():
        cot_copy(True).wait_send()

    cot_copy(False).wait_send()

    @pl.when(middle)
    def _():
        for batch in range(2):
            sibling_copy(batch).wait_send()
        for which in range(3):
            sum_copy(which).wait_send()

    for at in range(count):

        @pl.when(jnp.logical_not(middle & (mine_slice == at)))
        def _():
            arrive(slices.at[at], 64 + at)

    @pl.when(middle)
    def _():
        for step in range(count):
            for turned in range(2):
                if step + turned > 0:
                    slice_copy(step, turned).wait_send()

    for at in range(count):
        grad_out_ref[:, at * 256 : (at + 1) * 256] = slices[at].astype(jnp.float32)


def write_kernel(*refs):
    sems = refs[6]
    copies = [pltpu.make_async_copy(refs[at], refs[at + 3], sems.at[at]) for at in range(3)]
    for copy in copies:
        copy.start()
    for copy in copies:
        copy.wait()


def fused(frames, lengths, cotangent, w_query, w_key, w_value, w_out):
    vmem = pl.BlockSpec(memory_space=pltpu.VMEM)
    hbm = pl.BlockSpec(memory_space=pltpu.HBM)
    bf16, f32 = jnp.bfloat16, jnp.float32
    per_head = pltpu.VMEM((4, 512, HEAD), bf16)
    own_head = pltpu.VMEM((4, 128, HEAD), bf16)
    results = pl.pallas_call(
        fused_kernel,
        out_shape=(
            pltpu.VMEM(frames.shape, bf16),
            pltpu.VMEM(frames.shape, bf16),
            pltpu.VMEM(w_out.shape, f32),
        ),
        in_specs=[hbm, pl.BlockSpec(memory_space=pltpu.SMEM)] + [hbm] * 5,
        out_specs=(vmem, vmem, vmem),
        scratch_shapes=[
            pltpu.VMEM((4, 128, 1024), bf16),
            pltpu.VMEM((128, 1024), bf16),
            pltpu.VMEM((2, 128, 512), bf16),
            pltpu.VMEM((4, 128, 512), bf16),
            pltpu.VMEM((4, 256, 512), bf16),
            pltpu.VMEM((4, 256, 512), bf16),
            pltpu.VMEM((4, 256, 512), bf16),
            pltpu.VMEM((4, 128, 1024), bf16),
            per_head,
            per_head,
            per_head,
            pltpu.VMEM((4, 4, 128, HEAD), bf16),
            per_head,
            pltpu.VMEM((4, 512, 1), f32),
            pltpu.VMEM((4, 512, 512), bf16),
            pltpu.VMEM((4, 512, 1), f32),
            pltpu.VMEM((128, 1024), f32),
            pltpu.VMEM((4, 128, HEAD), f32),
            pltpu.VMEM((4, 128, HEAD), f32),
            own_head,
            own_head,
            own_head,
            pltpu.VMEM((2, 128, 512), bf16),
            pltpu.VMEM((2, 128, 512), bf16),
            pltpu.VMEM((2, 2, 128, 256), bf16),
            pltpu.VMEM((3, 128, 256), bf16),
            pltpu.VMEM((4, 128, 256), bf16),
            pltpu.SemaphoreType.DMA((72,)),
            pltpu.SemaphoreType.DMA((72,)),
            pltpu.SemaphoreType.DMA((6,)),
        ],
        compiler_params=pltpu.CompilerParams(
            collective_id=0, has_side_effects=True, vmem_limit_bytes=56 * 1024 * 1024
        ),
    )(frames, lengths, cotangent, w_query, w_key, w_value, w_out)
    return pl.pallas_call(
        write_kernel,
        out_shape=tuple(jax.ShapeDtypeStruct(r.shape, r.dtype) for r in results),
        in_specs=[vmem] * 3,
        out_specs=(hbm, hbm, hbm),
        scratch_shapes=[pltpu.SemaphoreType.DMA((3,))],
        compiler_params=pltpu.CompilerParams(vmem_limit_bytes=4 * 1024 * 1024),
    )(*results)


def either(sizes, frames, lengths, cotangent, w_query, w_key, w_value, w_out):
    fits = sizes == (2, 4, 4) and frames.shape == (1, 128, 1024) and w_query.shape == (256, 512)
    chosen = fused if fits else shards
    return chosen(frames, lengths, cotangent, w_query, w_key, w_value, w_out)


def solution(mesh):
    in_specs = (
        P(("rep", "dp"), "ctx", None),
        P(("rep", "dp")),
        P(("rep", "dp"), "ctx", None),
        P("dp", None),
        P("dp", None),
        P("dp", None),
        P("dp", None),
    )
    out_specs = (P(("rep", "dp"), "ctx", None), P(("rep", "dp"), "ctx", None), P("dp", None))
    sizes = (mesh.shape["rep"], mesh.shape["dp"], mesh.shape["ctx"])
    body = functools.partial(either, sizes)
    return jax.shard_map(body, mesh=mesh, in_specs=in_specs, out_specs=out_specs, check_vma=False)
```

```python
import functools
import math

import jax
import jax.numpy as jnp
from jax import lax
from jax.experimental import pallas as pl
from jax.experimental.pallas import tpu as pltpu
from jax.sharding import PartitionSpec as P

HEAD = 128


MASKED_SCORE = -1e30


def head_split(matrix, head_count):
    return matrix.reshape(matrix.shape[0], head_count, matrix.shape[1] // head_count)


def forward_step(carry, key_part, value_part, offset, query_heads, length, score_scale):
    head_count = query_heads.shape[1]
    amount = key_part.shape[0]
    maxima, totals, accumulated = carry
    key_heads = head_split(key_part, head_count)
    value_heads = head_split(value_part, head_count)
    scores = (
        jnp.einsum("rhe,nhe->hrn", query_heads, key_heads, preferred_element_type=jnp.float32)
        * score_scale
    )
    usable = offset + jnp.arange(amount) < length
    scores = jnp.where(usable[None, None, :], scores, MASKED_SCORE)
    new_maxima = jnp.maximum(maxima, jnp.max(scores, axis=2))
    factor = jnp.exp(maxima - new_maxima)
    exponent = jnp.where(usable[None, None, :], jnp.exp(scores - new_maxima[:, :, None]), 0.0)
    totals = totals * factor + jnp.sum(exponent, axis=2)
    mixed = jnp.einsum(
        "hrn,nhe->hre",
        exponent.astype(jnp.bfloat16),
        value_heads,
        preferred_element_type=jnp.float32,
    )
    accumulated = accumulated * factor[:, :, None] + mixed
    return (new_maxima, totals, accumulated)


def query_step(
    grad_accum,
    key_part,
    value_part,
    offset,
    query_heads,
    context_heads,
    logsum,
    deltas,
    length,
    score_scale,
):
    head_count = query_heads.shape[1]
    amount = key_part.shape[0]
    key_heads = head_split(key_part, head_count)
    value_heads = head_split(value_part, head_count)
    scores = (
        jnp.einsum("rhe,nhe->hrn", query_heads, key_heads, preferred_element_type=jnp.float32)
        * score_scale
    )
    usable = offset + jnp.arange(amount) < length
    attention = jnp.where(usable[None, None, :], jnp.exp(scores - logsum[:, :, None]), 0.0)
    grad_prob = jnp.einsum(
        "rhe,nhe->hrn", context_heads, value_heads, preferred_element_type=jnp.float32
    )
    grad_score = (attention * (grad_prob - deltas[:, :, None])).astype(jnp.bfloat16)
    added = jnp.einsum("hrn,nhe->rhe", grad_score, key_heads, preferred_element_type=jnp.float32)
    return grad_accum + added * score_scale


def key_step(
    query_part,
    context_part,
    all_logsum,
    all_deltas,
    key_heads,
    value_heads,
    key_usable,
    score_scale,
):
    head_count = key_heads.shape[1]
    query_heads = head_split(query_part, head_count)
    context_heads = head_split(context_part, head_count)
    scores = (
        jnp.einsum("rhe,nhe->hrn", query_heads, key_heads, preferred_element_type=jnp.float32)
        * score_scale
    )
    attention = jnp.where(key_usable[None, None, :], jnp.exp(scores - all_logsum[:, :, None]), 0.0)
    grad_value = jnp.einsum(
        "hrn,rhe->nhe",
        attention.astype(jnp.bfloat16),
        context_heads,
        preferred_element_type=jnp.float32,
    )
    grad_prob = jnp.einsum(
        "rhe,nhe->hrn", context_heads, value_heads, preferred_element_type=jnp.float32
    )
    grad_score = (attention * (grad_prob - all_deltas[:, :, None])).astype(jnp.bfloat16)
    added = jnp.einsum("hrn,rhe->nhe", grad_score, query_heads, preferred_element_type=jnp.float32)
    return (added * score_scale, grad_value)


def back_project(gradient, weight):
    return lax.dot_general(
        gradient, weight, (((1,), (1,)), ((), ())), preferred_element_type=jnp.float32
    )


def shards(frames, lengths, cotangent, w_query, w_key, w_value, w_out):
    full_query, full_key, full_value, full_out = (
        lax.all_gather(w_query, "dp", axis=0, tiled=True),
        lax.all_gather(w_key, "dp", axis=0, tiled=True),
        lax.all_gather(w_value, "dp", axis=0, tiled=True),
        lax.all_gather(w_out, "dp", axis=0, tiled=True),
    )
    inputs = frames[0]
    upstream = cotangent[0]
    length = lengths[0]
    row_count = inputs.shape[0]
    inner_width = full_query.shape[1]
    head_count = inner_width // HEAD
    score_scale = HEAD ** (-0.5)
    first_frame = lax.axis_index("ctx") * row_count
    row_usable = first_frame + jnp.arange(row_count) < length
    queries = jnp.dot(inputs, full_query, preferred_element_type=jnp.float32).astype(jnp.bfloat16)
    keys = jnp.dot(inputs, full_key, preferred_element_type=jnp.float32).astype(jnp.bfloat16)
    values = jnp.dot(inputs, full_value, preferred_element_type=jnp.float32).astype(jnp.bfloat16)
    query_heads = head_split(queries, head_count)
    key_heads = head_split(keys, head_count)
    value_heads = head_split(values, head_count)
    start_state = (
        jnp.full((head_count, row_count), MASKED_SCORE, jnp.float32),
        jnp.zeros((head_count, row_count), jnp.float32),
        jnp.zeros((head_count, row_count, HEAD), jnp.float32),
    )
    all_keys, all_values = (
        lax.all_gather(keys, "ctx", axis=0, tiled=True),
        lax.all_gather(values, "ctx", axis=0, tiled=True),
    )
    key_block = row_count * math.gcd(max(1, 512 // row_count), lax.axis_size("ctx"))
    block_count = all_keys.shape[0] // key_block
    key_blocks = all_keys.reshape(block_count, key_block, inner_width)
    value_blocks = all_values.reshape(block_count, key_block, inner_width)
    block_starts = jnp.arange(block_count, dtype=jnp.int32) * key_block

    def scan_forward(current, scan_item):
        return (
            forward_step(
                current, scan_item[0], scan_item[1], scan_item[2], query_heads, length, score_scale
            ),
            None,
        )

    softmax_state, unused = lax.scan(
        scan_forward, start_state, (key_blocks, value_blocks, block_starts)
    )
    maxima, totals, accumulated = softmax_state
    context = (
        (accumulated / totals[:, :, None])
        .transpose(1, 0, 2)
        .reshape(row_count, inner_width)
        .astype(jnp.bfloat16)
    )
    logsum = maxima + jnp.log(totals)
    attended = jnp.dot(context, full_out, preferred_element_type=jnp.float32)
    attended = jnp.where(row_usable[:, None], attended, 0.0).astype(jnp.bfloat16)
    masked_grad = jnp.where(row_usable[:, None], upstream, jnp.zeros_like(upstream))
    grad_context = back_project(masked_grad, full_out).astype(jnp.bfloat16)
    deltas = jnp.sum(
        (grad_context.astype(jnp.float32) * context.astype(jnp.float32)).reshape(
            row_count, head_count, HEAD
        ),
        axis=2,
    )
    context_heads = head_split(grad_context, head_count)
    delta_heads = deltas.T
    all_logsum, all_deltas = (
        lax.all_gather(logsum, "ctx", axis=1, tiled=True),
        lax.all_gather(delta_heads, "ctx", axis=1, tiled=True),
    )
    zero_grad = jnp.zeros((row_count, head_count, HEAD), jnp.float32)

    def scan_query(current, scan_item):
        return (
            query_step(
                current,
                scan_item[0],
                scan_item[1],
                scan_item[2],
                query_heads,
                context_heads,
                logsum,
                delta_heads,
                length,
                score_scale,
            ),
            None,
        )

    grad_query, unused = lax.scan(scan_query, zero_grad, (key_blocks, value_blocks, block_starts))
    grad_key, grad_value = key_step(
        lax.all_gather(queries, "ctx", axis=0, tiled=True),
        lax.all_gather(grad_context, "ctx", axis=0, tiled=True),
        all_logsum,
        all_deltas,
        key_heads,
        value_heads,
        row_usable,
        score_scale,
    )
    grad_query = grad_query.reshape(row_count, inner_width).astype(jnp.bfloat16)
    grad_key = grad_key.reshape(row_count, inner_width).astype(jnp.bfloat16)
    grad_value = grad_value.reshape(row_count, inner_width).astype(jnp.bfloat16)
    grad_input = (
        back_project(grad_query, full_query)
        + back_project(grad_key, full_key)
        + back_project(grad_value, full_value)
    )
    grad_frames = grad_input.astype(jnp.bfloat16)
    summed_grad = lax.psum(
        lax.dot_general(
            context, masked_grad, (((0,), (0,)), ((), ())), preferred_element_type=jnp.float32
        ),
        ("rep", "ctx"),
    )
    grad_out = lax.psum_scatter(summed_grad, "dp", scatter_dimension=0, tiled=True)
    return (attended[None], grad_frames[None], grad_out)


MESH = pl.DeviceIdType.MESH


def dot(left, right, left_dim, right_dim):
    return lax.dot_general(
        left, right, (((left_dim,), (right_dim,)), ((), ())), preferred_element_type=jnp.float32
    )


def fused_kernel(
    frames_ref,
    length_ref,
    cot_ref,
    wq_ref,
    wk_ref,
    wv_ref,
    wo_ref,
    attended_ref,
    grad_frames_ref,
    grad_out_ref,
    xs,
    upstream,
    mine,
    cs,
    wq,
    wk,
    wv,
    wo,
    qs,
    ks,
    vs,
    gs,
    ctx,
    logsum,
    exps,
    inverse,
    from_queries,
    key_sum,
    value_sum,
    dq,
    dk,
    dv,
    part,
    part_in,
    sums,
    sums_in,
    slices,
    send_sem,
    recv_sem,
    local_sem,
):
    rep, dp, z = lax.axis_index("rep"), lax.axis_index("dp"), lax.axis_index("ctx")
    count = 4
    heads = 4
    rows = frames_ref.shape[1]
    full = rows * count
    scale = HEAD ** (-0.5)
    base2 = scale * math.log2(math.e)
    sibling = dp + 1 - 2 * lax.rem(dp, 2)
    across = lax.rem(dp + 2, 4)
    across_sibling = lax.rem(sibling + 2, 4)
    other_rep = 1 - rep
    group = rep * 4 + dp
    lower = z < 2
    middle = (z == 1) | (z == 2)
    side_at = jnp.clip(z - 1, 0, 1)

    local = [
        pltpu.make_async_copy(source, target, local_sem.at[at])
        for at, (source, target) in enumerate(
            (
                (cot_ref.at[0], upstream),
                (frames_ref.at[0], xs.at[z]),
                (wk_ref, wk.at[dp]),
                (wv_ref, wv.at[dp]),
                (wq_ref, wq.at[dp]),
                (wo_ref, wo.at[dp]),
            )
        )
    ]
    for copy in local:
        copy.start()

    barrier = pltpu.get_barrier_semaphore()
    for step in range(1, count):
        for to_rep in (rep, other_rep):
            pl.semaphore_signal(
                barrier,
                inc=1,
                device_id=(to_rep, dp, lax.rem(z + step, count)),
                device_id_type=MESH,
            )
    for step in range(1, 8):
        peer = lax.rem(group + step, 8)
        pl.semaphore_signal(
            barrier, inc=1, device_id=(peer // 4, lax.rem(peer, 4), z), device_id_type=MESH
        )
    pl.semaphore_wait(barrier, 13)

    def remote(source, target, sent, received, device):
        return pltpu.make_async_remote_copy(
            src_ref=source,
            dst_ref=target,
            send_sem=send_sem.at[sent],
            recv_sem=recv_sem.at[received],
            device_id=device,
            device_id_type=MESH,
        )

    def arrive(target, received):
        remote(target, target, received, received, (rep, dp, z)).wait_recv()

    def piece_of(which, slot, at):
        if which == 0:
            return xs.at[slot, pl.ds(at * (rows // 2), rows // 2)]
        return gs.at[slot, pl.ds(at * 2, 2)]

    def chain(which, side, hop, at):
        sign = 1 - 2 * side
        owner = z - sign * (hop - 1)
        slot = jnp.clip(owner, 0, count - 1)
        source = piece_of(which, slot, at)
        if which == 0 and hop == 1:
            source = frames_ref.at[0, pl.ds(at * (rows // 2), rows // 2)]
        target = jnp.clip(z + sign, 0, count - 1)
        index = which * 12 + side * 6 + (hop - 1) * 2 + at
        valid = (z + sign >= 0) & (z + sign < count) & (owner >= 0) & (owner < count)
        copy = remote(source, piece_of(which, slot, at), index, index, (rep, dp, target))
        return valid, copy

    def chain_send(which, hop, at):
        for side in range(2):
            valid, copy = chain(which, side, hop, at)

            @pl.when(valid)
            def _():
                copy.start()

    def chain_recv(which, hop, at):
        for side in range(2):
            owner = z - (1 - 2 * side) * hop
            slot = jnp.clip(owner, 0, count - 1)
            index = which * 12 + side * 6 + (hop - 1) * 2 + at

            @pl.when((owner >= 0) & (owner < count))
            def _():
                arrive(piece_of(which, slot, at), index)

    def gradient_pass(inward):
        for at in range(2):
            for side in range(2):

                @pl.when(middle & (lower == ((side == 0) == inward)))
                def _():
                    owner = z - (1 - 2 * side)
                    arrive(piece_of(1, owner, at), 12 + side * 6 + at)
                    chain(1, side, 2, at)[1].start()

    def chain_pass(which, hop, at):
        chain_recv(which, hop, at)
        if hop < 3:
            chain_send(which, hop + 1, at)

    weights = ((wo_ref, wo), (wk_ref, wk), (wq_ref, wq), (wv_ref, wv))

    def half(ref, which):
        size = ref.shape[0] // 2
        return ref.at[pl.ds(pl.multiple_of(which * size, size), size)]

    def chunk(ref, which, at):
        size = ref.shape[0] // 4
        return ref.at[pl.ds(pl.multiple_of((which * 2 + at) * size, size), size)]

    def weight_copy(piece, step):
        shard, pool = weights[piece]
        index = 24 + piece * 7 + step
        if step == 0:
            return remote(shard, pool.at[dp], index, index, (rep, sibling, z))
        if step < 3:
            target = chunk(pool.at[dp], rep, step - 1)
            return remote(chunk(shard, rep, step - 1), target, index, index, (rep, across, z))
        mine_at = pool.at[across]
        if step < 5:
            source = chunk(mine_at, rep, step - 3)
            return remote(source, source, index, index, (other_rep, dp, z))
        source = half(mine_at, rep if step == 5 else other_rep)
        return remote(source, source, index, index, (rep, sibling, z))

    def weight_recv(piece, step):
        pool = weights[piece][1]
        if step == 0:
            target = pool.at[sibling]
        elif step < 3:
            target = chunk(pool.at[across], rep, step - 1)
        elif step < 5:
            target = chunk(pool.at[across], other_rep, step - 3)
        else:
            target = half(pool.at[across_sibling], rep if step == 5 else other_rep)
        arrive(target, 24 + piece * 7 + step)

    def from_y(at):
        weight_recv(at // 2, 1 + at % 2)
        weight_copy(at // 2, 3 + at % 2).start()
        if at % 2 == 1:
            weight_copy(at // 2, 5).start()

    def from_x(at):
        weight_recv(at // 2, 3 + at % 2)
        if at % 2 == 1:
            weight_copy(at // 2, 6).start()

    def cot_copy(near):
        to = jnp.where(lower, 1, 2) if near else jnp.where(lower, 2, 1)
        sent = 52 + (0 if near else 1)
        return remote(mine.at[to - 1], cs.at[z], sent, 52 + z, (rep, dp, to))

    for at in range(2):
        chain_send(0, 1, at)
    for piece in range(4):
        for step in (1, 2):
            weight_copy(piece, step).start()
    for piece in range(4):
        weight_copy(piece, 0).start()
    for copy in local:
        copy.wait()

    length = length_ref[0]
    width = mine.shape[2]
    real = z * rows + lax.broadcasted_iota(jnp.int32, (rows, width), 0) < length
    for at in range(2):
        kept = upstream[:, at * width : (at + 1) * width].astype(jnp.float32)
        mine[at] = jnp.where(real, kept, 0.0).astype(jnp.bfloat16)
    cs[z] = mine[side_at]

    def whole(piece):
        for step in (0, 5, 6):
            weight_recv(piece, step)

    def project(pool, kept, first, blocks):
        inputs = xs[pl.ds(first, blocks)].reshape(blocks * rows, 1024)
        start = pl.multiple_of(first * rows, rows)
        matrix = dot(inputs, pool[...].reshape(1024, 512), 1, 0).astype(jnp.bfloat16)
        for head in range(heads):
            kept[head, pl.ds(start, blocks * rows), :] = matrix[:, head * HEAD : (head + 1) * HEAD]

    three = jnp.where(lower, 0, 1)
    last = jnp.where(lower, 3, 0)

    @pl.when(jnp.logical_not(middle))
    def _():
        cot_copy(True).start()
        cot_copy(False).start()

    from_y(0)
    chain_pass(0, 1, 0)
    from_y(1)
    from_y(2)
    chain_pass(0, 1, 1)
    from_x(0)
    from_y(3)

    @pl.when(middle)
    def _():
        cot_copy(False).start()

    from_x(1)
    from_y(4)
    from_x(2)
    from_y(5)
    from_x(3)
    from_y(6)
    chain_pass(0, 2, 0)
    from_x(4)
    from_y(7)
    whole(0)
    masked = jnp.concatenate([mine[0], mine[1]], axis=1)
    matrix = dot(masked, wo[...].reshape(512, 1024), 1, 1).astype(jnp.bfloat16)
    for head in range(heads):
        gs[z, head] = matrix[:, head * HEAD : (head + 1) * HEAD]
    for at in range(2):
        chain_send(1, 1, at)
    from_x(5)
    chain_pass(0, 2, 1)
    whole(1)
    from_x(6)
    project(wk, ks, three, 3)
    whole(2)
    project(wq, qs, three, 3)

    def project_last():
        project(wk, ks, last, 1)
        project(wq, qs, last, 1)

    def key_mask(amount):
        return lax.broadcasted_iota(jnp.int32, (amount, full), 1) < length

    def exponents(head, carry):
        amount = full // 2
        usable = key_mask(amount)
        for at in range(2):
            some = pl.ds(at * amount, amount)
            scores = dot(qs[head, some, :], ks[head], 1, 1)
            scores = jnp.where(usable, scores, MASKED_SCORE)
            maxima = jnp.max(scores, axis=1, keepdims=True)
            exponent = jnp.exp2((scores - maxima) * base2)
            totals = jnp.sum(exponent, axis=1, keepdims=True)
            exps[head, some, :] = exponent.astype(jnp.bfloat16)
            inverse[head, some, :] = 1.0 / totals
            logsum[head, some, :] = maxima * base2 + jnp.log2(totals)
        return carry

    @pl.when(middle)
    def _():
        project_last()
        for head in range(4):
            exponents(head, 0)
            if head == 1:
                from_x(7)
                gradient_pass(True)

    @pl.when(jnp.logical_not(middle))
    def _():
        from_x(7)
        for at in range(2):
            chain_pass(0, 3, at)
        project_last()
        for head in range(4):
            exponents(head, 0)

    whole(3)
    project(wv, vs, 0, 4)

    def sibling_copy(batch):
        sent = 56 + batch
        return remote(part.at[batch], part_in.at[batch], sent, sent, (rep, sibling, z))

    def sum_copy(which):
        to_rep, to_dp = ((rep, across), (other_rep, across), (other_rep, dp))[which]
        source = sums.at[which // 2, to_rep]
        sent = 58 + which
        return remote(source, sums_in.at[which], sent, sent, (to_rep, to_dp, z))

    def attend(head):
        mixed = dot(exps[head], vs[head], 1, 0)
        ctx[head] = (mixed * inverse[head]).astype(jnp.bfloat16)

    def pair_product(first):
        far = lax.rem(first + 2, 4)
        pair = jnp.concatenate([ctx[far], ctx[first]], axis=1)
        return dot(pair, cs[...].reshape(full, width), 0, 0)

    attend(lax.rem(sibling + 2, 4))
    attend(sibling)

    @pl.when(middle)
    def _():
        for source in range(count):

            @pl.when(z != source)
            def _():
                arrive(cs.at[source], 52 + source)

        product = pair_product(sibling)
        for batch in range(2):
            part[batch] = product[batch * 128 : (batch + 1) * 128].astype(jnp.bfloat16)
            sibling_copy(batch).start()

    gradient_pass(False)
    attend(lax.rem(dp + 2, 4))
    attend(dp)

    @pl.when(middle)
    def _():
        product = pair_product(dp)
        for batch in range(2):
            arrive(part_in.at[batch], 56 + batch)
            kept = product[batch * 128 : (batch + 1) * 128]
            kept = kept + part_in[batch].astype(jnp.float32)
            for at in range(2):
                sums[batch, at] = kept[:, at * 256 : (at + 1) * 256].astype(jnp.bfloat16)
            if batch == 0:
                sum_copy(0).start()
                sum_copy(1).start()
            else:
                sum_copy(2).start()


    @pl.when(jnp.logical_not(middle))
    def _():
        for at in range(2):
            chain_recv(1, 1, at)

    for at in range(2):
        chain_pass(1, 2, at)
    own = pl.ds(pl.multiple_of(z * rows, rows), rows)
    own_context = jnp.concatenate([ctx[head, own, :] for head in range(heads)], axis=1)
    attended = dot(own_context, wo[...].reshape(512, 1024), 1, 0)
    row_at = z * rows + lax.broadcasted_iota(jnp.int32, attended.shape, 0)
    attended_ref[0] = jnp.where(row_at < length, attended, 0.0).astype(jnp.bfloat16)
    def row_deltas(grads, context):
        terms = grads.astype(jnp.float32) * context.astype(jnp.float32)
        return jnp.sum(terms, axis=1, keepdims=True)

    def own_queries(head, carry):
        grads = gs[z, head]
        scores = dot(qs[head, own, :], ks[head], 1, 1) * base2
        attention = jnp.where(key_mask(rows), jnp.exp2(scores - logsum[head, own, :]), 0.0)
        grad_prob = dot(grads, vs[head], 1, 1)
        minus = row_deltas(grads, ctx[head, own, :])
        grad_score = (attention * (grad_prob - minus)).astype(jnp.bfloat16)
        dq[head] = (dot(grad_score, ks[head], 1, 0) * scale).astype(jnp.bfloat16)
        return carry

    def own_keys(first, blocks, head):
        some = pl.ds(pl.multiple_of(first * rows, rows), blocks * rows)
        queries = qs[head, some, :]
        grads = gs[pl.ds(first, blocks), head].reshape(blocks * rows, HEAD)
        scores = dot(queries, ks[head, own, :], 1, 1) * base2
        at = z * rows + lax.broadcasted_iota(jnp.int32, scores.shape, 1)
        attention = jnp.where(at < length, jnp.exp2(scores - logsum[head, some, :]), 0.0)
        values = dot(attention.astype(jnp.bfloat16), grads, 0, 0)
        grad_prob = dot(grads, vs[head, own, :], 1, 1)
        minus = row_deltas(grads, ctx[head, some, :])
        grad_score = (attention * (grad_prob - minus)).astype(jnp.bfloat16)
        return dot(grad_score, queries, 0, 0), values

    lax.fori_loop(0, heads, own_queries, 0)

    mine_slice = side_at * 2 + rep

    def slice_copy(step, turned):
        to_rep = other_rep if turned else rep
        block = slices.at[mine_slice]
        return remote(
            block,
            block,
            64 + step * 2 + turned,
            64 + mine_slice,
            (to_rep, dp, lax.rem(z + step, count)),
        )

    @pl.when(middle)
    def _():
        total = sums[1, rep].astype(jnp.float32)
        for which in range(3):
            arrive(sums_in.at[which], 58 + which)
            total = total + sums_in[which].astype(jnp.float32)
        slices[mine_slice] = total.astype(jnp.bfloat16)
        low, high, mate = lax.rem(count - z, count), 3 - z, jnp.where(lower, 1, 3)
        for step in (low, mate, high):
            for turned in (1, 0):
                slice_copy(step, turned).start()
        slice_copy(0, 1).start()

    def three_keys(head, carry):
        key_sum[head], value_sum[head] = own_keys(three, 3, head)
        return carry

    lax.fori_loop(0, heads, three_keys, 0)
    by_query = jnp.concatenate([dq[head] for head in range(heads)], axis=1)
    for shard in range(4):
        from_queries[:, shard * 256 : (shard + 1) * 256] = dot(by_query, wq[shard], 1, 1)

    for at in range(2):
        chain_pass(1, 3, at)

    def last_keys(head, carry):
        keys, values = own_keys(last, 1, head)
        dk[head] = ((key_sum[head] + keys) * scale).astype(jnp.bfloat16)
        dv[head] = (value_sum[head] + values).astype(jnp.bfloat16)
        return carry

    lax.fori_loop(0, heads, last_keys, 0)

    by_key, by_value = (
        jnp.concatenate([kept[head] for head in range(heads)], axis=1) for kept in (dk, dv)
    )
    for shard in range(4):
        columns = slice(shard * 256, (shard + 1) * 256)
        added = dot(by_key, wk[shard], 1, 1) + dot(by_value, wv[shard], 1, 1)
        added = added + from_queries[:, columns]
        grad_frames_ref[0, :, columns] = added.astype(jnp.bfloat16)

    for piece in range(4):
        for step in range(7):
            weight_copy(piece, step).wait_send()
    for which in range(2):
        for hop in range(1, count):
            for at in range(2):
                for side in range(2):
                    valid, copy = chain(which, side, hop, at)

                    @pl.when(valid)
                    def _():
                        copy.wait_send()

    @pl.when(jnp.logical_not(middle))
    def _():
        cot_copy(True).wait_send()

    cot_copy(False).wait_send()

    @pl.when(middle)
    def _():
        for batch in range(2):
            sibling_copy(batch).wait_send()
        for which in range(3):
            sum_copy(which).wait_send()

    for at in range(count):

        @pl.when(jnp.logical_not(middle & (mine_slice == at)))
        def _():
            arrive(slices.at[at], 64 + at)

    @pl.when(middle)
    def _():
        for step in range(count):
            for turned in range(2):
                if step + turned > 0:
                    slice_copy(step, turned).wait_send()

    for at in range(count):
        grad_out_ref[:, at * 256 : (at + 1) * 256] = slices[at].astype(jnp.float32)


def write_kernel(*refs):
    sems = refs[6]
    copies = [pltpu.make_async_copy(refs[at], refs[at + 3], sems.at[at]) for at in range(3)]
    for copy in copies:
        copy.start()
    for copy in copies:
        copy.wait()


def fused(frames, lengths, cotangent, w_query, w_key, w_value, w_out):
    vmem = pl.BlockSpec(memory_space=pltpu.VMEM)
    hbm = pl.BlockSpec(memory_space=pltpu.HBM)
    bf16, f32 = jnp.bfloat16, jnp.float32
    per_head = pltpu.VMEM((4, 512, HEAD), bf16)
    own_head = pltpu.VMEM((4, 128, HEAD), bf16)
    results = pl.pallas_call(
        fused_kernel,
        out_shape=(
            pltpu.VMEM(frames.shape, bf16),
            pltpu.VMEM(frames.shape, bf16),
            pltpu.VMEM(w_out.shape, f32),
        ),
        in_specs=[hbm, pl.BlockSpec(memory_space=pltpu.SMEM)] + [hbm] * 5,
        out_specs=(vmem, vmem, vmem),
        scratch_shapes=[
            pltpu.VMEM((4, 128, 1024), bf16),
            pltpu.VMEM((128, 1024), bf16),
            pltpu.VMEM((2, 128, 512), bf16),
            pltpu.VMEM((4, 128, 512), bf16),
            pltpu.VMEM((4, 256, 512), bf16),
            pltpu.VMEM((4, 256, 512), bf16),
            pltpu.VMEM((4, 256, 512), bf16),
            pltpu.VMEM((4, 128, 1024), bf16),
            per_head,
            per_head,
            per_head,
            pltpu.VMEM((4, 4, 128, HEAD), bf16),
            per_head,
            pltpu.VMEM((4, 512, 1), f32),
            pltpu.VMEM((4, 512, 512), bf16),
            pltpu.VMEM((4, 512, 1), f32),
            pltpu.VMEM((128, 1024), f32),
            pltpu.VMEM((4, 128, HEAD), f32),
            pltpu.VMEM((4, 128, HEAD), f32),
            own_head,
            own_head,
            own_head,
            pltpu.VMEM((2, 128, 512), bf16),
            pltpu.VMEM((2, 128, 512), bf16),
            pltpu.VMEM((2, 2, 128, 256), bf16),
            pltpu.VMEM((3, 128, 256), bf16),
            pltpu.VMEM((4, 128, 256), bf16),
            pltpu.SemaphoreType.DMA((72,)),
            pltpu.SemaphoreType.DMA((72,)),
            pltpu.SemaphoreType.DMA((6,)),
        ],
        compiler_params=pltpu.CompilerParams(
            collective_id=0, has_side_effects=True, vmem_limit_bytes=56 * 1024 * 1024
        ),
    )(frames, lengths, cotangent, w_query, w_key, w_value, w_out)
    return pl.pallas_call(
        write_kernel,
        out_shape=tuple(jax.ShapeDtypeStruct(r.shape, r.dtype) for r in results),
        in_specs=[vmem] * 3,
        out_specs=(hbm, hbm, hbm),
        scratch_shapes=[pltpu.SemaphoreType.DMA((3,))],
        compiler_params=pltpu.CompilerParams(vmem_limit_bytes=4 * 1024 * 1024),
    )(*results)


def either(sizes, frames, lengths, cotangent, w_query, w_key, w_value, w_out):
    fits = sizes == (2, 4, 4) and frames.shape == (1, 128, 1024) and w_query.shape == (256, 512)
    chosen = fused if fits else shards
    return chosen(frames, lengths, cotangent, w_query, w_key, w_value, w_out)


def solution(mesh):
    in_specs = (
        P(("rep", "dp"), "ctx", None),
        P(("rep", "dp")),
        P(("rep", "dp"), "ctx", None),
        P("dp", None),
        P("dp", None),
        P("dp", None),
        P("dp", None),
    )
    out_specs = (P(("rep", "dp"), "ctx", None), P(("rep", "dp"), "ctx", None), P("dp", None))
    sizes = (mesh.shape["rep"], mesh.shape["dp"], mesh.shape["ctx"])
    body = functools.partial(either, sizes)
    return jax.shard_map(body, mesh=mesh, in_specs=in_specs, out_specs=out_specs, check_vma=False)
```

```python
import functools
import math

import jax
import jax.numpy as jnp
from jax import lax
from jax.experimental import pallas as pl
from jax.experimental.pallas import tpu as pltpu
from jax.sharding import PartitionSpec as P

HEAD = 128


MASKED_SCORE = -1e30


def head_split(matrix, head_count):
    return matrix.reshape(matrix.shape[0], head_count, matrix.shape[1] // head_count)


def forward_step(carry, key_part, value_part, offset, query_heads, length, score_scale):
    head_count = query_heads.shape[1]
    amount = key_part.shape[0]
    maxima, totals, accumulated = carry
    key_heads = head_split(key_part, head_count)
    value_heads = head_split(value_part, head_count)
    scores = (
        jnp.einsum("rhe,nhe->hrn", query_heads, key_heads, preferred_element_type=jnp.float32)
        * score_scale
    )
    usable = offset + jnp.arange(amount) < length
    scores = jnp.where(usable[None, None, :], scores, MASKED_SCORE)
    new_maxima = jnp.maximum(maxima, jnp.max(scores, axis=2))
    factor = jnp.exp(maxima - new_maxima)
    exponent = jnp.where(usable[None, None, :], jnp.exp(scores - new_maxima[:, :, None]), 0.0)
    totals = totals * factor + jnp.sum(exponent, axis=2)
    mixed = jnp.einsum(
        "hrn,nhe->hre",
        exponent.astype(jnp.bfloat16),
        value_heads,
        preferred_element_type=jnp.float32,
    )
    accumulated = accumulated * factor[:, :, None] + mixed
    return (new_maxima, totals, accumulated)


def query_step(
    grad_accum,
    key_part,
    value_part,
    offset,
    query_heads,
    context_heads,
    logsum,
    deltas,
    length,
    score_scale,
):
    head_count = query_heads.shape[1]
    amount = key_part.shape[0]
    key_heads = head_split(key_part, head_count)
    value_heads = head_split(value_part, head_count)
    scores = (
        jnp.einsum("rhe,nhe->hrn", query_heads, key_heads, preferred_element_type=jnp.float32)
        * score_scale
    )
    usable = offset + jnp.arange(amount) < length
    attention = jnp.where(usable[None, None, :], jnp.exp(scores - logsum[:, :, None]), 0.0)
    grad_prob = jnp.einsum(
        "rhe,nhe->hrn", context_heads, value_heads, preferred_element_type=jnp.float32
    )
    grad_score = (attention * (grad_prob - deltas[:, :, None])).astype(jnp.bfloat16)
    added = jnp.einsum("hrn,nhe->rhe", grad_score, key_heads, preferred_element_type=jnp.float32)
    return grad_accum + added * score_scale


def key_step(
    query_part,
    context_part,
    all_logsum,
    all_deltas,
    key_heads,
    value_heads,
    key_usable,
    score_scale,
):
    head_count = key_heads.shape[1]
    query_heads = head_split(query_part, head_count)
    context_heads = head_split(context_part, head_count)
    scores = (
        jnp.einsum("rhe,nhe->hrn", query_heads, key_heads, preferred_element_type=jnp.float32)
        * score_scale
    )
    attention = jnp.where(key_usable[None, None, :], jnp.exp(scores - all_logsum[:, :, None]), 0.0)
    grad_value = jnp.einsum(
        "hrn,rhe->nhe",
        attention.astype(jnp.bfloat16),
        context_heads,
        preferred_element_type=jnp.float32,
    )
    grad_prob = jnp.einsum(
        "rhe,nhe->hrn", context_heads, value_heads, preferred_element_type=jnp.float32
    )
    grad_score = (attention * (grad_prob - all_deltas[:, :, None])).astype(jnp.bfloat16)
    added = jnp.einsum("hrn,rhe->nhe", grad_score, query_heads, preferred_element_type=jnp.float32)
    return (added * score_scale, grad_value)


def back_project(gradient, weight):
    return lax.dot_general(
        gradient, weight, (((1,), (1,)), ((), ())), preferred_element_type=jnp.float32
    )


def shards(frames, lengths, cotangent, w_query, w_key, w_value, w_out):
    full_query, full_key, full_value, full_out = (
        lax.all_gather(w_query, "dp", axis=0, tiled=True),
        lax.all_gather(w_key, "dp", axis=0, tiled=True),
        lax.all_gather(w_value, "dp", axis=0, tiled=True),
        lax.all_gather(w_out, "dp", axis=0, tiled=True),
    )
    inputs = frames[0]
    upstream = cotangent[0]
    length = lengths[0]
    row_count = inputs.shape[0]
    inner_width = full_query.shape[1]
    head_count = inner_width // HEAD
    score_scale = HEAD ** (-0.5)
    first_frame = lax.axis_index("ctx") * row_count
    row_usable = first_frame + jnp.arange(row_count) < length
    queries = jnp.dot(inputs, full_query, preferred_element_type=jnp.float32).astype(jnp.bfloat16)
    keys = jnp.dot(inputs, full_key, preferred_element_type=jnp.float32).astype(jnp.bfloat16)
    values = jnp.dot(inputs, full_value, preferred_element_type=jnp.float32).astype(jnp.bfloat16)
    query_heads = head_split(queries, head_count)
    key_heads = head_split(keys, head_count)
    value_heads = head_split(values, head_count)
    start_state = (
        jnp.full((head_count, row_count), MASKED_SCORE, jnp.float32),
        jnp.zeros((head_count, row_count), jnp.float32),
        jnp.zeros((head_count, row_count, HEAD), jnp.float32),
    )
    all_keys, all_values = (
        lax.all_gather(keys, "ctx", axis=0, tiled=True),
        lax.all_gather(values, "ctx", axis=0, tiled=True),
    )
    key_block = row_count * math.gcd(max(1, 512 // row_count), lax.axis_size("ctx"))
    block_count = all_keys.shape[0] // key_block
    key_blocks = all_keys.reshape(block_count, key_block, inner_width)
    value_blocks = all_values.reshape(block_count, key_block, inner_width)
    block_starts = jnp.arange(block_count, dtype=jnp.int32) * key_block

    def scan_forward(current, scan_item):
        return (
            forward_step(
                current, scan_item[0], scan_item[1], scan_item[2], query_heads, length, score_scale
            ),
            None,
        )

    softmax_state, unused = lax.scan(
        scan_forward, start_state, (key_blocks, value_blocks, block_starts)
    )
    maxima, totals, accumulated = softmax_state
    context = (
        (accumulated / totals[:, :, None])
        .transpose(1, 0, 2)
        .reshape(row_count, inner_width)
        .astype(jnp.bfloat16)
    )
    logsum = maxima + jnp.log(totals)
    attended = jnp.dot(context, full_out, preferred_element_type=jnp.float32)
    attended = jnp.where(row_usable[:, None], attended, 0.0).astype(jnp.bfloat16)
    masked_grad = jnp.where(row_usable[:, None], upstream, jnp.zeros_like(upstream))
    grad_context = back_project(masked_grad, full_out).astype(jnp.bfloat16)
    deltas = jnp.sum(
        (grad_context.astype(jnp.float32) * context.astype(jnp.float32)).reshape(
            row_count, head_count, HEAD
        ),
        axis=2,
    )
    context_heads = head_split(grad_context, head_count)
    delta_heads = deltas.T
    all_logsum, all_deltas = (
        lax.all_gather(logsum, "ctx", axis=1, tiled=True),
        lax.all_gather(delta_heads, "ctx", axis=1, tiled=True),
    )
    zero_grad = jnp.zeros((row_count, head_count, HEAD), jnp.float32)

    def scan_query(current, scan_item):
        return (
            query_step(
                current,
                scan_item[0],
                scan_item[1],
                scan_item[2],
                query_heads,
                context_heads,
                logsum,
                delta_heads,
                length,
                score_scale,
            ),
            None,
        )

    grad_query, unused = lax.scan(scan_query, zero_grad, (key_blocks, value_blocks, block_starts))
    grad_key, grad_value = key_step(
        lax.all_gather(queries, "ctx", axis=0, tiled=True),
        lax.all_gather(grad_context, "ctx", axis=0, tiled=True),
        all_logsum,
        all_deltas,
        key_heads,
        value_heads,
        row_usable,
        score_scale,
    )
    grad_query = grad_query.reshape(row_count, inner_width).astype(jnp.bfloat16)
    grad_key = grad_key.reshape(row_count, inner_width).astype(jnp.bfloat16)
    grad_value = grad_value.reshape(row_count, inner_width).astype(jnp.bfloat16)
    grad_input = (
        back_project(grad_query, full_query)
        + back_project(grad_key, full_key)
        + back_project(grad_value, full_value)
    )
    grad_frames = grad_input.astype(jnp.bfloat16)
    summed_grad = lax.psum(
        lax.dot_general(
            context, masked_grad, (((0,), (0,)), ((), ())), preferred_element_type=jnp.float32
        ),
        ("rep", "ctx"),
    )
    grad_out = lax.psum_scatter(summed_grad, "dp", scatter_dimension=0, tiled=True)
    return (attended[None], grad_frames[None], grad_out)


MESH = pl.DeviceIdType.MESH


def dot(left, right, left_dim, right_dim):
    return lax.dot_general(
        left, right, (((left_dim,), (right_dim,)), ((), ())), preferred_element_type=jnp.float32
    )


def fused_kernel(
    frames_ref,
    length_ref,
    cot_ref,
    wq_ref,
    wk_ref,
    wv_ref,
    wo_ref,
    attended_ref,
    grad_frames_ref,
    grad_out_ref,
    xs,
    upstream,
    mine,
    cs,
    wq,
    wk,
    wv,
    wo,
    qs,
    ks,
    vs,
    gs,
    ctx,
    logsum,
    exps,
    inverse,
    from_queries,
    key_sum,
    value_sum,
    dq,
    dk,
    dv,
    part,
    part_in,
    sums,
    sums_in,
    slices,
    send_sem,
    recv_sem,
    local_sem,
):
    rep, dp, z = lax.axis_index("rep"), lax.axis_index("dp"), lax.axis_index("ctx")
    count = 4
    heads = 4
    rows = frames_ref.shape[1]
    full = rows * count
    scale = HEAD ** (-0.5)
    base2 = scale * math.log2(math.e)
    sibling = dp + 1 - 2 * lax.rem(dp, 2)
    across = lax.rem(dp + 2, 4)
    across_sibling = lax.rem(sibling + 2, 4)
    other_rep = 1 - rep
    group = rep * 4 + dp
    lower = z < 2
    middle = (z == 1) | (z == 2)
    side_at = jnp.clip(z - 1, 0, 1)

    local = [
        pltpu.make_async_copy(source, target, local_sem.at[at])
        for at, (source, target) in enumerate(
            (
                (cot_ref.at[0], upstream),
                (frames_ref.at[0], xs.at[z]),
                (wk_ref, wk.at[dp]),
                (wv_ref, wv.at[dp]),
                (wq_ref, wq.at[dp]),
                (wo_ref, wo.at[dp]),
            )
        )
    ]
    for copy in local:
        copy.start()

    barrier = pltpu.get_barrier_semaphore()
    for step in range(1, count):
        for to_rep in (rep, other_rep):
            pl.semaphore_signal(
                barrier,
                inc=1,
                device_id=(to_rep, dp, lax.rem(z + step, count)),
                device_id_type=MESH,
            )
    for step in range(1, 8):
        peer = lax.rem(group + step, 8)
        pl.semaphore_signal(
            barrier, inc=1, device_id=(peer // 4, lax.rem(peer, 4), z), device_id_type=MESH
        )
    pl.semaphore_wait(barrier, 13)

    def remote(source, target, sent, received, device):
        return pltpu.make_async_remote_copy(
            src_ref=source,
            dst_ref=target,
            send_sem=send_sem.at[sent],
            recv_sem=recv_sem.at[received],
            device_id=device,
            device_id_type=MESH,
        )

    def arrive(target, received):
        remote(target, target, received, received, (rep, dp, z)).wait_recv()

    def piece_of(which, slot, at):
        if which == 0:
            return xs.at[slot, pl.ds(at * (rows // 2), rows // 2)]
        return gs.at[slot, pl.ds(at * 2, 2)]

    def chain(which, side, hop, at):
        sign = 1 - 2 * side
        owner = z - sign * (hop - 1)
        slot = jnp.clip(owner, 0, count - 1)
        source = piece_of(which, slot, at)
        if which == 0 and hop == 1:
            source = frames_ref.at[0, pl.ds(at * (rows // 2), rows // 2)]
        target = jnp.clip(z + sign, 0, count - 1)
        index = which * 12 + side * 6 + (hop - 1) * 2 + at
        valid = (z + sign >= 0) & (z + sign < count) & (owner >= 0) & (owner < count)
        copy = remote(source, piece_of(which, slot, at), index, index, (rep, dp, target))
        return valid, copy

    def chain_send(which, hop, at):
        for side in range(2):
            valid, copy = chain(which, side, hop, at)

            @pl.when(valid)
            def _():
                copy.start()

    def chain_recv(which, hop, at):
        for side in range(2):
            owner = z - (1 - 2 * side) * hop
            slot = jnp.clip(owner, 0, count - 1)
            index = which * 12 + side * 6 + (hop - 1) * 2 + at

            @pl.when((owner >= 0) & (owner < count))
            def _():
                arrive(piece_of(which, slot, at), index)

    def gradient_pass(inward):
        for at in range(2):
            for side in range(2):

                @pl.when(middle & (lower == ((side == 0) == inward)))
                def _():
                    owner = z - (1 - 2 * side)
                    arrive(piece_of(1, owner, at), 12 + side * 6 + at)
                    chain(1, side, 2, at)[1].start()

    def chain_pass(which, hop, at):
        chain_recv(which, hop, at)
        if hop < 3:
            chain_send(which, hop + 1, at)

    weights = ((wo_ref, wo), (wk_ref, wk), (wq_ref, wq), (wv_ref, wv))

    def half(ref, which):
        size = ref.shape[0] // 2
        return ref.at[pl.ds(pl.multiple_of(which * size, size), size)]

    def chunk(ref, which, at):
        size = ref.shape[0] // 4
        return ref.at[pl.ds(pl.multiple_of((which * 2 + at) * size, size), size)]

    def weight_copy(piece, step):
        shard, pool = weights[piece]
        index = 24 + piece * 7 + step
        if step == 0:
            return remote(shard, pool.at[dp], index, index, (rep, sibling, z))
        if step < 3:
            target = chunk(pool.at[dp], rep, step - 1)
            return remote(chunk(shard, rep, step - 1), target, index, index, (rep, across, z))
        mine_at = pool.at[across]
        if step < 5:
            source = chunk(mine_at, rep, step - 3)
            return remote(source, source, index, index, (other_rep, dp, z))
        source = half(mine_at, rep if step == 5 else other_rep)
        return remote(source, source, index, index, (rep, sibling, z))

    def weight_recv(piece, step):
        pool = weights[piece][1]
        if step == 0:
            target = pool.at[sibling]
        elif step < 3:
            target = chunk(pool.at[across], rep, step - 1)
        elif step < 5:
            target = chunk(pool.at[across], other_rep, step - 3)
        else:
            target = half(pool.at[across_sibling], rep if step == 5 else other_rep)
        arrive(target, 24 + piece * 7 + step)

    def from_y(at):
        weight_recv(at // 2, 1 + at % 2)
        weight_copy(at // 2, 3 + at % 2).start()
        if at % 2 == 1:
            weight_copy(at // 2, 5).start()

    def from_x(at):
        weight_recv(at // 2, 3 + at % 2)
        if at % 2 == 1:
            weight_copy(at // 2, 6).start()

    def cot_copy(near):
        to = jnp.where(lower, 1, 2) if near else jnp.where(lower, 2, 1)
        sent = 52 + (0 if near else 1)
        return remote(mine.at[to - 1], cs.at[z], sent, 52 + z, (rep, dp, to))

    for at in range(2):
        chain_send(0, 1, at)
    for piece in range(4):
        for step in (1, 2):
            weight_copy(piece, step).start()
    for piece in range(4):
        weight_copy(piece, 0).start()
    for copy in local:
        copy.wait()

    length = length_ref[0]
    width = mine.shape[2]
    real = z * rows + lax.broadcasted_iota(jnp.int32, (rows, width), 0) < length
    for at in range(2):
        kept = upstream[:, at * width : (at + 1) * width].astype(jnp.float32)
        mine[at] = jnp.where(real, kept, 0.0).astype(jnp.bfloat16)
    cs[z] = mine[side_at]

    def whole(piece):
        for step in (0, 5, 6):
            weight_recv(piece, step)

    def project(pool, kept, first, blocks):
        inputs = xs[pl.ds(first, blocks)].reshape(blocks * rows, 1024)
        start = pl.multiple_of(first * rows, rows)
        matrix = dot(inputs, pool[...].reshape(1024, 512), 1, 0).astype(jnp.bfloat16)
        for head in range(heads):
            kept[head, pl.ds(start, blocks * rows), :] = matrix[:, head * HEAD : (head + 1) * HEAD]

    three = jnp.where(lower, 0, 1)
    last = jnp.where(lower, 3, 0)

    @pl.when(jnp.logical_not(middle))
    def _():
        cot_copy(True).start()
        cot_copy(False).start()

    from_y(0)
    chain_pass(0, 1, 0)
    from_y(1)
    from_y(2)
    chain_pass(0, 1, 1)
    from_x(0)
    from_y(3)

    @pl.when(middle)
    def _():
        cot_copy(False).start()

    from_x(1)
    from_y(4)
    from_x(2)
    from_y(5)
    from_x(3)
    from_y(6)
    chain_pass(0, 2, 0)
    from_x(4)
    from_y(7)
    whole(0)
    masked = jnp.concatenate([mine[0], mine[1]], axis=1)
    matrix = dot(masked, wo[...].reshape(512, 1024), 1, 1).astype(jnp.bfloat16)
    for head in range(heads):
        gs[z, head] = matrix[:, head * HEAD : (head + 1) * HEAD]
    for at in range(2):
        chain_send(1, 1, at)
    from_x(5)
    chain_pass(0, 2, 1)
    whole(1)
    from_x(6)
    project(wk, ks, three, 3)
    whole(2)
    project(wq, qs, three, 3)

    def project_last():
        project(wk, ks, last, 1)
        project(wq, qs, last, 1)

    def key_mask(amount):
        return lax.broadcasted_iota(jnp.int32, (amount, full), 1) < length

    def exponents(head, carry):
        amount = full // 2
        usable = key_mask(amount)
        for at in range(2):
            some = pl.ds(at * amount, amount)
            scores = dot(qs[head, some, :], ks[head], 1, 1)
            scores = jnp.where(usable, scores, MASKED_SCORE)
            maxima = jnp.max(scores, axis=1, keepdims=True)
            exponent = jnp.exp2((scores - maxima) * base2)
            totals = jnp.sum(exponent, axis=1, keepdims=True)
            exps[head, some, :] = exponent.astype(jnp.bfloat16)
            inverse[head, some, :] = 1.0 / totals
            logsum[head, some, :] = maxima * base2 + jnp.log2(totals)
        return carry

    @pl.when(middle)
    def _():
        project_last()
        for head in range(4):
            exponents(head, 0)
            if head == 1:
                from_x(7)
            if head == 3:
                gradient_pass(True)

    @pl.when(jnp.logical_not(middle))
    def _():
        from_x(7)
        for at in range(2):
            chain_pass(0, 3, at)
        project_last()
        for head in range(4):
            exponents(head, 0)

    whole(3)
    project(wv, vs, 0, 4)

    def sibling_copy(batch):
        sent = 56 + batch
        return remote(part.at[batch], part_in.at[batch], sent, sent, (rep, sibling, z))

    def sum_copy(which):
        to_rep, to_dp = ((rep, across), (other_rep, across), (other_rep, dp))[which]
        source = sums.at[which // 2, to_rep]
        sent = 58 + which
        return remote(source, sums_in.at[which], sent, sent, (to_rep, to_dp, z))

    def attend(head):
        mixed = dot(exps[head], vs[head], 1, 0)
        ctx[head] = (mixed * inverse[head]).astype(jnp.bfloat16)

    def pair_product(first):
        far = lax.rem(first + 2, 4)
        pair = jnp.concatenate([ctx[far], ctx[first]], axis=1)
        return dot(pair, cs[...].reshape(full, width), 0, 0)

    attend(lax.rem(sibling + 2, 4))
    attend(sibling)

    @pl.when(middle)
    def _():
        for source in range(count):

            @pl.when(z != source)
            def _():
                arrive(cs.at[source], 52 + source)

        product = pair_product(sibling)
        for batch in range(2):
            part[batch] = product[batch * 128 : (batch + 1) * 128].astype(jnp.bfloat16)
            sibling_copy(batch).start()

    gradient_pass(False)
    attend(lax.rem(dp + 2, 4))
    attend(dp)

    @pl.when(middle)
    def _():
        product = pair_product(dp)
        for batch in range(2):
            arrive(part_in.at[batch], 56 + batch)
            kept = product[batch * 128 : (batch + 1) * 128]
            kept = kept + part_in[batch].astype(jnp.float32)
            for at in range(2):
                sums[batch, at] = kept[:, at * 256 : (at + 1) * 256].astype(jnp.bfloat16)
            if batch == 0:
                sum_copy(0).start()
                sum_copy(1).start()
            else:
                sum_copy(2).start()


    @pl.when(jnp.logical_not(middle))
    def _():
        for at in range(2):
            chain_recv(1, 1, at)

    for at in range(2):
        chain_pass(1, 2, at)
    own = pl.ds(pl.multiple_of(z * rows, rows), rows)
    own_context = jnp.concatenate([ctx[head, own, :] for head in range(heads)], axis=1)
    attended = dot(own_context, wo[...].reshape(512, 1024), 1, 0)
    row_at = z * rows + lax.broadcasted_iota(jnp.int32, attended.shape, 0)
    attended_ref[0] = jnp.where(row_at < length, attended, 0.0).astype(jnp.bfloat16)
    def row_deltas(grads, context):
        terms = grads.astype(jnp.float32) * context.astype(jnp.float32)
        return jnp.sum(terms, axis=1, keepdims=True)

    def own_queries(head, carry):
        grads = gs[z, head]
        scores = dot(qs[head, own, :], ks[head], 1, 1) * base2
        attention = jnp.where(key_mask(rows), jnp.exp2(scores - logsum[head, own, :]), 0.0)
        grad_prob = dot(grads, vs[head], 1, 1)
        minus = row_deltas(grads, ctx[head, own, :])
        grad_score = (attention * (grad_prob - minus)).astype(jnp.bfloat16)
        dq[head] = (dot(grad_score, ks[head], 1, 0) * scale).astype(jnp.bfloat16)
        return carry

    def own_keys(first, blocks, head):
        some = pl.ds(pl.multiple_of(first * rows, rows), blocks * rows)
        queries = qs[head, some, :]
        grads = gs[pl.ds(first, blocks), head].reshape(blocks * rows, HEAD)
        scores = dot(queries, ks[head, own, :], 1, 1) * base2
        at = z * rows + lax.broadcasted_iota(jnp.int32, scores.shape, 1)
        attention = jnp.where(at < length, jnp.exp2(scores - logsum[head, some, :]), 0.0)
        values = dot(attention.astype(jnp.bfloat16), grads, 0, 0)
        grad_prob = dot(grads, vs[head, own, :], 1, 1)
        minus = row_deltas(grads, ctx[head, some, :])
        grad_score = (attention * (grad_prob - minus)).astype(jnp.bfloat16)
        return dot(grad_score, queries, 0, 0), values

    lax.fori_loop(0, heads, own_queries, 0)

    mine_slice = side_at * 2 + rep

    def slice_copy(step, turned):
        to_rep = other_rep if turned else rep
        block = slices.at[mine_slice]
        return remote(
            block,
            block,
            64 + step * 2 + turned,
            64 + mine_slice,
            (to_rep, dp, lax.rem(z + step, count)),
        )

    @pl.when(middle)
    def _():
        total = sums[1, rep].astype(jnp.float32)
        for which in range(3):
            arrive(sums_in.at[which], 58 + which)
            total = total + sums_in[which].astype(jnp.float32)
        slices[mine_slice] = total.astype(jnp.bfloat16)
        low, high, mate = lax.rem(count - z, count), 3 - z, jnp.where(lower, 1, 3)
        for step in (low, mate, high):
            for turned in (1, 0):
                slice_copy(step, turned).start()
        slice_copy(0, 1).start()

    def three_keys(head, carry):
        key_sum[head], value_sum[head] = own_keys(three, 3, head)
        return carry

    lax.fori_loop(0, heads, three_keys, 0)
    by_query = jnp.concatenate([dq[head] for head in range(heads)], axis=1)
    for shard in range(4):
        from_queries[:, shard * 256 : (shard + 1) * 256] = dot(by_query, wq[shard], 1, 1)

    for at in range(2):
        chain_pass(1, 3, at)

    def last_keys(head, carry):
        keys, values = own_keys(last, 1, head)
        dk[head] = ((key_sum[head] + keys) * scale).astype(jnp.bfloat16)
        dv[head] = (value_sum[head] + values).astype(jnp.bfloat16)
        return carry

    lax.fori_loop(0, heads, last_keys, 0)

    by_key, by_value = (
        jnp.concatenate([kept[head] for head in range(heads)], axis=1) for kept in (dk, dv)
    )
    for shard in range(4):
        columns = slice(shard * 256, (shard + 1) * 256)
        added = dot(by_key, wk[shard], 1, 1) + dot(by_value, wv[shard], 1, 1)
        added = added + from_queries[:, columns]
        grad_frames_ref[0, :, columns] = added.astype(jnp.bfloat16)

    for piece in range(4):
        for step in range(7):
            weight_copy(piece, step).wait_send()
    for which in range(2):
        for hop in range(1, count):
            for at in range(2):
                for side in range(2):
                    valid, copy = chain(which, side, hop, at)

                    @pl.when(valid)
                    def _():
                        copy.wait_send()

    @pl.when(jnp.logical_not(middle))
    def _():
        cot_copy(True).wait_send()

    cot_copy(False).wait_send()

    @pl.when(middle)
    def _():
        for batch in range(2):
            sibling_copy(batch).wait_send()
        for which in range(3):
            sum_copy(which).wait_send()

    for at in range(count):

        @pl.when(jnp.logical_not(middle & (mine_slice == at)))
        def _():
            arrive(slices.at[at], 64 + at)

    @pl.when(middle)
    def _():
        for step in range(count):
            for turned in range(2):
                if step + turned > 0:
                    slice_copy(step, turned).wait_send()

    for at in range(count):
        grad_out_ref[:, at * 256 : (at + 1) * 256] = slices[at].astype(jnp.float32)


def write_kernel(*refs):
    sems = refs[6]
    copies = [pltpu.make_async_copy(refs[at], refs[at + 3], sems.at[at]) for at in range(3)]
    for copy in copies:
        copy.start()
    for copy in copies:
        copy.wait()


def fused(frames, lengths, cotangent, w_query, w_key, w_value, w_out):
    vmem = pl.BlockSpec(memory_space=pltpu.VMEM)
    hbm = pl.BlockSpec(memory_space=pltpu.HBM)
    bf16, f32 = jnp.bfloat16, jnp.float32
    per_head = pltpu.VMEM((4, 512, HEAD), bf16)
    own_head = pltpu.VMEM((4, 128, HEAD), bf16)
    results = pl.pallas_call(
        fused_kernel,
        out_shape=(
            pltpu.VMEM(frames.shape, bf16),
            pltpu.VMEM(frames.shape, bf16),
            pltpu.VMEM(w_out.shape, f32),
        ),
        in_specs=[hbm, pl.BlockSpec(memory_space=pltpu.SMEM)] + [hbm] * 5,
        out_specs=(vmem, vmem, vmem),
        scratch_shapes=[
            pltpu.VMEM((4, 128, 1024), bf16),
            pltpu.VMEM((128, 1024), bf16),
            pltpu.VMEM((2, 128, 512), bf16),
            pltpu.VMEM((4, 128, 512), bf16),
            pltpu.VMEM((4, 256, 512), bf16),
            pltpu.VMEM((4, 256, 512), bf16),
            pltpu.VMEM((4, 256, 512), bf16),
            pltpu.VMEM((4, 128, 1024), bf16),
            per_head,
            per_head,
            per_head,
            pltpu.VMEM((4, 4, 128, HEAD), bf16),
            per_head,
            pltpu.VMEM((4, 512, 1), f32),
            pltpu.VMEM((4, 512, 512), bf16),
            pltpu.VMEM((4, 512, 1), f32),
            pltpu.VMEM((128, 1024), f32),
            pltpu.VMEM((4, 128, HEAD), f32),
            pltpu.VMEM((4, 128, HEAD), f32),
            own_head,
            own_head,
            own_head,
            pltpu.VMEM((2, 128, 512), bf16),
            pltpu.VMEM((2, 128, 512), bf16),
            pltpu.VMEM((2, 2, 128, 256), bf16),
            pltpu.VMEM((3, 128, 256), bf16),
            pltpu.VMEM((4, 128, 256), bf16),
            pltpu.SemaphoreType.DMA((72,)),
            pltpu.SemaphoreType.DMA((72,)),
            pltpu.SemaphoreType.DMA((6,)),
        ],
        compiler_params=pltpu.CompilerParams(
            collective_id=0, has_side_effects=True, vmem_limit_bytes=56 * 1024 * 1024
        ),
    )(frames, lengths, cotangent, w_query, w_key, w_value, w_out)
    return pl.pallas_call(
        write_kernel,
        out_shape=tuple(jax.ShapeDtypeStruct(r.shape, r.dtype) for r in results),
        in_specs=[vmem] * 3,
        out_specs=(hbm, hbm, hbm),
        scratch_shapes=[pltpu.SemaphoreType.DMA((3,))],
        compiler_params=pltpu.CompilerParams(vmem_limit_bytes=4 * 1024 * 1024),
    )(*results)


def either(sizes, frames, lengths, cotangent, w_query, w_key, w_value, w_out):
    fits = sizes == (2, 4, 4) and frames.shape == (1, 128, 1024) and w_query.shape == (256, 512)
    chosen = fused if fits else shards
    return chosen(frames, lengths, cotangent, w_query, w_key, w_value, w_out)


def solution(mesh):
    in_specs = (
        P(("rep", "dp"), "ctx", None),
        P(("rep", "dp")),
        P(("rep", "dp"), "ctx", None),
        P("dp", None),
        P("dp", None),
        P("dp", None),
        P("dp", None),
    )
    out_specs = (P(("rep", "dp"), "ctx", None), P(("rep", "dp"), "ctx", None), P("dp", None))
    sizes = (mesh.shape["rep"], mesh.shape["dp"], mesh.shape["ctx"])
    body = functools.partial(either, sizes)
    return jax.shard_map(body, mesh=mesh, in_specs=in_specs, out_specs=out_specs, check_vma=False)
```
